512 devices in a mesh: narrow: 8 (over z_lo), wide: 64 (over x, y, z_hi, core).
Axes of the slice: x: 4, y: 4, z: 16 (z_hi: 2, z_lo: 8; z = z_hi * 8 + z_lo), core: 2. Of those that a mesh axis runs over, the one named last changes fastest.
Arguments:
- state: float32 [5120, 5120], P('wide', 'narrow'), may hold values from 0 to 10, as said below
- in_pattern: int32 [20, 20], replicated, may hold values from 0 to 1, as said below
- out_pattern: int32 [20, 20], replicated, may hold values from 0 to 1, as said below
Outputs:
- clustered: float32 [5120, 5120], P('wide', 'narrow')
The draws below stay inside these ranges and needn't reach their ends.
Inputs may be any that keep to these rules, and one draw needn't show every extreme that they name: `in_pattern`: entries are 0 or 1 and every diagonal block is 1. `out_pattern`: entries are 0 or 1 and every diagonal block is 1. `state`: nonnegative; the diagonal lies between 0.5 and 1.
All inputs are finite; a program needn't handle non-finite values.
Results may differ from the reference program's by a relative error of at most 0.00011.
Values sent between devices are 32-bit elements; how exact they have to be, the bound alone decides.
No kernel may reach another device: no remote copies, remote signals or barrier semaphores. Data moves between devices by JAX's collectives and lax.ppermute only.
A program may use at most 64 MiB of HBM per device.

```python
import jax
import jax.numpy as jnp
from jax import lax

BLK = 256
NODES = 5120
NBLK = 20


def draw_state(key, part):
    key = jax.random.fold_in(key, 1)
    key_live, key_vals, key_diag = jax.random.split(key, 3)
    live = (jax.random.randint(key_live, (NODES, NODES), 0, 2) == 0).astype(jnp.float32)
    vals = jnp.exp(jax.random.uniform(key_vals, (NODES, NODES), jnp.float32, -6.9, 0.0))
    diag = jax.random.uniform(key_diag, (NODES, 1), jnp.float32, 0.5, 1.0)
    rows = jnp.arange(NODES)[:, None]
    cols = jnp.arange(NODES)[None, :]
    return jnp.where(rows == cols, diag, vals * live)


def draw_in_pattern(key, part):
    key = jax.random.fold_in(key, 2)
    picks = (jax.random.randint(key, (NBLK, NBLK), 0, 8) < 3).astype(jnp.int32)
    return jnp.maximum(picks, jnp.eye(NBLK, dtype=jnp.int32))


def draw_out_pattern(key, part):
    key = jax.random.fold_in(key, 3)
    picks = (jax.random.randint(key, (NBLK, NBLK), 0, 8) < 5).astype(jnp.int32)
    return jnp.maximum(picks, jnp.eye(NBLK, dtype=jnp.int32))


def setup_inputs(seed: int = 0) -> dict:
    streams_of = jax.random.split(jax.random.key(seed), 4)
    return {
        "state": draw_state(jax.random.fold_in(streams_of[3], 71), 0),
        "in_pattern": draw_in_pattern(jax.random.fold_in(streams_of[3], 71), 0),
        "out_pattern": draw_out_pattern(jax.random.fold_in(streams_of[3], 71), 0),
    }


def expand_pattern(pattern):
    grown = jnp.repeat(jnp.repeat(pattern.astype(jnp.float32), BLK, axis=0), BLK, axis=1)
    return grown


def reference(state, in_pattern, out_pattern):
    masked = state * expand_pattern(in_pattern)
    expanded = jnp.dot(masked, masked, preferred_element_type=jnp.float32, precision=lax.Precision.HIGHEST)
    inflated = expanded * expanded * expand_pattern(out_pattern)
    totals = jnp.sum(inflated, axis=1)
    return inflated * (NODES / totals)[:, None]
```

```python
import jax
import jax.numpy as jnp
from jax import lax
from jax.sharding import Mesh, PartitionSpec as P

BLK = 256
ROWS = ("x", "y", "zh", "c")


def tile_mask(pattern, row_start, rows, col_start, cols):
    blocks = pattern.shape[0]
    pattern = pattern.astype(jnp.float32)
    row_blk = (row_start + jnp.arange(rows)) // BLK
    first = row_start // BLK
    low = lax.dynamic_slice_in_dim(pattern, first, 1, 0)[0]
    high = lax.dynamic_slice_in_dim(pattern, jnp.minimum(first + 1, blocks - 1), 1, 0)[0]
    col_blk = (col_start + jnp.arange(cols)) // BLK
    pick = col_blk[:, None] == jnp.arange(blocks)[None, :]
    low = jnp.sum(jnp.where(pick, low[None, :], 0.0), axis=1)
    high = jnp.sum(jnp.where(pick, high[None, :], 0.0), axis=1)
    return jnp.where((row_blk == first)[:, None], low[None, :], high[None, :])


def body(state, in_pattern, out_pattern):
    rows, cols = state.shape
    n_y, n_zl = lax.axis_size("y"), lax.axis_size("zl")
    part = rows // n_y
    nodes_all = cols * n_zl
    row_start = lax.axis_index(ROWS) * rows
    col_start = lax.axis_index("zl") * cols
    masked = state * tile_mask(in_pattern, row_start, rows, col_start, cols)

    pieces = masked.reshape(rows, 2, 2, 2, n_y, part)
    pieces = pieces.transpose(4, 0, 3, 2, 1, 5).reshape(n_y, rows, cols // n_y)
    left = lax.all_to_all(pieces, "y", 0, 0).reshape(n_y * rows, cols // n_y)
    left = lax.all_gather(left, "zl", axis=0)

    right = lax.all_to_all(masked.reshape(n_y, part, cols), "y", 0, 0)
    right = right.reshape(2, 2 * part, cols)
    right = lax.all_gather(right, "zh", axis=1)
    right = lax.all_gather(right, "x", axis=0)
    right = lax.all_gather(right, "c", axis=2)
    right = right.reshape(n_zl, cols // n_y, cols)

    partial = jnp.einsum(
        "zik,zkj->ij",
        left,
        right,
        preferred_element_type=jnp.float32,
        precision=lax.Precision.HIGH,
    )
    shares = lax.all_to_all(partial.reshape(n_y, rows, cols), "y", 0, 0)
    expanded = jnp.sum(shares, axis=0)
    inflated = expanded * expanded * tile_mask(out_pattern, row_start, rows, col_start, cols)
    sums = jnp.broadcast_to(jnp.sum(inflated, axis=1)[None, :], (n_zl, rows))
    totals = jnp.sum(lax.all_to_all(sums, "zl", 0, 0), axis=0)
    return inflated * (nodes_all / totals)[:, None]


def solution(mesh):
    fine = Mesh(
        mesh.devices.reshape(8, 4, 4, 2, 2), ("zl", "x", "y", "zh", "c")
    )
    return jax.shard_map(
        body,
        mesh=fine,
        in_specs=(P(ROWS, "zl"), P(), P()),
        out_specs=P(ROWS, "zl"),
        check_vma=False,
    )
```

```python
import jax
import jax.numpy as jnp
from jax import lax
from jax.sharding import Mesh, PartitionSpec as P

BLK = 256
ROWS = ("x", "y", "zh", "c")


def tile_mask(pattern, row_start, rows, col_start, cols):
    blocks = pattern.shape[0]
    pattern = pattern.astype(jnp.float32)
    row_blk = (row_start + jnp.arange(rows)) // BLK
    first = row_start // BLK
    low = lax.dynamic_slice_in_dim(pattern, first, 1, 0)[0]
    high = lax.dynamic_slice_in_dim(pattern, jnp.minimum(first + 1, blocks - 1), 1, 0)[0]
    col_blk = (col_start + jnp.arange(cols)) // BLK
    pick = col_blk[:, None] == jnp.arange(blocks)[None, :]
    low = jnp.sum(jnp.where(pick, low[None, :], 0.0), axis=1)
    high = jnp.sum(jnp.where(pick, high[None, :], 0.0), axis=1)
    return jnp.where((row_blk == first)[:, None], low[None, :], high[None, :])


def gather(block, axis_name, axis):
    size = lax.axis_size(axis_name)
    copies = jnp.broadcast_to(block[None], (size,) + block.shape)
    return jnp.moveaxis(lax.all_to_all(copies, axis_name, 0, 0), 0, axis)


def body(state, in_pattern, out_pattern):
    rows, cols = state.shape
    n_y, n_zl = lax.axis_size("y"), lax.axis_size("zl")
    part = rows // n_y
    nodes_all = cols * n_zl
    row_start = lax.axis_index(ROWS) * rows
    col_start = lax.axis_index("zl") * cols
    masked = state * tile_mask(in_pattern, row_start, rows, col_start, cols)

    pieces = masked.reshape(rows, 2, 2, 2, n_y, part)
    pieces = pieces.transpose(4, 0, 3, 2, 1, 5).reshape(n_y, rows, cols // n_y)
    left = lax.all_to_all(pieces, "y", 0, 0).reshape(n_y * rows, cols // n_y)

    mine, left = lax.optimization_barrier((masked, left))
    left = lax.all_gather(left, "zl", axis=0)
    right = lax.all_to_all(mine.reshape(n_y, part, cols), "y", 0, 0)
    right = right.reshape(2, 2 * part, cols)
    right = gather(right, "zh", 1)
    right = gather(right, "x", 0)
    right = gather(right, "c", 2)
    right = right.reshape(n_zl, cols // n_y, cols)

    partial = jnp.einsum(
        "zik,zkj->ij",
        left,
        right,
        preferred_element_type=jnp.float32,
        precision=lax.Precision.HIGH,
    )
    shares = lax.all_to_all(partial.reshape(n_y, rows, cols), "y", 0, 0)
    expanded = jnp.sum(shares, axis=0)
    inflated = expanded * expanded * tile_mask(out_pattern, row_start, rows, col_start, cols)
    sums = jnp.broadcast_to(jnp.sum(inflated, axis=1)[None, :], (n_zl, rows))
    totals = jnp.sum(lax.all_to_all(sums, "zl", 0, 0), axis=0)
    return inflated * (nodes_all / totals)[:, None]


def solution(mesh):
    fine = Mesh(
        mesh.devices.reshape(8, 4, 4, 2, 2), ("zl", "x", "y", "zh", "c")
    )
    return jax.shard_map(
        body,
        mesh=fine,
        in_specs=(P(ROWS, "zl"), P(), P()),
        out_specs=P(ROWS, "zl"),
        check_vma=False,
    )
```

```python
import jax
import jax.numpy as jnp
from jax import lax
from jax.sharding import Mesh, PartitionSpec as P

BLK = 256
ROWS = ("x", "y", "zh", "c")


def tile_mask(pattern, row_start, rows, col_start, cols):
    blocks = pattern.shape[0]
    pattern = pattern.astype(jnp.float32)
    row_blk = (row_start + jnp.arange(rows)) // BLK
    first = row_start // BLK
    low = lax.dynamic_slice_in_dim(pattern, first, 1, 0)[0]
    high = lax.dynamic_slice_in_dim(pattern, jnp.minimum(first + 1, blocks - 1), 1, 0)[0]
    col_blk = (col_start + jnp.arange(cols)) // BLK
    pick = col_blk[:, None] == jnp.arange(blocks)[None, :]
    low = jnp.sum(jnp.where(pick, low[None, :], 0.0), axis=1)
    high = jnp.sum(jnp.where(pick, high[None, :], 0.0), axis=1)
    return jnp.where((row_blk == first)[:, None], low[None, :], high[None, :])


def gather(block, axis_name, axis):
    size = lax.axis_size(axis_name)
    copies = jnp.broadcast_to(block[None], (size,) + block.shape)
    return jnp.moveaxis(lax.all_to_all(copies, axis_name, 0, 0), 0, axis)


def body(state, in_pattern, out_pattern):
    rows, cols = state.shape
    n_y, n_zl = lax.axis_size("y"), lax.axis_size("zl")
    part = rows // n_y
    nodes_all = cols * n_zl
    row_start = lax.axis_index(ROWS) * rows
    col_start = lax.axis_index("zl") * cols
    masked = state * tile_mask(in_pattern, row_start, rows, col_start, cols)

    other = lax.ppermute(masked, "zh", [(0, 1), (1, 0)])

    pieces = masked.reshape(rows, 2, 2, 2, n_y, part)
    pieces = pieces.transpose(4, 0, 3, 2, 1, 5).reshape(n_y, rows, cols // n_y)
    left = lax.all_to_all(pieces, "y", 0, 0).reshape(n_y * rows, cols // n_y)

    mine, left = lax.optimization_barrier((masked, left))
    left = lax.all_gather(left, "zl", axis=0)
    mine = lax.all_to_all(mine.reshape(n_y, part, cols), "y", 0, 0)
    other, mine = lax.optimization_barrier((other, mine))
    other = lax.all_to_all(other.reshape(n_y, part, cols), "y", 0, 0)
    mine = mine.reshape(2, 2 * part, cols)
    other = other.reshape(2, 2 * part, cols)
    low = lax.axis_index("zh") == 0
    right = jnp.where(low, jnp.stack([mine, other], 1), jnp.stack([other, mine], 1))
    right = gather(right, "x", 0)
    right = gather(right, "c", 2)
    right = right.reshape(n_zl, cols // n_y, cols)

    partial = jnp.einsum(
        "zik,zkj->ij",
        left,
        right,
        preferred_element_type=jnp.float32,
        precision=lax.Precision.HIGH,
    )
    shares = lax.all_to_all(partial.reshape(n_y, rows, cols), "y", 0, 0)
    expanded = jnp.sum(shares, axis=0)
    inflated = expanded * expanded * tile_mask(out_pattern, row_start, rows, col_start, cols)
    sums = jnp.broadcast_to(jnp.sum(inflated, axis=1)[None, :], (n_zl, rows))
    totals = jnp.sum(lax.all_to_all(sums, "zl", 0, 0), axis=0)
    return inflated * (nodes_all / totals)[:, None]


def solution(mesh):
    fine = Mesh(
        mesh.devices.reshape(8, 4, 4, 2, 2), ("zl", "x", "y", "zh", "c")
    )
    return jax.shard_map(
        body,
        mesh=fine,
        in_specs=(P(ROWS, "zl"), P(), P()),
        out_specs=P(ROWS, "zl"),
        check_vma=False,
    )
```

```python
import functools

import jax
import jax.numpy as jnp
from jax import lax
from jax.experimental import pallas as pl
from jax.experimental.pallas import tpu as pltpu
from jax.sharding import Mesh, PartitionSpec as P

BLK = 256
ROWS = ("x", "y", "zh", "c")
SLOTS = 256
EXACT = lax.Precision.HIGHEST


def tile_mask(pattern, row_start, rows, col_start, cols):
    blocks = pattern.shape[0]
    row_blk = (row_start + jnp.arange(rows)) // BLK
    first = row_start // BLK
    low = lax.dynamic_slice_in_dim(pattern, first, 1, 0)[0]
    high = lax.dynamic_slice_in_dim(pattern, jnp.minimum(first + 1, blocks - 1), 1, 0)[0]
    col_blk = (col_start + jnp.arange(cols)) // BLK
    pick = col_blk[:, None] == jnp.arange(blocks)[None, :]
    low = jnp.sum(jnp.where(pick, low[None, :], 0.0), axis=1)
    high = jnp.sum(jnp.where(pick, high[None, :], 0.0), axis=1)
    return jnp.where((row_blk == first)[:, None], low[None, :], high[None, :])


def places(pattern, zh, c):
    q = jnp.arange(80)
    chunk = 20 * (q // 5) + 10 * zh + 5 * c + q % 5
    half = jnp.arange(40)
    row_pick = (chunk[:, None] // 16 == jnp.arange(20)[None, :]).astype(jnp.float32)
    col_pick = (half[None, :] // 2 == jnp.arange(20)[:, None]).astype(jnp.float32)
    live = row_pick @ pattern @ col_pick
    before = (q[:, None] > q[None, :]).astype(jnp.float32) @ live
    same = (half[:, None] // 5 == half[None, :] // 5) & (half[:, None] < half[None, :])
    earlier = jnp.sum(live, axis=0, keepdims=True) @ same.astype(jnp.float32)
    return jnp.where(live > 0, before + earlier, -1.0), live


def most_live(pattern):
    g = jnp.arange(16)[:, None] * 20 + jnp.arange(5)[None, :]
    chunk = (jnp.arange(4) * 5)[:, None, None] + g[None]
    weight = jnp.sum((chunk[..., None] // 16 == jnp.arange(20)).astype(jnp.float32), (1, 2))
    half = jnp.arange(40).reshape(8, 5)
    wide = jnp.sum((half[..., None] // 2 == jnp.arange(20)).astype(jnp.float32), 1)
    return jnp.max(weight @ pattern @ wide.T)


def split(x):
    hi = x.astype(jnp.bfloat16)
    return hi, (x - hi.astype(jnp.float32)).astype(jnp.bfloat16)


def dot(a, b):
    return jnp.dot(a, b, preferred_element_type=jnp.float32)


def product_kernel(slots, place_ref, packed_ref, right_ref, out_ref, left_ref):
    lane = lax.broadcasted_iota(jnp.int32, (80, 128), 1) // 32
    slot = lax.broadcasted_iota(jnp.int32, (80, slots), 1).astype(jnp.float32)
    place = place_ref[...]
    units, group = [], 0
    for z in range(8):
        hi, lo = split(packed_ref[z])
        both = jnp.concatenate([hi, lo], axis=1)
        pick = jnp.concatenate(
            [
                (place[:, 5 * z + h : 5 * z + h + 1] == slot).astype(jnp.bfloat16)
                for h in range(5)
            ],
            axis=0,
        )
        got = dot(pick, both)
        got = got[:, :128] + got[:, 128:]
        units += [got[80 * h : 80 * h + 80] for h in range(5)]
        while len(units) >= 4:
            four, units = units[:4], units[4:]
            for r in range(4):
                tile = jnp.zeros((80, 128), jnp.float32)
                for j in range(4):
                    moved = four[j]
                    if j != r:
                        moved = pltpu.roll(moved, 32 * ((j - r) % 4), 1)
                    tile = jnp.where(lane == j, moved, tile)
                left_ref[80 * r : 80 * r + 80, 128 * group : 128 * group + 128] = tile
            group += 1
    to = lax.broadcasted_iota(jnp.int32, (320, 1), 0)
    source = (to % 20) // 5 * 80 + to // 20 * 5 + to % 5
    order = (source == lax.broadcasted_iota(jnp.int32, (320, 320), 1)).astype(jnp.bfloat16)
    left_hi, left_lo = split(left_ref[...])
    left_hi = dot(order, left_hi).astype(jnp.bfloat16)
    left_lo = dot(order, left_lo).astype(jnp.bfloat16)
    right_hi, right_lo = split(right_ref[...])
    out_ref[...] = dot(left_hi, right_hi) + (dot(left_hi, right_lo) + dot(left_lo, right_hi))


def product(place, packed, right):
    slots = packed.shape[1]
    vmem = pl.BlockSpec(memory_space=pltpu.VMEM)
    return pl.pallas_call(
        functools.partial(product_kernel, slots),
        out_shape=jax.ShapeDtypeStruct((320, 640), jnp.float32),
        in_specs=[vmem] * 3,
        out_specs=vmem,
        scratch_shapes=[pltpu.VMEM((320, 1280), jnp.float32)],
        compiler_params=pltpu.CompilerParams(vmem_limit_bytes=48 * 2**20),
        cost_estimate=pl.CostEstimate(
            flops=3 * 10**9, bytes_accessed=6 * 10**6, transcendentals=0
        ),
    )(place, packed, right)


def gather(block, axis_name, axis):
    size = lax.axis_size(axis_name)
    copies = jnp.broadcast_to(block[None], (size,) + block.shape)
    return jnp.moveaxis(lax.all_to_all(copies, axis_name, 0, 0), 0, axis)


def partial_product(slots, units, place, masked):
    zl = lax.axis_index("zl")
    mine = lax.dynamic_slice_in_dim(place, 5 * zl, 5, 1).reshape(400, 1)
    pick = (mine == jnp.arange(slots, dtype=jnp.float32)[None, :]).astype(jnp.float32)
    packed = jnp.dot(pick.T, units, precision=EXACT)
    masked, packed = lax.optimization_barrier((masked, packed))
    packed = lax.all_gather(packed, "zl", axis=0)

    right = masked.reshape(5, 4, 4, 640).transpose(1, 0, 2, 3).reshape(4, 1, 20, 640)
    right = jnp.broadcast_to(right, (4, 2, 20, 640)).reshape(8, 20, 640)
    right = lax.all_to_all(right, ("y", "zh"), 0, 0)
    right = right.reshape(2, 2, 2, 20, 640)
    right = gather(right, "x", 0)
    right = gather(right, "c", 4).reshape(1280, 640)
    return product(place, packed, right)


def body(state, in_pattern, out_pattern):
    rows, cols = state.shape
    nodes_all = cols * lax.axis_size("zl")
    row_start = lax.axis_index(ROWS) * rows
    col_start = lax.axis_index("zl") * cols
    in_pattern = in_pattern.astype(jnp.float32)
    out_pattern = out_pattern.astype(jnp.float32)
    masked = state * tile_mask(in_pattern, row_start, rows, col_start, cols)
    place, _ = places(in_pattern, lax.axis_index("zh"), lax.axis_index("c"))

    units = masked.reshape(5, 4, 4, 5, 8, 4, 4)
    units = units.transpose(1, 5, 0, 3, 2, 4, 6).reshape(16, 25, 128)
    units = lax.all_to_all(units, ("x", "y"), 0, 0).reshape(400, 128)

    shares = lax.cond(
        most_live(in_pattern) <= SLOTS,
        functools.partial(partial_product, SLOTS),
        functools.partial(partial_product, 400),
        units,
        place,
        masked,
    )
    shares = lax.all_to_all(shares.reshape(16, 20, 640), ("x", "y"), 0, 0)
    expanded = jnp.sum(shares.reshape(4, 4, 4, 5, 640), axis=1)
    expanded = expanded.transpose(2, 0, 1, 3).reshape(rows, cols)
    inflated = expanded * expanded * tile_mask(out_pattern, row_start, rows, col_start, cols)
    sums = jnp.broadcast_to(jnp.sum(inflated, axis=1)[None, :], (8, rows))
    totals = jnp.sum(lax.all_to_all(sums, "zl", 0, 0), axis=0)
    return inflated * (nodes_all / totals)[:, None]


def solution(mesh):
    fine = Mesh(
        mesh.devices.reshape(8, 4, 4, 2, 2), ("zl", "x", "y", "zh", "c")
    )
    return jax.shard_map(
        body,
        mesh=fine,
        in_specs=(P(ROWS, "zl"), P(), P()),
        out_specs=P(ROWS, "zl"),
        check_vma=False,
    )
```

```python
import functools

import jax
import jax.numpy as jnp
from jax import lax
from jax.experimental import pallas as pl
from jax.experimental.pallas import tpu as pltpu
from jax.sharding import Mesh, PartitionSpec as P

BLK = 256
ROWS = ("x", "y", "zh", "c")
MAIN, REST = 80, 24
LEFT = MAIN + REST
RUN, PAD = 20, 24
PIECE = LEFT + 5 * PAD
VMEM = pl.BlockSpec(memory_space=pltpu.VMEM)
SMEM = pl.BlockSpec(memory_space=pltpu.SMEM)


def split(x):
    hi = x.astype(jnp.bfloat16)
    return hi, (x - hi.astype(jnp.float32)).astype(jnp.bfloat16)


def dot(a, b):
    return jnp.dot(a, b, preferred_element_type=jnp.float32)


def call(kernel, outs, in_specs, args, scratch=(), flops=10**6, size=10**6):
    return pl.pallas_call(
        kernel,
        out_shape=outs,
        in_specs=in_specs,
        out_specs=jax.tree.map(lambda _: VMEM, outs),
        scratch_shapes=scratch,
        compiler_params=pltpu.CompilerParams(vmem_limit_bytes=40 * 2**20),
        cost_estimate=pl.CostEstimate(
            flops=flops, bytes_accessed=size, transcendentals=0
        ),
    )(*args)


def masked_block(at_ref, pattern_ref, h, x):
    row = at_ref[0] * 80
    col = (5 * at_ref[1] + h) // 2
    first = row // BLK
    low = pattern_ref[first, col].astype(jnp.float32)
    high = pattern_ref[jnp.minimum(first + 1, 19), col].astype(jnp.float32)
    here = lax.broadcasted_iota(jnp.int32, (80, 128), 0) + row < (first + 1) * BLK
    return x * jnp.where(here, low, high)


def pieces_kernel(at_ref, pattern_ref, state_ref, out_ref, masked_ref):
    zh, c = at_ref[2], at_ref[3]
    for h in range(5):
        lanes = slice(128 * h, 128 * h + 128)
        masked_ref[:, lanes] = masked_block(at_ref, pattern_ref, h, state_ref[:, lanes])
    out_ref[...] = jnp.zeros_like(out_ref)
    for y in range(4):
        for h in range(5):
            out_ref[y, LEFT + PAD * h : LEFT + PAD * h + RUN] = masked_ref[
                RUN * y : RUN * y + RUN, 128 * h : 128 * h + 128
            ]
    n = lax.broadcasted_iota(jnp.int32, (1, 640), 1)
    late = n >= 512
    y = jnp.where(late, (n - 512) // 32, n // 128)
    m = jnp.where(late, 128 + n % 32, n % 128)
    dzh, dc, y0, t = m // 80, m // 40 % 2, m // 20 % 2, m % 20
    zh_of = jnp.where(dzh == 0, zh, 1 - zh)
    c_of = jnp.where(dc == 0, c, 1 - c)
    source = 80 * (4 * y0 + 2 * zh_of + c_of) + 20 * y + t
    order = lax.broadcasted_iota(jnp.int32, (640, 640), 0) == source
    order = order.astype(jnp.float32).astype(jnp.bfloat16)
    x = masked_ref[...]
    hi, rest = x.astype(jnp.bfloat16), x
    rest = x - hi.astype(jnp.float32)
    mid, low = split(rest)
    moved = (dot(hi, order) + dot(mid, order)) + dot(low, order)
    lane = lax.broadcasted_iota(jnp.int32, (8, 128), 1) // 32
    for y in range(4):
        out_ref[y, :MAIN] = moved[:, 128 * y : 128 * y + 128]
        for slot in range(3):
            tile = jnp.zeros((8, 128), jnp.float32)
            for j in range(min(4, 10 - 4 * slot)):
                rows = 8 * (4 * slot + j)
                part = moved[rows : rows + 8, 512:]
                if j != y:
                    part = pltpu.roll(part, 32 * ((j - y) % 4), 1)
                tile = jnp.where(lane == j, part, tile)
            out_ref[y, MAIN + 8 * slot : MAIN + 8 * slot + 8] = tile


def unpack_kernel(got_ref, left_ref, right_ref):
    left_ref[...] = got_ref[:, :LEFT]
    for y in range(4):
        for h in range(5):
            right_ref[y // 2, RUN * (y % 2) : RUN * (y % 2) + RUN, 128 * h : 128 * h + 128] = (
                got_ref[y, LEFT + PAD * h : LEFT + PAD * h + RUN]
            )


def product_kernel(at_ref, *refs):
    lefts, rights, out_ref, hi_ref, lo_ref = refs[:8], refs[8:12], *refs[12:]
    for part, ref in enumerate(rights):
        for dx in range(4):
            for y1 in range(2):
                hi, lo = split(ref[dx, y1])
                rows = slice(40 * part, 40 * part + 40)
                hi_ref[2 * dx + y1, rows] = hi
                lo_ref[2 * dx + y1, rows] = lo
    lane = lax.broadcasted_iota(jnp.int32, (8, 128), 1) // 32
    zl, x = at_ref[1], at_ref[4]
    total = jnp.zeros((320, 640), jnp.float32)
    for d, ref in enumerate(lefts):
        source = lax.rem(zl - d + 8, 8)
        block = 2 * lax.rem(x - source // 2 + 4, 4) + lax.rem(source, 2)
        whole = []
        for y in range(4):
            rest = []
            for tile in range(10):
                rows = MAIN + 8 * (tile // 4)
                rest.append(jnp.where(lane == tile % 4, ref[y, rows : rows + 8], 0.0))
            rest = jnp.concatenate(rest, axis=0)
            whole.append(jnp.concatenate([ref[y, :MAIN], rest], axis=1))
        left_hi, left_lo = split(jnp.concatenate(whole, axis=0))
        right_hi, right_lo = hi_ref[block], lo_ref[block]
        right_hi = jnp.concatenate([right_hi] + [right_hi[128:]] * 3, axis=0)
        right_lo = jnp.concatenate([right_lo] + [right_lo[128:]] * 3, axis=0)
        total += dot(left_hi, right_hi) + (dot(left_hi, right_lo) + dot(left_lo, right_hi))
    out_ref[...] = total.reshape(4, 80, 640)


def inflate_kernel(at_ref, pattern_ref, shares_ref, out_ref, sums_ref):
    for h in range(5):
        lanes = slice(128 * h, 128 * h + 128)
        x = (shares_ref[0, :, lanes] + shares_ref[1, :, lanes]) + (
            shares_ref[2, :, lanes] + shares_ref[3, :, lanes]
        )
        out_ref[:, lanes] = masked_block(at_ref, pattern_ref, h, x * x)
    sums_ref[...] = lax.dot_general(
        jnp.ones((8, 640), jnp.float32),
        out_ref[...],
        (((1,), (1,)), ((), ())),
        precision=lax.Precision.HIGHEST,
        preferred_element_type=jnp.float32,
    )


def scale_kernel(nodes, inflated_ref, sums_ref, out_ref):
    totals = lax.dot_general(
        sums_ref[...],
        jnp.ones((8, 128), jnp.float32),
        (((0,), (0,)), ((), ())),
        precision=lax.Precision.HIGHEST,
        preferred_element_type=jnp.float32,
    )
    scale = nodes / totals
    for h in range(5):
        lanes = slice(128 * h, 128 * h + 128)
        out_ref[:, lanes] = inflated_ref[:, lanes] * scale


def shift(x, axis_name, by):
    size = lax.axis_size(axis_name)
    return lax.ppermute(x, axis_name, [(i, (i + by) % size) for i in range(size)])


def across_x(block):
    return jnp.stack([block] + [shift(block, "x", by) for by in (1, 2, 3)], 0)


def f32(*shape):
    return jax.ShapeDtypeStruct(shape, jnp.float32)


def body(state, in_pattern, out_pattern):
    rows, cols = state.shape
    nodes = cols * lax.axis_size("zl")
    at = jnp.stack(
        [lax.axis_index(ROWS)] + [lax.axis_index(a) for a in ("zl", "zh", "c", "x")]
    ).astype(jnp.int32)

    pieces = call(
        pieces_kernel,
        f32(4, PIECE, 128),
        [SMEM, SMEM, VMEM],
        (at, in_pattern, state),
        [pltpu.VMEM((rows, cols), jnp.float32)],
    )
    got = lax.all_to_all(pieces, "y", 0, 0)
    left, right = call(
        unpack_kernel, (f32(4, LEFT, 128), f32(2, 2 * RUN, cols)), [VMEM], (got,)
    )

    tie = lax.optimization_barrier
    up, down = shift(left, "zl", 1), shift(left, "zl", -1)
    far = shift(right, "zh", 1)
    near = across_x(right)
    lefts = [left, up, None, None, None, None, None, down]
    up, down, near, far = tie((up, down, near, far))
    up, down = shift(up, "zl", 1), shift(down, "zl", -1)
    far = across_x(far)
    near_swapped = shift(near, "c", 1)
    lefts[2], lefts[6] = up, down
    up, down, far, near_swapped = tie((up, down, far, near_swapped))
    up, down = shift(up, "zl", 1), shift(down, "zl", -1)
    far_swapped = shift(far, "c", 1)
    lefts[3], lefts[5] = up, down
    lefts[4] = shift(up, "zl", 1)

    partial = call(
        product_kernel,
        f32(4, rows, cols),
        [SMEM] + [VMEM] * 12,
        (at, *lefts, near, near_swapped, far, far_swapped),
        [pltpu.VMEM((8, 160, cols), jnp.bfloat16)] * 2,
        flops=3 * 10**9,
        size=6 * 10**6,
    )
    shares = lax.all_to_all(partial, "y", 0, 0)
    inflated, sums = call(
        inflate_kernel,
        (f32(rows, cols), f32(8, rows)),
        [SMEM, SMEM, VMEM],
        (at, out_pattern, shares),
    )
    sums = lax.all_to_all(sums.reshape(8, 1, rows), "zl", 0, 0).reshape(8, rows)
    return call(
        functools.partial(scale_kernel, float(nodes)),
        f32(rows, cols),
        [VMEM, VMEM],
        (inflated, sums),
    )


def solution(mesh):
    fine = Mesh(
        mesh.devices.reshape(8, 4, 4, 2, 2), ("zl", "x", "y", "zh", "c")
    )
    return jax.shard_map(
        body,
        mesh=fine,
        in_specs=(P(ROWS, "zl"), P(), P()),
        out_specs=P(ROWS, "zl"),
        check_vma=False,
    )
```

```python
import functools

import jax
import jax.numpy as jnp
from jax import lax
from jax.experimental import pallas as pl
from jax.experimental.pallas import tpu as pltpu
from jax.sharding import Mesh, PartitionSpec as P

BLK = 256
ROWS = ("x", "y", "zh", "c")
MAIN, REST = 80, 24
LEFT = MAIN + REST
RUN, PAD = 20, 24
PIECE = LEFT + 5 * PAD
VMEM = pl.BlockSpec(memory_space=pltpu.VMEM)
SMEM = pl.BlockSpec(memory_space=pltpu.SMEM)


def split(x):
    hi = x.astype(jnp.bfloat16)
    return hi, (x - hi.astype(jnp.float32)).astype(jnp.bfloat16)


def dot(a, b):
    return jnp.dot(a, b, preferred_element_type=jnp.float32)


def call(kernel, outs, in_specs, args, scratch=(), flops=10**6, size=10**6):
    return pl.pallas_call(
        kernel,
        out_shape=outs,
        in_specs=in_specs,
        out_specs=jax.tree.map(lambda _: VMEM, outs),
        scratch_shapes=scratch,
        compiler_params=pltpu.CompilerParams(vmem_limit_bytes=40 * 2**20),
        cost_estimate=pl.CostEstimate(
            flops=flops, bytes_accessed=size, transcendentals=0
        ),
    )(*args)


def masked_block(at_ref, owner, pattern_ref, h, x):
    row = owner * 80
    col = (5 * at_ref[1] + h) // 2
    first = row // BLK
    low = pattern_ref[first, col].astype(jnp.float32)
    high = pattern_ref[jnp.minimum(first + 1, 19), col].astype(jnp.float32)
    here = lax.broadcasted_iota(jnp.int32, (80, 128), 0) + row < (first + 1) * BLK
    return x * jnp.where(here, low, high)


def pack_right(at_ref, owner, pattern_ref, state_ref, masked_ref, out_ref, base):
    for h in range(5):
        lanes = slice(128 * h, 128 * h + 128)
        masked_ref[:, lanes] = masked_block(at_ref, owner, pattern_ref, h, state_ref[:, lanes])
    out_ref[...] = jnp.zeros_like(out_ref)
    for y in range(4):
        for h in range(5):
            rows = slice(base + PAD * h, base + PAD * h + RUN)
            out_ref[y, rows] = masked_ref[RUN * y : RUN * y + RUN, 128 * h : 128 * h + 128]


def far_kernel(at_ref, pattern_ref, state_ref, out_ref, masked_ref):
    owner = at_ref[0] + 2 - 4 * at_ref[2]
    pack_right(at_ref, owner, pattern_ref, state_ref, masked_ref, out_ref, 0)


def pieces_kernel(at_ref, pattern_ref, state_ref, out_ref, masked_ref):
    zh, c = at_ref[2], at_ref[3]
    pack_right(at_ref, at_ref[0], pattern_ref, state_ref, masked_ref, out_ref, LEFT)
    n = lax.broadcasted_iota(jnp.int32, (1, 640), 1)
    late = n >= 512
    y = jnp.where(late, (n - 512) // 32, n // 128)
    m = jnp.where(late, 128 + n % 32, n % 128)
    dzh, dc, y0, t = m // 80, m // 40 % 2, m // 20 % 2, m % 20
    zh_of = jnp.where(dzh == 0, zh, 1 - zh)
    c_of = jnp.where(dc == 0, c, 1 - c)
    source = 80 * (4 * y0 + 2 * zh_of + c_of) + 20 * y + t
    order = lax.broadcasted_iota(jnp.int32, (640, 640), 0) == source
    order = order.astype(jnp.float32).astype(jnp.bfloat16)
    x = masked_ref[...]
    hi, rest = x.astype(jnp.bfloat16), x
    rest = x - hi.astype(jnp.float32)
    mid, low = split(rest)
    moved = (dot(hi, order) + dot(mid, order)) + dot(low, order)
    lane = lax.broadcasted_iota(jnp.int32, (8, 128), 1) // 32
    for y in range(4):
        out_ref[y, :MAIN] = moved[:, 128 * y : 128 * y + 128]
        for slot in range(3):
            tile = jnp.zeros((8, 128), jnp.float32)
            for j in range(min(4, 10 - 4 * slot)):
                rows = 8 * (4 * slot + j)
                part = moved[rows : rows + 8, 512:]
                if j != y:
                    part = pltpu.roll(part, 32 * ((j - y) % 4), 1)
                tile = jnp.where(lane == j, part, tile)
            out_ref[y, MAIN + 8 * slot : MAIN + 8 * slot + 8] = tile


def unpack_right(got_ref, right_ref, base):
    for y in range(4):
        for h in range(5):
            right_ref[y // 2, RUN * (y % 2) : RUN * (y % 2) + RUN, 128 * h : 128 * h + 128] = (
                got_ref[y, base + PAD * h : base + PAD * h + RUN]
            )


def unpack_kernel(got_ref, left_ref, right_ref):
    left_ref[...] = got_ref[:, :LEFT]
    unpack_right(got_ref, right_ref, LEFT)


def unpack_far_kernel(got_ref, right_ref):
    unpack_right(got_ref, right_ref, 0)


def product_kernel(at_ref, left_ref, right_ref, out_ref, hi_ref, lo_ref):
    for dc in range(2):
        c = lax.rem(at_ref[3] + dc, 2)
        for dzh in range(2):
            rows = slice(40 * (2 * dzh + dc), 40 * (2 * dzh + dc) + 40)
            for x in range(4):
                for y1 in range(2):
                    hi, lo = split(right_ref[c, x, dzh, y1])
                    hi_ref[2 * x + y1, rows] = hi
                    lo_ref[2 * x + y1, rows] = lo
    lane = lax.broadcasted_iota(jnp.int32, (8, 128), 1) // 32
    total = jnp.zeros((320, 640), jnp.float32)
    for block in range(8):
        whole = []
        for y in range(4):
            rest = []
            for tile in range(10):
                rows = MAIN + 8 * (tile // 4)
                part = left_ref[block, y, rows : rows + 8]
                rest.append(jnp.where(lane == tile % 4, part, 0.0))
            rest = jnp.concatenate(rest, axis=0)
            whole.append(jnp.concatenate([left_ref[block, y, :MAIN], rest], axis=1))
        left_hi, left_lo = split(jnp.concatenate(whole, axis=0))
        right_hi, right_lo = hi_ref[block], lo_ref[block]
        right_hi = jnp.concatenate([right_hi] + [right_hi[128:]] * 3, axis=0)
        right_lo = jnp.concatenate([right_lo] + [right_lo[128:]] * 3, axis=0)
        total += dot(left_hi, right_hi) + (dot(left_hi, right_lo) + dot(left_lo, right_hi))
    out_ref[...] = total.reshape(4, 80, 640)


def inflate_kernel(at_ref, pattern_ref, shares_ref, out_ref, sums_ref):
    for h in range(5):
        lanes = slice(128 * h, 128 * h + 128)
        x = (shares_ref[0, :, lanes] + shares_ref[1, :, lanes]) + (
            shares_ref[2, :, lanes] + shares_ref[3, :, lanes]
        )
        out_ref[:, lanes] = masked_block(at_ref, at_ref[0], pattern_ref, h, x * x)
    sums_ref[...] = lax.dot_general(
        jnp.ones((8, 640), jnp.float32),
        out_ref[...],
        (((1,), (1,)), ((), ())),
        precision=lax.Precision.HIGHEST,
        preferred_element_type=jnp.float32,
    )


def scale_kernel(nodes, inflated_ref, sums_ref, out_ref):
    totals = lax.dot_general(
        sums_ref[...],
        jnp.ones((8, 128), jnp.float32),
        (((0,), (0,)), ((), ())),
        precision=lax.Precision.HIGHEST,
        preferred_element_type=jnp.float32,
    )
    scale = nodes / totals
    for h in range(5):
        lanes = slice(128 * h, 128 * h + 128)
        out_ref[:, lanes] = inflated_ref[:, lanes] * scale


def gather(block, axis_name):
    size = lax.axis_size(axis_name)
    copies = jnp.broadcast_to(block[None], (size,) + block.shape)
    return lax.all_to_all(copies, axis_name, 0, 0)


def f32(*shape):
    return jax.ShapeDtypeStruct(shape, jnp.float32)


def body(state, in_pattern, out_pattern):
    rows, cols = state.shape
    nodes = cols * lax.axis_size("zl")
    at = jnp.stack(
        [lax.axis_index(ROWS)] + [lax.axis_index(a) for a in ("zl", "zh", "c")]
    ).astype(jnp.int32)

    other = lax.ppermute(state, "zh", [(0, 1), (1, 0)])
    work = [pltpu.VMEM((rows, cols), jnp.float32)]
    pieces = call(
        pieces_kernel,
        f32(4, PIECE, 128),
        [SMEM, SMEM, VMEM],
        (at, in_pattern, state),
        work,
    )
    got = lax.all_to_all(pieces, "y", 0, 0)
    got, other = lax.optimization_barrier((got, other))
    left, near = call(
        unpack_kernel, (f32(4, LEFT, 128), f32(2, 2 * RUN, cols)), [VMEM], (got,)
    )
    far = call(
        far_kernel, f32(4, 5 * PAD, 128), [SMEM, SMEM, VMEM], (at, in_pattern, other), work
    )
    left, far = lax.optimization_barrier((left, far))
    left = lax.all_gather(left, "zl", axis=0)
    far = lax.all_to_all(far, "y", 0, 0)
    far = call(unpack_far_kernel, f32(2, 2 * RUN, cols), [VMEM], (far,))
    right = gather(gather(jnp.stack([near, far]), "x"), "c")

    partial = call(
        product_kernel,
        f32(4, rows, cols),
        [SMEM, VMEM, VMEM],
        (at, left, right),
        [pltpu.VMEM((8, 160, cols), jnp.bfloat16)] * 2,
        flops=3 * 10**9,
        size=6 * 10**6,
    )
    shares = lax.all_to_all(partial, "y", 0, 0)
    inflated, sums = call(
        inflate_kernel,
        (f32(rows, cols), f32(8, rows)),
        [SMEM, SMEM, VMEM],
        (at, out_pattern, shares),
    )
    sums = lax.all_to_all(sums.reshape(8, 1, rows), "zl", 0, 0).reshape(8, rows)
    return call(
        functools.partial(scale_kernel, float(nodes)),
        f32(rows, cols),
        [VMEM, VMEM],
        (inflated, sums),
    )


def solution(mesh):
    fine = Mesh(
        mesh.devices.reshape(8, 4, 4, 2, 2), ("zl", "x", "y", "zh", "c")
    )
    return jax.shard_map(
        body,
        mesh=fine,
        in_specs=(P(ROWS, "zl"), P(), P()),
        out_specs=P(ROWS, "zl"),
        check_vma=False,
    )
```

```python
import functools

import jax
import jax.numpy as jnp
from jax import lax
from jax.experimental import pallas as pl
from jax.experimental.pallas import tpu as pltpu
from jax.sharding import Mesh, PartitionSpec as P

BLK = 256
ROWS = ("x", "y", "zh", "c")
MAIN, REST = 80, 24
LEFT = MAIN + REST
RUN, PAD = 20, 24
PIECE = LEFT + 5 * PAD
VMEM = pl.BlockSpec(memory_space=pltpu.VMEM)
SMEM = pl.BlockSpec(memory_space=pltpu.SMEM)


def split(x):
    hi = x.astype(jnp.bfloat16)
    return hi, (x - hi.astype(jnp.float32)).astype(jnp.bfloat16)


def dot(a, b):
    return jnp.dot(a, b, preferred_element_type=jnp.float32)


def call(kernel, outs, in_specs, args, scratch=(), flops=10**6, size=10**6):
    return pl.pallas_call(
        kernel,
        out_shape=outs,
        in_specs=in_specs,
        out_specs=jax.tree.map(lambda _: VMEM, outs),
        scratch_shapes=scratch,
        compiler_params=pltpu.CompilerParams(vmem_limit_bytes=40 * 2**20),
        cost_estimate=pl.CostEstimate(
            flops=flops, bytes_accessed=size, transcendentals=0
        ),
    )(*args)


def masked_block(at_ref, owner, pattern_ref, h, x):
    row = owner * 80
    col = (5 * at_ref[1] + h) // 2
    first = row // BLK
    low = pattern_ref[first, col].astype(jnp.float32)
    high = pattern_ref[jnp.minimum(first + 1, 19), col].astype(jnp.float32)
    here = lax.broadcasted_iota(jnp.int32, (80, 128), 0) + row < (first + 1) * BLK
    return x * jnp.where(here, low, high)


def pack_right(at_ref, owner, pattern_ref, state_ref, masked_ref, out_ref, base):
    for h in range(5):
        lanes = slice(128 * h, 128 * h + 128)
        masked_ref[:, lanes] = masked_block(at_ref, owner, pattern_ref, h, state_ref[:, lanes])
    out_ref[...] = jnp.zeros_like(out_ref)
    for y in range(4):
        for h in range(5):
            rows = slice(base + PAD * h, base + PAD * h + RUN)
            out_ref[y, rows] = masked_ref[RUN * y : RUN * y + RUN, 128 * h : 128 * h + 128]


def far_kernel(at_ref, pattern_ref, state_ref, out_ref, masked_ref):
    owner = at_ref[0] + 2 - 4 * at_ref[2]
    pack_right(at_ref, owner, pattern_ref, state_ref, masked_ref, out_ref, 0)


def pieces_kernel(at_ref, pattern_ref, state_ref, out_ref, masked_ref):
    zh, c = at_ref[2], at_ref[3]
    pack_right(at_ref, at_ref[0], pattern_ref, state_ref, masked_ref, out_ref, LEFT)
    n = lax.broadcasted_iota(jnp.int32, (1, 640), 1)
    late = n >= 512
    y = jnp.where(late, (n - 512) // 32, n // 128)
    m = jnp.where(late, 128 + n % 32, n % 128)
    dzh, dc, y0, t = m // 80, m // 40 % 2, m // 20 % 2, m % 20
    zh_of = jnp.where(dzh == 0, zh, 1 - zh)
    c_of = jnp.where(dc == 0, c, 1 - c)
    source = 80 * (4 * y0 + 2 * zh_of + c_of) + 20 * y + t
    order = lax.broadcasted_iota(jnp.int32, (640, 640), 0) == source
    order = order.astype(jnp.float32).astype(jnp.bfloat16)
    x = masked_ref[...]
    hi, rest = x.astype(jnp.bfloat16), x
    rest = x - hi.astype(jnp.float32)
    mid, low = split(rest)
    moved = (dot(hi, order) + dot(mid, order)) + dot(low, order)
    lane = lax.broadcasted_iota(jnp.int32, (8, 128), 1) // 32
    for y in range(4):
        out_ref[y, :MAIN] = moved[:, 128 * y : 128 * y + 128]
        for slot in range(3):
            tile = jnp.zeros((8, 128), jnp.float32)
            for j in range(min(4, 10 - 4 * slot)):
                rows = 8 * (4 * slot + j)
                part = moved[rows : rows + 8, 512:]
                if j != y:
                    part = pltpu.roll(part, 32 * ((j - y) % 4), 1)
                tile = jnp.where(lane == j, part, tile)
            out_ref[y, MAIN + 8 * slot : MAIN + 8 * slot + 8] = tile


def unpack_right(got_ref, right_ref, base):
    for y in range(4):
        for h in range(5):
            right_ref[y // 2, RUN * (y % 2) : RUN * (y % 2) + RUN, 128 * h : 128 * h + 128] = (
                got_ref[y, base + PAD * h : base + PAD * h + RUN]
            )


def unpack_kernel(got_ref, left_ref, right_ref):
    left_ref[...] = got_ref[:, :LEFT]
    unpack_right(got_ref, right_ref, LEFT)


def unpack_far_kernel(got_ref, right_ref):
    unpack_right(got_ref, right_ref, 0)


def product_kernel(at_ref, *refs):
    lefts, rights, out_ref, hi_ref, lo_ref = refs[:8], refs[8:12], *refs[12:]
    for part, ref in enumerate(rights):
        for dx in range(4):
            for y1 in range(2):
                hi, lo = split(ref[dx, y1])
                rows = slice(40 * part, 40 * part + 40)
                hi_ref[2 * dx + y1, rows] = hi
                lo_ref[2 * dx + y1, rows] = lo
    lane = lax.broadcasted_iota(jnp.int32, (8, 128), 1) // 32
    zl, x = at_ref[1], at_ref[4]
    total = jnp.zeros((320, 640), jnp.float32)
    for d, ref in enumerate(lefts):
        source = lax.rem(zl - d + 8, 8)
        block = 2 * lax.rem(x - source // 2 + 4, 4) + lax.rem(source, 2)
        whole = []
        for y in range(4):
            rest = []
            for tile in range(10):
                rows = MAIN + 8 * (tile // 4)
                rest.append(jnp.where(lane == tile % 4, ref[y, rows : rows + 8], 0.0))
            rest = jnp.concatenate(rest, axis=0)
            whole.append(jnp.concatenate([ref[y, :MAIN], rest], axis=1))
        left_hi, left_lo = split(jnp.concatenate(whole, axis=0))
        right_hi, right_lo = hi_ref[block], lo_ref[block]
        right_hi = jnp.concatenate([right_hi] + [right_hi[128:]] * 3, axis=0)
        right_lo = jnp.concatenate([right_lo] + [right_lo[128:]] * 3, axis=0)
        total += dot(left_hi, right_hi) + (dot(left_hi, right_lo) + dot(left_lo, right_hi))
    out_ref[...] = total.reshape(4, 80, 640)


def inflate_kernel(at_ref, pattern_ref, shares_ref, out_ref, sums_ref):
    for h in range(5):
        lanes = slice(128 * h, 128 * h + 128)
        x = (shares_ref[0, :, lanes] + shares_ref[1, :, lanes]) + (
            shares_ref[2, :, lanes] + shares_ref[3, :, lanes]
        )
        out_ref[:, lanes] = masked_block(at_ref, at_ref[0], pattern_ref, h, x * x)
    sums_ref[...] = lax.dot_general(
        jnp.ones((8, 640), jnp.float32),
        out_ref[...],
        (((1,), (1,)), ((), ())),
        precision=lax.Precision.HIGHEST,
        preferred_element_type=jnp.float32,
    )


def scale_kernel(nodes, inflated_ref, sums_ref, out_ref):
    totals = lax.dot_general(
        sums_ref[...],
        jnp.ones((8, 128), jnp.float32),
        (((0,), (0,)), ((), ())),
        precision=lax.Precision.HIGHEST,
        preferred_element_type=jnp.float32,
    )
    scale = nodes / totals
    for h in range(5):
        lanes = slice(128 * h, 128 * h + 128)
        out_ref[:, lanes] = inflated_ref[:, lanes] * scale


def shift(x, axis_name, by):
    size = lax.axis_size(axis_name)
    return lax.ppermute(x, axis_name, [(i, (i + by) % size) for i in range(size)])


def across_x(block):
    return jnp.stack([block] + [shift(block, "x", by) for by in (1, 2, 3)], 0)


def f32(*shape):
    return jax.ShapeDtypeStruct(shape, jnp.float32)


def body(state, in_pattern, out_pattern):
    rows, cols = state.shape
    nodes = cols * lax.axis_size("zl")
    at = jnp.stack(
        [lax.axis_index(ROWS)] + [lax.axis_index(a) for a in ("zl", "zh", "c", "x")]
    ).astype(jnp.int32)

    tie = lax.optimization_barrier
    work = [pltpu.VMEM((rows, cols), jnp.float32)]
    far = shift(state, "zh", 1)
    pieces = call(
        pieces_kernel,
        f32(4, PIECE, 128),
        [SMEM, SMEM, VMEM],
        (at, in_pattern, state),
        work,
    )
    got = lax.all_to_all(pieces, "y", 0, 0)
    left, near = call(
        unpack_kernel, (f32(4, LEFT, 128), f32(2, 2 * RUN, cols)), [VMEM], (got,)
    )
    near = across_x(near)
    left, near, far = tie((left, near, far))

    up, down = shift(left, "zl", 1), shift(left, "zl", -1)
    far = call(
        far_kernel, f32(4, 5 * PAD, 128), [SMEM, SMEM, VMEM], (at, in_pattern, far), work
    )
    far = lax.all_to_all(far, "y", 0, 0)
    far = call(unpack_far_kernel, f32(2, 2 * RUN, cols), [VMEM], (far,))
    lefts = [left, up, None, None, None, None, None, down]
    up, down, far = tie((up, down, far))

    up, down = shift(up, "zl", 1), shift(down, "zl", -1)
    far = across_x(far)
    lefts[2], lefts[6] = up, down
    up, down, far = tie((up, down, far))

    up, down = shift(up, "zl", 1), shift(down, "zl", -1)
    near_swapped, far_swapped = shift(near, "c", 1), shift(far, "c", 1)
    lefts[3], lefts[5] = up, down
    lefts[4] = shift(up, "zl", 1)

    partial = call(
        product_kernel,
        f32(4, rows, cols),
        [SMEM] + [VMEM] * 12,
        (at, *lefts, near, near_swapped, far, far_swapped),
        [pltpu.VMEM((8, 160, cols), jnp.bfloat16)] * 2,
        flops=3 * 10**9,
        size=6 * 10**6,
    )
    shares = lax.all_to_all(partial, "y", 0, 0)
    inflated, sums = call(
        inflate_kernel,
        (f32(rows, cols), f32(8, rows)),
        [SMEM, SMEM, VMEM],
        (at, out_pattern, shares),
    )
    sums = lax.all_to_all(sums.reshape(8, 1, rows), "zl", 0, 0).reshape(8, rows)
    return call(
        functools.partial(scale_kernel, float(nodes)),
        f32(rows, cols),
        [VMEM, VMEM],
        (inflated, sums),
    )


def solution(mesh):
    fine = Mesh(
        mesh.devices.reshape(8, 4, 4, 2, 2), ("zl", "x", "y", "zh", "c")
    )
    return jax.shard_map(
        body,
        mesh=fine,
        in_specs=(P(ROWS, "zl"), P(), P()),
        out_specs=P(ROWS, "zl"),
        check_vma=False,
    )
```

```python
import functools

import jax
import jax.numpy as jnp
from jax import lax
from jax.experimental import pallas as pl
from jax.experimental.pallas import tpu as pltpu
from jax.sharding import Mesh, PartitionSpec as P

BLK = 256
ROWS = ("x", "y", "zh", "c")
MAIN, REST = 80, 24
LEFT = MAIN + REST
RUN, PAD = 20, 24
PIECE = LEFT + 5 * PAD
VMEM = pl.BlockSpec(memory_space=pltpu.VMEM)
SMEM = pl.BlockSpec(memory_space=pltpu.SMEM)


def split(x):
    hi = x.astype(jnp.bfloat16)
    return hi, (x - hi.astype(jnp.float32)).astype(jnp.bfloat16)


def dot(a, b):
    return jnp.dot(a, b, preferred_element_type=jnp.float32)


def call(kernel, outs, in_specs, args, scratch=(), flops=10**6, size=10**6):
    return pl.pallas_call(
        kernel,
        out_shape=outs,
        in_specs=in_specs,
        out_specs=jax.tree.map(lambda _: VMEM, outs),
        scratch_shapes=scratch,
        compiler_params=pltpu.CompilerParams(vmem_limit_bytes=40 * 2**20),
        cost_estimate=pl.CostEstimate(
            flops=flops, bytes_accessed=size, transcendentals=0
        ),
    )(*args)


def masked_block(at_ref, owner, pattern_ref, h, x):
    row = owner * 80
    col = (5 * at_ref[1] + h) // 2
    first = row // BLK
    low = pattern_ref[first, col].astype(jnp.float32)
    high = pattern_ref[jnp.minimum(first + 1, 19), col].astype(jnp.float32)
    here = lax.broadcasted_iota(jnp.int32, (80, 128), 0) + row < (first + 1) * BLK
    return x * jnp.where(here, low, high)


def pack_right(at_ref, owner, pattern_ref, state_ref, masked_ref, out_ref, base):
    for h in range(5):
        lanes = slice(128 * h, 128 * h + 128)
        masked_ref[:, lanes] = masked_block(at_ref, owner, pattern_ref, h, state_ref[:, lanes])
    out_ref[...] = jnp.zeros_like(out_ref)
    for y in range(4):
        for h in range(5):
            rows = slice(base + PAD * h, base + PAD * h + RUN)
            out_ref[y, rows] = masked_ref[RUN * y : RUN * y + RUN, 128 * h : 128 * h + 128]


def pieces_kernel(at_ref, pattern_ref, state_ref, out_ref, masked_ref):
    zh, c = at_ref[2], at_ref[3]
    pack_right(at_ref, at_ref[0], pattern_ref, state_ref, masked_ref, out_ref, LEFT)
    n = lax.broadcasted_iota(jnp.int32, (1, 640), 1)
    late = n >= 512
    y = jnp.where(late, (n - 512) // 32, n // 128)
    m = jnp.where(late, 128 + n % 32, n % 128)
    dzh, dc, y0, t = m // 80, m // 40 % 2, m // 20 % 2, m % 20
    zh_of = jnp.where(dzh == 0, zh, 1 - zh)
    c_of = jnp.where(dc == 0, c, 1 - c)
    source = 80 * (4 * y0 + 2 * zh_of + c_of) + 20 * y + t
    order = lax.broadcasted_iota(jnp.int32, (640, 640), 0) == source
    order = order.astype(jnp.float32).astype(jnp.bfloat16)
    x = masked_ref[...]
    hi, rest = x.astype(jnp.bfloat16), x
    rest = x - hi.astype(jnp.float32)
    mid, low = split(rest)
    moved = (dot(hi, order) + dot(mid, order)) + dot(low, order)
    lane = lax.broadcasted_iota(jnp.int32, (8, 128), 1) // 32
    for y in range(4):
        out_ref[y, :MAIN] = moved[:, 128 * y : 128 * y + 128]
        for slot in range(3):
            tile = jnp.zeros((8, 128), jnp.float32)
            for j in range(min(4, 10 - 4 * slot)):
                rows = 8 * (4 * slot + j)
                part = moved[rows : rows + 8, 512:]
                if j != y:
                    part = pltpu.roll(part, 32 * ((j - y) % 4), 1)
                tile = jnp.where(lane == j, part, tile)
            out_ref[y, MAIN + 8 * slot : MAIN + 8 * slot + 8] = tile


def unpack_right(got_ref, right_ref, base):
    for y in range(4):
        for h in range(5):
            right_ref[y // 2, RUN * (y % 2) : RUN * (y % 2) + RUN, 128 * h : 128 * h + 128] = (
                got_ref[y, base + PAD * h : base + PAD * h + RUN]
            )


def unpack_kernel(got_ref, left_ref, right_ref):
    left_ref[...] = got_ref[:, :LEFT]
    unpack_right(got_ref, right_ref, LEFT)


def product_kernel(at_ref, *refs):
    lefts, rights, out_ref, hi_ref, lo_ref = refs[:8], refs[8:10], *refs[10:]
    zl, zh = at_ref[1], at_ref[2]
    for dc, ref in enumerate(rights):
        for dzh in range(2):
            rows = slice(40 * (2 * dzh + dc), 40 * (2 * dzh + dc) + 40)
            for x in range(4):
                for y1 in range(2):
                    hi, lo = split(ref[2 * x + lax.rem(zh + dzh, 2), y1])
                    hi_ref[2 * x + y1, rows] = hi
                    lo_ref[2 * x + y1, rows] = lo
    lane = lax.broadcasted_iota(jnp.int32, (8, 128), 1) // 32
    total = jnp.zeros((320, 640), jnp.float32)
    for d, ref in enumerate(lefts):
        block = lax.rem(zl - d + 8, 8)
        whole = []
        for y in range(4):
            rest = []
            for tile in range(10):
                rows = MAIN + 8 * (tile // 4)
                rest.append(jnp.where(lane == tile % 4, ref[y, rows : rows + 8], 0.0))
            rest = jnp.concatenate(rest, axis=0)
            whole.append(jnp.concatenate([ref[y, :MAIN], rest], axis=1))
        left_hi, left_lo = split(jnp.concatenate(whole, axis=0))
        right_hi, right_lo = hi_ref[block], lo_ref[block]
        right_hi = jnp.concatenate([right_hi] + [right_hi[128:]] * 3, axis=0)
        right_lo = jnp.concatenate([right_lo] + [right_lo[128:]] * 3, axis=0)
        total += dot(left_hi, right_hi) + (dot(left_hi, right_lo) + dot(left_lo, right_hi))
    out_ref[...] = total.reshape(4, 80, 640)


def inflate_kernel(at_ref, pattern_ref, shares_ref, out_ref, sums_ref):
    for h in range(5):
        lanes = slice(128 * h, 128 * h + 128)
        x = (shares_ref[0, :, lanes] + shares_ref[1, :, lanes]) + (
            shares_ref[2, :, lanes] + shares_ref[3, :, lanes]
        )
        out_ref[:, lanes] = masked_block(at_ref, at_ref[0], pattern_ref, h, x * x)
    sums_ref[...] = lax.dot_general(
        jnp.ones((8, 640), jnp.float32),
        out_ref[...],
        (((1,), (1,)), ((), ())),
        precision=lax.Precision.HIGHEST,
        preferred_element_type=jnp.float32,
    )


def scale_kernel(nodes, inflated_ref, sums_ref, out_ref):
    totals = lax.dot_general(
        sums_ref[...],
        jnp.ones((8, 128), jnp.float32),
        (((0,), (0,)), ((), ())),
        precision=lax.Precision.HIGHEST,
        preferred_element_type=jnp.float32,
    )
    scale = nodes / totals
    for h in range(5):
        lanes = slice(128 * h, 128 * h + 128)
        out_ref[:, lanes] = inflated_ref[:, lanes] * scale


def shift(x, axis_name, by):
    size = lax.axis_size(axis_name)
    return lax.ppermute(x, axis_name, [(i, (i + by) % size) for i in range(size)])


def f32(*shape):
    return jax.ShapeDtypeStruct(shape, jnp.float32)


def body(state, in_pattern, out_pattern):
    rows, cols = state.shape
    nodes = cols * lax.axis_size("zl")
    at = jnp.stack(
        [lax.axis_index(ROWS)] + [lax.axis_index(a) for a in ("zl", "zh", "c")]
    ).astype(jnp.int32)

    pieces = call(
        pieces_kernel,
        f32(4, PIECE, 128),
        [SMEM, SMEM, VMEM],
        (at, in_pattern, state),
        [pltpu.VMEM((rows, cols), jnp.float32)],
    )
    got = lax.all_to_all(pieces, "y", 0, 0)
    left, right = call(
        unpack_kernel, (f32(4, LEFT, 128), f32(2, 2 * RUN, cols)), [VMEM], (got,)
    )

    right = lax.all_gather(right, ("x", "zh"), axis=0)
    lefts = [left] * 8
    for d in (1, 2, 3):
        lefts[d] = shift(lefts[d - 1], "zl", 1)
        lefts[8 - d] = shift(lefts[(9 - d) % 8], "zl", -1)
    lefts[3], lefts[5], right = lax.optimization_barrier((lefts[3], lefts[5], right))
    lefts[4] = shift(lefts[3], "zl", 1)
    swapped = shift(right, "c", 1)

    partial = call(
        product_kernel,
        f32(4, rows, cols),
        [SMEM] + [VMEM] * 10,
        (at, *lefts, right, swapped),
        [pltpu.VMEM((8, 160, cols), jnp.bfloat16)] * 2,
        flops=3 * 10**9,
        size=6 * 10**6,
    )
    shares = lax.all_to_all(partial, "y", 0, 0)
    inflated, sums = call(
        inflate_kernel,
        (f32(rows, cols), f32(8, rows)),
        [SMEM, SMEM, VMEM],
        (at, out_pattern, shares),
    )
    sums = lax.all_to_all(sums.reshape(8, 1, rows), "zl", 0, 0).reshape(8, rows)
    return call(
        functools.partial(scale_kernel, float(nodes)),
        f32(rows, cols),
        [VMEM, VMEM],
        (inflated, sums),
    )


def solution(mesh):
    fine = Mesh(
        mesh.devices.reshape(8, 4, 4, 2, 2), ("zl", "x", "y", "zh", "c")
    )
    return jax.shard_map(
        body,
        mesh=fine,
        in_specs=(P(ROWS, "zl"), P(), P()),
        out_specs=P(ROWS, "zl"),
        check_vma=False,
    )
```

```python
import functools

import jax
import jax.numpy as jnp
from jax import lax
from jax.experimental import pallas as pl
from jax.experimental.pallas import tpu as pltpu
from jax.sharding import Mesh, PartitionSpec as P

BLK = 256
ROWS = ("x", "y", "zh", "c")
MAIN, REST = 80, 24
LEFT = MAIN + REST
RUN, PAD = 20, 24
PIECE = LEFT + 5 * PAD
VMEM = pl.BlockSpec(memory_space=pltpu.VMEM)
SMEM = pl.BlockSpec(memory_space=pltpu.SMEM)


def split(x):
    hi = x.astype(jnp.bfloat16)
    return hi, (x - hi.astype(jnp.float32)).astype(jnp.bfloat16)


def dot(a, b):
    return jnp.dot(a, b, preferred_element_type=jnp.float32)


def call(kernel, outs, in_specs, args, scratch=(), flops=10**6, size=10**6):
    return pl.pallas_call(
        kernel,
        out_shape=outs,
        in_specs=in_specs,
        out_specs=jax.tree.map(lambda _: VMEM, outs),
        scratch_shapes=scratch,
        compiler_params=pltpu.CompilerParams(vmem_limit_bytes=40 * 2**20),
        cost_estimate=pl.CostEstimate(
            flops=flops, bytes_accessed=size, transcendentals=0
        ),
    )(*args)


def masked_block(at_ref, owner, pattern_ref, h, x):
    row = owner * 80
    col = (5 * at_ref[1] + h) // 2
    first = row // BLK
    low = pattern_ref[first, col].astype(jnp.float32)
    high = pattern_ref[jnp.minimum(first + 1, 19), col].astype(jnp.float32)
    here = lax.broadcasted_iota(jnp.int32, (80, 128), 0) + row < (first + 1) * BLK
    return x * jnp.where(here, low, high)


def pack_right(at_ref, owner, pattern_ref, state_ref, masked_ref, out_ref, base):
    for h in range(5):
        lanes = slice(128 * h, 128 * h + 128)
        masked_ref[:, lanes] = masked_block(at_ref, owner, pattern_ref, h, state_ref[:, lanes])
    out_ref[...] = jnp.zeros_like(out_ref)
    for y in range(4):
        for h in range(5):
            rows = slice(base + PAD * h, base + PAD * h + RUN)
            out_ref[y, rows] = masked_ref[RUN * y : RUN * y + RUN, 128 * h : 128 * h + 128]


def far_kernel(at_ref, pattern_ref, top_ref, bottom_ref, out_ref, state_ref, masked_ref):
    state_ref[:40] = top_ref[...]
    state_ref[40:] = bottom_ref[...]
    owner = at_ref[0] + 2 - 4 * at_ref[2]
    pack_right(at_ref, owner, pattern_ref, state_ref, masked_ref, out_ref, 0)


def pieces_kernel(at_ref, pattern_ref, state_ref, out_ref, masked_ref):
    zh, c = at_ref[2], at_ref[3]
    pack_right(at_ref, at_ref[0], pattern_ref, state_ref, masked_ref, out_ref, LEFT)
    n = lax.broadcasted_iota(jnp.int32, (1, 640), 1)
    late = n >= 512
    y = jnp.where(late, (n - 512) // 32, n // 128)
    m = jnp.where(late, 128 + n % 32, n % 128)
    dzh, dc, y0, t = m // 80, m // 40 % 2, m // 20 % 2, m % 20
    zh_of = jnp.where(dzh == 0, zh, 1 - zh)
    c_of = jnp.where(dc == 0, c, 1 - c)
    source = 80 * (4 * y0 + 2 * zh_of + c_of) + 20 * y + t
    order = lax.broadcasted_iota(jnp.int32, (640, 640), 0) == source
    order = order.astype(jnp.float32).astype(jnp.bfloat16)
    x = masked_ref[...]
    hi, rest = x.astype(jnp.bfloat16), x
    rest = x - hi.astype(jnp.float32)
    mid, low = split(rest)
    moved = (dot(hi, order) + dot(mid, order)) + dot(low, order)
    lane = lax.broadcasted_iota(jnp.int32, (8, 128), 1) // 32
    for y in range(4):
        out_ref[y, :MAIN] = moved[:, 128 * y : 128 * y + 128]
        for slot in range(3):
            tile = jnp.zeros((8, 128), jnp.float32)
            for j in range(min(4, 10 - 4 * slot)):
                rows = 8 * (4 * slot + j)
                part = moved[rows : rows + 8, 512:]
                if j != y:
                    part = pltpu.roll(part, 32 * ((j - y) % 4), 1)
                tile = jnp.where(lane == j, part, tile)
            out_ref[y, MAIN + 8 * slot : MAIN + 8 * slot + 8] = tile


def unpack_right(got_ref, right_ref, base):
    for y in range(4):
        for h in range(5):
            right_ref[y // 2, RUN * (y % 2) : RUN * (y % 2) + RUN, 128 * h : 128 * h + 128] = (
                got_ref[y, base + PAD * h : base + PAD * h + RUN]
            )


def unpack_kernel(got_ref, left_ref, right_ref):
    left_ref[...] = got_ref[:, :LEFT]
    unpack_right(got_ref, right_ref, LEFT)


def unpack_far_kernel(got_ref, right_ref):
    unpack_right(got_ref, right_ref, 0)


def product_kernel(at_ref, *refs):
    lefts, rights, out_ref, hi_ref, lo_ref = refs[:8], refs[8:12], *refs[12:]
    zl = at_ref[1]
    for part, ref in enumerate(rights):
        rows = slice(40 * part, 40 * part + 40)
        for x in range(4):
            for y1 in range(2):
                hi, lo = split(ref[x, y1])
                hi_ref[2 * x + y1, rows] = hi
                lo_ref[2 * x + y1, rows] = lo
    lane = lax.broadcasted_iota(jnp.int32, (8, 128), 1) // 32
    total = jnp.zeros((320, 640), jnp.float32)
    for d, ref in enumerate(lefts):
        block = lax.rem(zl - d + 8, 8)
        whole = []
        for y in range(4):
            rest = []
            for tile in range(10):
                rows = MAIN + 8 * (tile // 4)
                rest.append(jnp.where(lane == tile % 4, ref[y, rows : rows + 8], 0.0))
            rest = jnp.concatenate(rest, axis=0)
            whole.append(jnp.concatenate([ref[y, :MAIN], rest], axis=1))
        left_hi, left_lo = split(jnp.concatenate(whole, axis=0))
        right_hi, right_lo = hi_ref[block], lo_ref[block]
        right_hi = jnp.concatenate([right_hi] + [right_hi[128:]] * 3, axis=0)
        right_lo = jnp.concatenate([right_lo] + [right_lo[128:]] * 3, axis=0)
        total += dot(left_hi, right_hi) + (dot(left_hi, right_lo) + dot(left_lo, right_hi))
    out_ref[...] = total.reshape(4, 80, 640)


def inflate_kernel(at_ref, pattern_ref, shares_ref, out_ref, sums_ref):
    for h in range(5):
        lanes = slice(128 * h, 128 * h + 128)
        x = (shares_ref[0, :, lanes] + shares_ref[1, :, lanes]) + (
            shares_ref[2, :, lanes] + shares_ref[3, :, lanes]
        )
        out_ref[:, lanes] = masked_block(at_ref, at_ref[0], pattern_ref, h, x * x)
    sums_ref[...] = lax.dot_general(
        jnp.ones((8, 640), jnp.float32),
        out_ref[...],
        (((1,), (1,)), ((), ())),
        precision=lax.Precision.HIGHEST,
        preferred_element_type=jnp.float32,
    )


def scale_kernel(nodes, inflated_ref, sums_ref, out_ref):
    totals = lax.dot_general(
        sums_ref[...],
        jnp.ones((8, 128), jnp.float32),
        (((0,), (0,)), ((), ())),
        precision=lax.Precision.HIGHEST,
        preferred_element_type=jnp.float32,
    )
    scale = nodes / totals
    for h in range(5):
        lanes = slice(128 * h, 128 * h + 128)
        out_ref[:, lanes] = inflated_ref[:, lanes] * scale


def shift(x, axis_name, by):
    size = lax.axis_size(axis_name)
    return lax.ppermute(x, axis_name, [(i, (i + by) % size) for i in range(size)])


def shift_z(x, by):
    pairs = []
    for z in range(16):
        to = (z + by) % 16
        pairs.append((z % 8 * 2 + z // 8, to % 8 * 2 + to // 8))
    return lax.ppermute(x, ("zl", "zh"), pairs)


def f32(*shape):
    return jax.ShapeDtypeStruct(shape, jnp.float32)


def body(state, in_pattern, out_pattern):
    rows, cols = state.shape
    nodes = cols * lax.axis_size("zl")
    at = jnp.stack(
        [lax.axis_index(ROWS)] + [lax.axis_index(a) for a in ("zl", "zh", "c")]
    ).astype(jnp.int32)

    tie = lax.optimization_barrier
    work = pltpu.VMEM((rows, cols), jnp.float32)
    top, bottom = shift_z(state[:40], 4), shift_z(state[40:], -4)
    pieces = call(
        pieces_kernel, f32(4, PIECE, 128), [SMEM, SMEM, VMEM], (at, in_pattern, state), [work]
    )
    got = lax.all_to_all(pieces, "y", 0, 0)
    top, bottom, got = tie((top, bottom, got))

    top, bottom = shift_z(top, 4), shift_z(bottom, -4)
    left, near = call(
        unpack_kernel, (f32(4, LEFT, 128), f32(2, 2 * RUN, cols)), [VMEM], (got,)
    )
    near = lax.all_gather(near, "x", axis=0)
    top, bottom, left, near = tie((top, bottom, left, near))

    up, down = shift(left, "zl", 1), shift(left, "zl", -1)
    far = call(
        far_kernel,
        f32(4, 5 * PAD, 128),
        [SMEM, SMEM, VMEM, VMEM],
        (at, in_pattern, top, bottom),
        [work, work],
    )
    far = lax.all_to_all(far, "y", 0, 0)
    far = call(unpack_far_kernel, f32(2, 2 * RUN, cols), [VMEM], (far,))
    lefts = [left, up, None, None, None, None, None, down]
    up, down, far, near = tie((up, down, far, near))

    up, down = shift(up, "zl", 1), shift(down, "zl", -1)
    far = lax.all_gather(far, "x", axis=0)
    near_swapped = shift(near, "c", 1)
    lefts[2], lefts[6] = up, down
    up, down, far, near_swapped = tie((up, down, far, near_swapped))

    up, down = shift(up, "zl", 1), shift(down, "zl", -1)
    far_swapped = shift(far, "c", 1)
    lefts[3], lefts[5] = up, down
    lefts[4] = shift(up, "zl", 1)

    partial = call(
        product_kernel,
        f32(4, rows, cols),
        [SMEM] + [VMEM] * 12,
        (at, *lefts, near, near_swapped, far, far_swapped),
        [pltpu.VMEM((8, 160, cols), jnp.bfloat16)] * 2,
        flops=3 * 10**9,
        size=6 * 10**6,
    )
    shares = lax.all_to_all(partial, "y", 0, 0)
    inflated, sums = call(
        inflate_kernel,
        (f32(rows, cols), f32(8, rows)),
        [SMEM, SMEM, VMEM],
        (at, out_pattern, shares),
    )
    sums = lax.all_to_all(sums.reshape(8, 1, rows), "zl", 0, 0).reshape(8, rows)
    return call(
        functools.partial(scale_kernel, float(nodes)),
        f32(rows, cols),
        [VMEM, VMEM],
        (inflated, sums),
    )


def solution(mesh):
    fine = Mesh(
        mesh.devices.reshape(8, 4, 4, 2, 2), ("zl", "x", "y", "zh", "c")
    )
    return jax.shard_map(
        body,
        mesh=fine,
        in_specs=(P(ROWS, "zl"), P(), P()),
        out_specs=P(ROWS, "zl"),
        check_vma=False,
    )
```

```python
import functools

import jax
import jax.numpy as jnp
from jax import lax
from jax.experimental import pallas as pl
from jax.experimental.pallas import tpu as pltpu
from jax.sharding import Mesh, PartitionSpec as P

BLK = 256
ROWS = ("x", "y", "zh", "c")
SLOTS = 248
ALL = 400
UNITS = 56
VMEM = pl.BlockSpec(memory_space=pltpu.VMEM)
SMEM = pl.BlockSpec(memory_space=pltpu.SMEM)
EXACT = lax.Precision.HIGHEST


def iota(shape, axis):
    return lax.broadcasted_iota(jnp.int32, shape, axis)


def one_hot(mask):
    return mask.astype(jnp.float32).astype(jnp.bfloat16)


def split(x):
    hi = x.astype(jnp.bfloat16)
    return hi, (x - hi.astype(jnp.float32)).astype(jnp.bfloat16)


def split3(x):
    hi = x.astype(jnp.bfloat16)
    return (hi, *split(x - hi.astype(jnp.float32)))


def dot(a, b, precision=None):
    return jnp.dot(a, b, preferred_element_type=jnp.float32, precision=precision)


def dot_rows(a, b, precision=None):
    return lax.dot_general(
        a, b, (((1,), (1,)), ((), ())), precision=precision, preferred_element_type=jnp.float32
    )


def call(kernel, outs, in_specs, args, out_specs=None, scratch=(), flops=10**6, size=10**6):
    return pl.pallas_call(
        kernel,
        out_shape=outs,
        in_specs=in_specs,
        out_specs=out_specs or jax.tree.map(lambda _: VMEM, outs),
        scratch_shapes=scratch,
        compiler_params=pltpu.CompilerParams(vmem_limit_bytes=48 * 2**20),
        cost_estimate=pl.CostEstimate(flops=flops, bytes_accessed=size, transcendentals=0),
    )(*args)


def chunk_of(q, zh, c):
    return 20 * (q // 5) + 10 * zh + 5 * c + q % 5


def places(pattern, zh, c):
    rows = one_hot(chunk_of(iota((80, 1), 0), zh, c) // 16 == iota((80, 20), 1))
    cols = one_hot(iota((20, 40), 1) // 2 == iota((20, 40), 0))
    live = dot(dot(rows, pattern).astype(jnp.bfloat16), cols)
    before = dot(one_hot(iota((80, 80), 1) < iota((80, 80), 0)), live.astype(jnp.bfloat16))
    total = jnp.broadcast_to(jnp.sum(live, axis=0, keepdims=True), (80, 40))
    a, b = iota((40, 40), 0), iota((40, 40), 1)
    earlier = dot(total.astype(jnp.bfloat16), one_hot((a // 5 == b // 5) & (a < b)))
    return jnp.where(live > 0, before + earlier, -1.0)


def places_across(pattern, zh, c):
    rows = one_hot(chunk_of(iota((1, 80), 1), zh, c) // 16 == iota((20, 80), 0))
    cols = one_hot(iota((40, 20), 0) // 2 == iota((40, 20), 1))
    live = dot(dot_rows(cols, pattern).astype(jnp.bfloat16), rows)
    before = dot(live.astype(jnp.bfloat16), one_hot(iota((80, 80), 0) < iota((80, 80), 1)))
    total = jnp.broadcast_to(jnp.sum(live, axis=1, keepdims=True), (40, 80))
    a, b = iota((40, 40), 1), iota((40, 40), 0)
    earlier = dot(one_hot((a // 5 == b // 5) & (a < b)), total.astype(jnp.bfloat16))
    return jnp.where(live > 0, before + earlier, -1.0)


def units_kernel(pattern_ref, state_ref, out_ref, most_ref, moved_ref, plain_ref):
    pattern = pattern_ref[...].astype(jnp.float32).astype(jnp.bfloat16)
    counts = []
    for group in range(4):
        rows = chunk_of(iota((80, 1), 0), group // 2, group % 2) // 16 == iota((80, 20), 1)
        counts.append(jnp.sum(rows.astype(jnp.float32), axis=0, keepdims=True))
    counts = jnp.concatenate(counts * 2, axis=0).astype(jnp.bfloat16)
    wide = jnp.zeros((20, 8), jnp.float32)
    for h in range(5):
        wide += ((5 * iota((20, 8), 1) + h) // 2 == iota((20, 8), 0)).astype(jnp.float32)
    most = dot(dot(counts, pattern).astype(jnp.bfloat16), wide.astype(jnp.bfloat16))
    most_ref[0, 0] = jnp.max(most).astype(jnp.int32)

    n = iota((1, 128), 1)
    source = 16 * (n % 32 // 4) + 4 * (n // 32) + n % 4
    order = one_hot(iota((128, 128), 0) == source)
    for h in range(5):
        lanes = slice(128 * h, 128 * h + 128)
        plain_ref[h] = state_ref[:, lanes]
        hi, mid, low = split3(state_ref[:, lanes])
        moved_ref[h] = (dot(hi, order) + dot(mid, order)) + dot(low, order)
    lane = iota((5, 128), 1) // 32
    for x in range(4):
        for y in range(4):
            for h in range(5):
                unit = jnp.zeros((5, 128), jnp.float32)
                for r in range(4):
                    part = moved_ref[h, pl.ds(4 * x + r, 5, stride=16), :]
                    if r != y:
                        part = pltpu.roll(part, 32 * ((r - y) % 4), 1)
                    unit = jnp.where(lane == r, part, unit)
                out_ref[4 * x + y, 5 * h : 5 * h + 5] = unit
                out_ref[4 * x + y, 25 + 5 * h : 30 + 5 * h] = plain_ref[
                    h, pl.ds(4 * y + x, 5, stride=16), :
                ]
            out_ref[4 * x + y, 50:] = jnp.zeros((UNITS - 50, 128), jnp.float32)


def pack_kernel(slots, at_ref, pattern_ref, got_ref, left_ref, right_ref):
    pattern = pattern_ref[...].astype(jnp.float32).astype(jnp.bfloat16)
    place = places_across(pattern, at_ref[2], at_ref[3])
    count = 16 * UNITS
    units = jnp.concatenate(split3(got_ref[...].reshape(count, 128)), axis=1)
    row = iota((1, count), 1)
    for start, ref in ((0, left_ref), (25, right_ref)):
        j = row % UNITS - start
        inside = (j >= 0) & (j < 25)
        q = 5 * (row // UNITS) + j % 5
        expand = (q == iota((80, count), 0)).astype(jnp.float32)
        spread = dot(place, expand, EXACT)
        mine = 5 * at_ref[1] + j // 5 == iota((40, count), 0)
        slot = jnp.sum(jnp.where(mine, spread, 0.0), axis=0, keepdims=True)
        slot = jnp.where(inside, slot, -1.0)
        pick = one_hot(slot == iota((slots, count), 0).astype(jnp.float32))
        got = dot(pick, units)
        ref[...] = (got[:, :128] + got[:, 128:256]) + got[:, 256:]


def product_kernel(slots, at_ref, pattern_ref, packed_ref, own_ref, swap_ref, out_ref, left_ref, right_ref):
    pattern = pattern_ref[...].astype(jnp.float32).astype(jnp.bfloat16)
    zl, zh, c = at_ref[1], at_ref[2], at_ref[3]
    slot = iota((80, slots), 1).astype(jnp.float32)

    half = iota((80, 40), 1)
    for dc, ref in ((0, own_ref), (1, swap_ref)):
        for dzh in range(2):
            place = places(pattern, jnp.abs(zh - dzh), jnp.abs(c - dc))
            pick = []
            for h in range(5):
                at = jnp.sum(jnp.where(half == 5 * zl + h, place, 0.0), axis=1, keepdims=True)
                pick.append(one_hot(at == slot))
            pick = jnp.concatenate(pick, axis=0)
            for t in range(4):
                got = dot(pick, jnp.concatenate(split(ref[t, dzh]), axis=1))
                got = got[:, :128] + got[:, 128:]
                base = 40 * (4 * (2 * dzh + dc) + t)
                for h in range(5):
                    for g in range(2):
                        right_ref[g, base : base + 40, 128 * h : 128 * h + 128] = got[
                            80 * h + 40 * g : 80 * h + 40 * g + 40
                        ]

    place = places(pattern, zh, c)
    lane = iota((80, 128), 1) // 32
    units, group = [], 0
    for z in range(8):
        pick = jnp.concatenate(
            [one_hot(place[:, 5 * z + h : 5 * z + h + 1] == slot) for h in range(5)], axis=0
        )
        got = dot(pick, jnp.concatenate(split(packed_ref[z]), axis=1))
        got = got[:, :128] + got[:, 128:]
        units += [got[80 * h : 80 * h + 80] for h in range(5)]
        while len(units) >= 4:
            four, units = units[:4], units[4:]
            for r in range(4):
                tile = jnp.zeros((80, 128), jnp.float32)
                for j in range(4):
                    moved = four[j]
                    if j != r:
                        moved = pltpu.roll(moved, 32 * ((j - r) % 4), 1)
                    tile = jnp.where(lane == j, moved, tile)
                left_ref[80 * r : 80 * r + 80, 128 * group : 128 * group + 128] = tile
            group += 1

    to = iota((320, 1), 0)
    rows = one_hot(to % 20 // 5 * 80 + to // 20 * 5 + to % 5 == iota((320, 320), 1))
    m = iota((1, 640), 1)
    p, x0, y, e = m // 40, m % 40 // 20, m % 20 // 5, m % 5
    zh_of, c_of = jnp.abs(zh - p // 8), jnp.abs(c - p // 4 % 2)
    source = 160 * (2 * x0 + y // 2) + 4 * (20 * (y % 2) + 10 * zh_of + 5 * c_of + e) + p % 4
    cols = one_hot(iota((640, 640), 0) == source)
    total = jnp.zeros((320, 640), jnp.float32)
    for g in range(2):
        left = []
        for part in split(left_ref[:, 640 * g : 640 * g + 640]):
            part = dot(rows, part).astype(jnp.bfloat16)
            left.append(dot(part, cols).astype(jnp.bfloat16))
        right = split(right_ref[g])
        total += dot(left[0], right[0]) + (dot(left[0], right[1]) + dot(left[1], right[0]))
    out_ref[...] = total.reshape(16, 20, 640)


def inflate_kernel(at_ref, pattern_ref, shares_ref, out_ref, sums_ref, sum_ref):
    for x in range(4):
        total = (shares_ref[4 * x] + shares_ref[4 * x + 1]) + (
            shares_ref[4 * x + 2] + shares_ref[4 * x + 3]
        )
        for r in range(4):
            for h in range(5):
                lanes = slice(128 * h, 128 * h + 128)
                sum_ref[h, pl.ds(4 * x + r, 5, stride=16), :] = total[5 * r : 5 * r + 5, lanes]
    row = at_ref[0] * 80
    first = row // BLK
    here = iota((80, 128), 0) + row < (first + 1) * BLK
    for h in range(5):
        lanes = slice(128 * h, 128 * h + 128)
        col = (5 * at_ref[1] + h) // 2
        low = pattern_ref[first, col].astype(jnp.float32)
        high = pattern_ref[jnp.minimum(first + 1, 19), col].astype(jnp.float32)
        value = sum_ref[h]
        out_ref[:, lanes] = value * value * jnp.where(here, low, high)
    sums_ref[...] = dot_rows(jnp.ones((8, 640), jnp.float32), out_ref[...], EXACT)


def scale_kernel(nodes, inflated_ref, sums_ref, out_ref):
    totals = lax.dot_general(
        sums_ref[...],
        jnp.ones((8, 128), jnp.float32),
        (((0,), (0,)), ((), ())),
        precision=EXACT,
        preferred_element_type=jnp.float32,
    )
    scale = nodes / totals
    for h in range(5):
        lanes = slice(128 * h, 128 * h + 128)
        out_ref[:, lanes] = inflated_ref[:, lanes] * scale


def swap(x, axis_name):
    return lax.ppermute(x, axis_name, [(0, 1), (1, 0)])


def f32(*shape):
    return jax.ShapeDtypeStruct(shape, jnp.float32)


def gather(x, axis_name, limit):
    rows = x.shape[-2]
    parts = -(-rows // limit)
    size = rows // parts
    done = [
        lax.all_gather(x[..., i * size : (i + 1) * size, :], axis_name, axis=0)
        for i in range(parts)
    ]
    return done[0] if parts == 1 else jnp.concatenate(done, axis=-2)


def partial_product(slots, at, in_pattern, got):
    left, right = call(
        functools.partial(pack_kernel, slots),
        (f32(slots, 128), f32(slots, 128)),
        [SMEM, VMEM, VMEM],
        (at, in_pattern, got),
    )
    far = swap(right, "zh")
    left = gather(left, "zl", SLOTS)
    left, far = lax.optimization_barrier((left, far))
    own = gather(jnp.stack([right, far]), "x", SLOTS)
    return call(
        functools.partial(product_kernel, slots),
        f32(16, 20, 640),
        [SMEM] + [VMEM] * 4,
        (at, in_pattern, left, own, swap(own, "c")),
        scratch=[pltpu.VMEM((320, 1280), jnp.float32), pltpu.VMEM((2, 640, 640), jnp.float32)],
        flops=5 * 10**9,
        size=5 * 10**6,
    )


def body(state, in_pattern, out_pattern):
    rows, cols = state.shape
    nodes = cols * lax.axis_size("zl")
    at = jnp.stack([lax.axis_index(ROWS)] + [lax.axis_index(a) for a in ("zl", "zh", "c")])
    at = at.astype(jnp.int32)
    units, most = call(
        units_kernel,
        (f32(16, UNITS, 128), jax.ShapeDtypeStruct((1, 1), jnp.int32)),
        [VMEM, VMEM],
        (in_pattern, state),
        out_specs=(VMEM, SMEM),
        scratch=[pltpu.VMEM((5, rows, 128), jnp.float32)] * 2,
    )
    got = lax.all_to_all(units, ("x", "y"), 0, 0)
    shares = lax.cond(
        most[0, 0] <= SLOTS,
        functools.partial(partial_product, SLOTS),
        functools.partial(partial_product, ALL),
        at,
        in_pattern,
        got,
    )
    shares = lax.all_to_all(shares, ("x", "y"), 0, 0)
    inflated, sums = call(
        inflate_kernel,
        (f32(rows, cols), f32(8, rows)),
        [SMEM, SMEM, VMEM],
        (at, out_pattern, shares),
        scratch=[pltpu.VMEM((5, rows, 128), jnp.float32)],
    )
    sums = lax.all_to_all(sums.reshape(8, 1, rows), "zl", 0, 0).reshape(8, rows)
    return call(
        functools.partial(scale_kernel, float(nodes)),
        f32(rows, cols),
        [VMEM, VMEM],
        (inflated, sums),
    )


def solution(mesh):
    fine = Mesh(
        mesh.devices.reshape(8, 4, 4, 2, 2), ("zl", "x", "y", "zh", "c")
    )
    return jax.shard_map(
        body,
        mesh=fine,
        in_specs=(P(ROWS, "zl"), P(), P()),
        out_specs=P(ROWS, "zl"),
        check_vma=False,
    )
```

```python
import functools

import jax
import jax.numpy as jnp
from jax import lax
from jax.experimental import pallas as pl
from jax.experimental.pallas import tpu as pltpu
from jax.sharding import Mesh, PartitionSpec as P

BLK = 256
ROWS = ("x", "y", "zh", "c")
SLOTS = 248
ALL = 400
UNITS = 56
VMEM = pl.BlockSpec(memory_space=pltpu.VMEM)
SMEM = pl.BlockSpec(memory_space=pltpu.SMEM)
EXACT = lax.Precision.HIGHEST


def iota(shape, axis):
    return lax.broadcasted_iota(jnp.int32, shape, axis)


def one_hot(mask):
    return mask.astype(jnp.float32).astype(jnp.bfloat16)


def split(x):
    hi = x.astype(jnp.bfloat16)
    return hi, (x - hi.astype(jnp.float32)).astype(jnp.bfloat16)


def split3(x):
    hi = x.astype(jnp.bfloat16)
    return (hi, *split(x - hi.astype(jnp.float32)))


def dot(a, b, precision=None):
    return jnp.dot(a, b, preferred_element_type=jnp.float32, precision=precision)


def dot_rows(a, b, precision=None):
    return lax.dot_general(
        a, b, (((1,), (1,)), ((), ())), precision=precision, preferred_element_type=jnp.float32
    )


def call(kernel, outs, in_specs, args, out_specs=None, scratch=(), flops=10**6, size=10**6):
    return pl.pallas_call(
        kernel,
        out_shape=outs,
        in_specs=in_specs,
        out_specs=out_specs or jax.tree.map(lambda _: VMEM, outs),
        scratch_shapes=scratch,
        compiler_params=pltpu.CompilerParams(vmem_limit_bytes=48 * 2**20),
        cost_estimate=pl.CostEstimate(flops=flops, bytes_accessed=size, transcendentals=0),
    )(*args)


def chunk_of(q, zh, c):
    return 20 * (q // 5) + 10 * zh + 5 * c + q % 5


def places(pattern, zh, c):
    rows = one_hot(chunk_of(iota((80, 1), 0), zh, c) // 16 == iota((80, 20), 1))
    cols = one_hot(iota((20, 40), 1) // 2 == iota((20, 40), 0))
    live = dot(dot(rows, pattern).astype(jnp.bfloat16), cols)
    before = dot(one_hot(iota((80, 80), 1) < iota((80, 80), 0)), live.astype(jnp.bfloat16))
    total = jnp.broadcast_to(jnp.sum(live, axis=0, keepdims=True), (80, 40))
    a, b = iota((40, 40), 0), iota((40, 40), 1)
    earlier = dot(total.astype(jnp.bfloat16), one_hot((a // 5 == b // 5) & (a < b)))
    return jnp.where(live > 0, before + earlier, -1.0)


def places_across(pattern, zh, c):
    rows = one_hot(chunk_of(iota((1, 80), 1), zh, c) // 16 == iota((20, 80), 0))
    cols = one_hot(iota((40, 20), 0) // 2 == iota((40, 20), 1))
    live = dot(dot_rows(cols, pattern).astype(jnp.bfloat16), rows)
    before = dot(live.astype(jnp.bfloat16), one_hot(iota((80, 80), 0) < iota((80, 80), 1)))
    total = jnp.broadcast_to(jnp.sum(live, axis=1, keepdims=True), (40, 80))
    a, b = iota((40, 40), 1), iota((40, 40), 0)
    earlier = dot(one_hot((a // 5 == b // 5) & (a < b)), total.astype(jnp.bfloat16))
    return jnp.where(live > 0, before + earlier, -1.0)


def units_kernel(pattern_ref, state_ref, out_ref, most_ref, moved_ref, plain_ref):
    pattern = pattern_ref[...].astype(jnp.float32).astype(jnp.bfloat16)
    counts = []
    for group in range(4):
        rows = chunk_of(iota((80, 1), 0), group // 2, group % 2) // 16 == iota((80, 20), 1)
        counts.append(jnp.sum(rows.astype(jnp.float32), axis=0, keepdims=True))
    counts = jnp.concatenate(counts * 2, axis=0).astype(jnp.bfloat16)
    wide = jnp.zeros((20, 8), jnp.float32)
    for h in range(5):
        wide += ((5 * iota((20, 8), 1) + h) // 2 == iota((20, 8), 0)).astype(jnp.float32)
    most = dot(dot(counts, pattern).astype(jnp.bfloat16), wide.astype(jnp.bfloat16))
    most_ref[0, 0] = jnp.max(most).astype(jnp.int32)

    n = iota((1, 128), 1)
    source = 16 * (n % 32 // 4) + 4 * (n // 32) + n % 4
    order = one_hot(iota((128, 128), 0) == source)
    for h in range(5):
        lanes = slice(128 * h, 128 * h + 128)
        plain_ref[h] = state_ref[:, lanes]
        hi, mid, low = split3(state_ref[:, lanes])
        moved_ref[h] = (dot(hi, order) + dot(mid, order)) + dot(low, order)
    lane = iota((5, 128), 1) // 32
    for x in range(4):
        for y in range(4):
            for h in range(5):
                unit = jnp.zeros((5, 128), jnp.float32)
                for r in range(4):
                    part = moved_ref[h, pl.ds(4 * x + r, 5, stride=16), :]
                    if r != y:
                        part = pltpu.roll(part, 32 * ((r - y) % 4), 1)
                    unit = jnp.where(lane == r, part, unit)
                out_ref[4 * x + y, 5 * h : 5 * h + 5] = unit
                out_ref[4 * x + y, 25 + 5 * h : 30 + 5 * h] = plain_ref[
                    h, pl.ds(4 * y + x, 5, stride=16), :
                ]
            out_ref[4 * x + y, 50:] = jnp.zeros((UNITS - 50, 128), jnp.float32)


def pack_kernel(slots, at_ref, pattern_ref, got_ref, left_ref, right_ref):
    pattern = pattern_ref[...].astype(jnp.float32).astype(jnp.bfloat16)
    place = places_across(pattern, at_ref[2], at_ref[3])
    count = 16 * UNITS
    units = jnp.concatenate(split3(got_ref[...].reshape(count, 128)), axis=1)
    row = iota((1, count), 1)
    for start, ref in ((0, left_ref), (25, right_ref)):
        j = row % UNITS - start
        inside = (j >= 0) & (j < 25)
        q = 5 * (row // UNITS) + j % 5
        expand = (q == iota((80, count), 0)).astype(jnp.float32)
        spread = dot(place, expand, EXACT)
        mine = 5 * at_ref[1] + j // 5 == iota((40, count), 0)
        slot = jnp.sum(jnp.where(mine, spread, 0.0), axis=0, keepdims=True)
        slot = jnp.where(inside, slot, -1.0)
        pick = one_hot(slot == iota((slots, count), 0).astype(jnp.float32))
        got = dot(pick, units)
        ref[...] = (got[:, :128] + got[:, 128:256]) + got[:, 256:]


def product_kernel(slots, at_ref, pattern_ref, packed_ref, own_ref, swap_ref, out_ref, left_ref, right_ref):
    pattern = pattern_ref[...].astype(jnp.float32).astype(jnp.bfloat16)
    zl, zh, c = at_ref[1], at_ref[2], at_ref[3]
    slot = iota((80, slots), 1).astype(jnp.float32)

    half = iota((80, 40), 1)
    for dc, ref in ((0, own_ref), (1, swap_ref)):
        for dzh in range(2):
            there = jnp.abs(zh - dzh)
            place = places(pattern, there, jnp.abs(c - dc))
            pick = []
            for h in range(5):
                at = jnp.sum(jnp.where(half == 5 * zl + h, place, 0.0), axis=1, keepdims=True)
                pick.append(one_hot(at == slot))
            pick = jnp.concatenate(pick, axis=0)
            for t in range(4):
                got = dot(pick, jnp.concatenate(split(ref[t, there]), axis=1))
                got = got[:, :128] + got[:, 128:]
                base = 40 * (4 * (2 * dzh + dc) + t)
                for h in range(5):
                    for g in range(2):
                        right_ref[g, base : base + 40, 128 * h : 128 * h + 128] = got[
                            80 * h + 40 * g : 80 * h + 40 * g + 40
                        ]

    place = places(pattern, zh, c)
    lane = iota((80, 128), 1) // 32
    units, group = [], 0
    for z in range(8):
        pick = jnp.concatenate(
            [one_hot(place[:, 5 * z + h : 5 * z + h + 1] == slot) for h in range(5)], axis=0
        )
        got = dot(pick, jnp.concatenate(split(packed_ref[z]), axis=1))
        got = got[:, :128] + got[:, 128:]
        units += [got[80 * h : 80 * h + 80] for h in range(5)]
        while len(units) >= 4:
            four, units = units[:4], units[4:]
            for r in range(4):
                tile = jnp.zeros((80, 128), jnp.float32)
                for j in range(4):
                    moved = four[j]
                    if j != r:
                        moved = pltpu.roll(moved, 32 * ((j - r) % 4), 1)
                    tile = jnp.where(lane == j, moved, tile)
                left_ref[80 * r : 80 * r + 80, 128 * group : 128 * group + 128] = tile
            group += 1

    to = iota((320, 1), 0)
    rows = one_hot(to % 20 // 5 * 80 + to // 20 * 5 + to % 5 == iota((320, 320), 1))
    m = iota((1, 640), 1)
    p, x0, y, e = m // 40, m % 40 // 20, m % 20 // 5, m % 5
    zh_of, c_of = jnp.abs(zh - p // 8), jnp.abs(c - p // 4 % 2)
    source = 160 * (2 * x0 + y // 2) + 4 * (20 * (y % 2) + 10 * zh_of + 5 * c_of + e) + p % 4
    cols = one_hot(iota((640, 640), 0) == source)
    total = jnp.zeros((320, 640), jnp.float32)
    for g in range(2):
        left = []
        for part in split(left_ref[:, 640 * g : 640 * g + 640]):
            part = dot(rows, part).astype(jnp.bfloat16)
            left.append(dot(part, cols).astype(jnp.bfloat16))
        right = split(right_ref[g])
        total += dot(left[0], right[0]) + (dot(left[0], right[1]) + dot(left[1], right[0]))
    out_ref[...] = total.reshape(16, 20, 640)


def inflate_kernel(at_ref, pattern_ref, shares_ref, out_ref, sums_ref, sum_ref):
    for x in range(4):
        total = (shares_ref[4 * x] + shares_ref[4 * x + 1]) + (
            shares_ref[4 * x + 2] + shares_ref[4 * x + 3]
        )
        for r in range(4):
            for h in range(5):
                lanes = slice(128 * h, 128 * h + 128)
                sum_ref[h, pl.ds(4 * x + r, 5, stride=16), :] = total[5 * r : 5 * r + 5, lanes]
    row = at_ref[0] * 80
    first = row // BLK
    here = iota((80, 128), 0) + row < (first + 1) * BLK
    for h in range(5):
        lanes = slice(128 * h, 128 * h + 128)
        col = (5 * at_ref[1] + h) // 2
        low = pattern_ref[first, col].astype(jnp.float32)
        high = pattern_ref[jnp.minimum(first + 1, 19), col].astype(jnp.float32)
        value = sum_ref[h]
        out_ref[:, lanes] = value * value * jnp.where(here, low, high)
    sums_ref[...] = dot_rows(jnp.ones((8, 640), jnp.float32), out_ref[...], EXACT)


def scale_kernel(nodes, inflated_ref, sums_ref, out_ref):
    totals = lax.dot_general(
        sums_ref[...],
        jnp.ones((8, 128), jnp.float32),
        (((0,), (0,)), ((), ())),
        precision=EXACT,
        preferred_element_type=jnp.float32,
    )
    scale = nodes / totals
    for h in range(5):
        lanes = slice(128 * h, 128 * h + 128)
        out_ref[:, lanes] = inflated_ref[:, lanes] * scale


def swap(x, axis_name):
    return lax.ppermute(x, axis_name, [(0, 1), (1, 0)])


def f32(*shape):
    return jax.ShapeDtypeStruct(shape, jnp.float32)


def gather(x, axis_name, limit):
    rows = x.shape[-2]
    parts = -(-rows // limit)
    size = rows // parts
    done = [
        lax.all_gather(x[..., i * size : (i + 1) * size, :], axis_name, axis=0)
        for i in range(parts)
    ]
    return done[0] if parts == 1 else jnp.concatenate(done, axis=-2)


def partial_product(slots, at, in_pattern, got):
    left, right = call(
        functools.partial(pack_kernel, slots),
        (f32(slots, 128), f32(slots, 128)),
        [SMEM, VMEM, VMEM],
        (at, in_pattern, got),
    )
    right = gather(right, "zh", SLOTS)
    left, right = lax.optimization_barrier((left, right))
    left = gather(left, "zl", SLOTS)
    right, left = lax.optimization_barrier((right, left))
    own = gather(right, "x", SLOTS)
    return call(
        functools.partial(product_kernel, slots),
        f32(16, 20, 640),
        [SMEM] + [VMEM] * 4,
        (at, in_pattern, left, own, swap(own, "c")),
        scratch=[pltpu.VMEM((320, 1280), jnp.float32), pltpu.VMEM((2, 640, 640), jnp.float32)],
        flops=5 * 10**9,
        size=5 * 10**6,
    )


def body(state, in_pattern, out_pattern):
    rows, cols = state.shape
    nodes = cols * lax.axis_size("zl")
    at = jnp.stack([lax.axis_index(ROWS)] + [lax.axis_index(a) for a in ("zl", "zh", "c")])
    at = at.astype(jnp.int32)
    units, most = call(
        units_kernel,
        (f32(16, UNITS, 128), jax.ShapeDtypeStruct((1, 1), jnp.int32)),
        [VMEM, VMEM],
        (in_pattern, state),
        out_specs=(VMEM, SMEM),
        scratch=[pltpu.VMEM((5, rows, 128), jnp.float32)] * 2,
    )
    got = lax.all_to_all(units, ("x", "y"), 0, 0)
    shares = lax.cond(
        most[0, 0] <= SLOTS,
        functools.partial(partial_product, SLOTS),
        functools.partial(partial_product, ALL),
        at,
        in_pattern,
        got,
    )
    shares = lax.all_to_all(shares, ("x", "y"), 0, 0)
    inflated, sums = call(
        inflate_kernel,
        (f32(rows, cols), f32(8, rows)),
        [SMEM, SMEM, VMEM],
        (at, out_pattern, shares),
        scratch=[pltpu.VMEM((5, rows, 128), jnp.float32)],
    )
    sums = lax.all_to_all(sums.reshape(8, 1, rows), "zl", 0, 0).reshape(8, rows)
    return call(
        functools.partial(scale_kernel, float(nodes)),
        f32(rows, cols),
        [VMEM, VMEM],
        (inflated, sums),
    )


def solution(mesh):
    fine = Mesh(
        mesh.devices.reshape(8, 4, 4, 2, 2), ("zl", "x", "y", "zh", "c")
    )
    return jax.shard_map(
        body,
        mesh=fine,
        in_specs=(P(ROWS, "zl"), P(), P()),
        out_specs=P(ROWS, "zl"),
        check_vma=False,
    )
```

```python
import functools

import jax
import jax.numpy as jnp
from jax import lax
from jax.experimental import pallas as pl
from jax.experimental.pallas import tpu as pltpu
from jax.sharding import Mesh, PartitionSpec as P

BLK = 256
ROWS = ("x", "y", "zh", "c")
MAIN, REST = 80, 24
LEFT = MAIN + REST
RUN, PAD = 20, 24
PIECE = LEFT + 5 * PAD
VMEM = pl.BlockSpec(memory_space=pltpu.VMEM)
SMEM = pl.BlockSpec(memory_space=pltpu.SMEM)


def split(x):
    hi = x.astype(jnp.bfloat16)
    return hi, (x - hi.astype(jnp.float32)).astype(jnp.bfloat16)


def dot(a, b):
    return jnp.dot(a, b, preferred_element_type=jnp.float32)


def call(kernel, outs, in_specs, args, scratch=(), flops=10**6, size=10**6):
    return pl.pallas_call(
        kernel,
        out_shape=outs,
        in_specs=in_specs,
        out_specs=jax.tree.map(lambda _: VMEM, outs),
        scratch_shapes=scratch,
        compiler_params=pltpu.CompilerParams(vmem_limit_bytes=40 * 2**20),
        cost_estimate=pl.CostEstimate(
            flops=flops, bytes_accessed=size, transcendentals=0
        ),
    )(*args)


def masked_block(at_ref, owner, pattern_ref, h, x):
    row = owner * 80
    col = (5 * at_ref[1] + h) // 2
    first = row // BLK
    low = pattern_ref[first, col].astype(jnp.float32)
    high = pattern_ref[jnp.minimum(first + 1, 19), col].astype(jnp.float32)
    here = lax.broadcasted_iota(jnp.int32, (80, 128), 0) + row < (first + 1) * BLK
    return x * jnp.where(here, low, high)


def pack_right(at_ref, owner, pattern_ref, state_ref, masked_ref, out_ref, base):
    for h in range(5):
        lanes = slice(128 * h, 128 * h + 128)
        masked_ref[:, lanes] = masked_block(at_ref, owner, pattern_ref, h, state_ref[:, lanes])
    out_ref[...] = jnp.zeros_like(out_ref)
    for y in range(4):
        for h in range(5):
            rows = slice(base + PAD * h, base + PAD * h + RUN)
            out_ref[y, rows] = masked_ref[RUN * y : RUN * y + RUN, 128 * h : 128 * h + 128]


def pieces_kernel(at_ref, pattern_ref, state_ref, out_ref, masked_ref):
    zh, c = at_ref[2], at_ref[3]
    pack_right(at_ref, at_ref[0], pattern_ref, state_ref, masked_ref, out_ref, LEFT)
    n = lax.broadcasted_iota(jnp.int32, (1, 640), 1)
    late = n >= 512
    y = jnp.where(late, (n - 512) // 32, n // 128)
    m = jnp.where(late, 128 + n % 32, n % 128)
    dzh, dc, y0, t = m // 80, m // 40 % 2, m // 20 % 2, m % 20
    zh_of = jnp.where(dzh == 0, zh, 1 - zh)
    c_of = jnp.where(dc == 0, c, 1 - c)
    source = 80 * (4 * y0 + 2 * zh_of + c_of) + 20 * y + t
    order = lax.broadcasted_iota(jnp.int32, (640, 640), 0) == source
    order = order.astype(jnp.float32).astype(jnp.bfloat16)
    x = masked_ref[...]
    hi, rest = x.astype(jnp.bfloat16), x
    rest = x - hi.astype(jnp.float32)
    mid, low = split(rest)
    moved = (dot(hi, order) + dot(mid, order)) + dot(low, order)
    lane = lax.broadcasted_iota(jnp.int32, (8, 128), 1) // 32
    for y in range(4):
        out_ref[y, :MAIN] = moved[:, 128 * y : 128 * y + 128]
        for slot in range(3):
            tile = jnp.zeros((8, 128), jnp.float32)
            for j in range(min(4, 10 - 4 * slot)):
                rows = 8 * (4 * slot + j)
                part = moved[rows : rows + 8, 512:]
                if j != y:
                    part = pltpu.roll(part, 32 * ((j - y) % 4), 1)
                tile = jnp.where(lane == j, part, tile)
            out_ref[y, MAIN + 8 * slot : MAIN + 8 * slot + 8] = tile


def unpack_right(got_ref, right_ref, base):
    for y in range(4):
        for h in range(5):
            right_ref[y // 2, RUN * (y % 2) : RUN * (y % 2) + RUN, 128 * h : 128 * h + 128] = (
                got_ref[y, base + PAD * h : base + PAD * h + RUN]
            )


def unpack_kernel(got_ref, left_ref, right_ref):
    left_ref[...] = got_ref[:, :LEFT]
    unpack_right(got_ref, right_ref, LEFT)


def product_kernel(at_ref, left_ref, right_ref, out_ref, hi_ref, lo_ref):
    for dc in range(2):
        c = lax.rem(at_ref[3] + dc, 2)
        for dzh in range(2):
            rows = slice(40 * (2 * dzh + dc), 40 * (2 * dzh + dc) + 40)
            for x in range(4):
                for y1 in range(2):
                    hi, lo = split(right_ref[c, x, lax.rem(at_ref[2] + dzh, 2), y1])
                    hi_ref[2 * x + y1, rows] = hi
                    lo_ref[2 * x + y1, rows] = lo
    lane = lax.broadcasted_iota(jnp.int32, (8, 128), 1) // 32
    total = jnp.zeros((320, 640), jnp.float32)
    for block in range(8):
        whole = []
        for y in range(4):
            rest = []
            for tile in range(10):
                rows = MAIN + 8 * (tile // 4)
                part = left_ref[block, y, rows : rows + 8]
                rest.append(jnp.where(lane == tile % 4, part, 0.0))
            rest = jnp.concatenate(rest, axis=0)
            whole.append(jnp.concatenate([left_ref[block, y, :MAIN], rest], axis=1))
        left_hi, left_lo = split(jnp.concatenate(whole, axis=0))
        right_hi, right_lo = hi_ref[block], lo_ref[block]
        right_hi = jnp.concatenate([right_hi] + [right_hi[128:]] * 3, axis=0)
        right_lo = jnp.concatenate([right_lo] + [right_lo[128:]] * 3, axis=0)
        total += dot(left_hi, right_hi) + (dot(left_hi, right_lo) + dot(left_lo, right_hi))
    out_ref[...] = total.reshape(4, 80, 640)


def inflate_kernel(at_ref, pattern_ref, shares_ref, out_ref, sums_ref):
    for h in range(5):
        lanes = slice(128 * h, 128 * h + 128)
        x = (shares_ref[0, :, lanes] + shares_ref[1, :, lanes]) + (
            shares_ref[2, :, lanes] + shares_ref[3, :, lanes]
        )
        out_ref[:, lanes] = masked_block(at_ref, at_ref[0], pattern_ref, h, x * x)
    sums_ref[...] = lax.dot_general(
        jnp.ones((8, 640), jnp.float32),
        out_ref[...],
        (((1,), (1,)), ((), ())),
        precision=lax.Precision.HIGHEST,
        preferred_element_type=jnp.float32,
    )


def scale_kernel(nodes, inflated_ref, sums_ref, out_ref):
    totals = lax.dot_general(
        sums_ref[...],
        jnp.ones((8, 128), jnp.float32),
        (((0,), (0,)), ((), ())),
        precision=lax.Precision.HIGHEST,
        preferred_element_type=jnp.float32,
    )
    scale = nodes / totals
    for h in range(5):
        lanes = slice(128 * h, 128 * h + 128)
        out_ref[:, lanes] = inflated_ref[:, lanes] * scale


def gather(block, axis_name):
    size = lax.axis_size(axis_name)
    copies = jnp.broadcast_to(block[None], (size,) + block.shape)
    return lax.all_to_all(copies, axis_name, 0, 0)


def f32(*shape):
    return jax.ShapeDtypeStruct(shape, jnp.float32)


def body(state, in_pattern, out_pattern):
    rows, cols = state.shape
    nodes = cols * lax.axis_size("zl")
    at = jnp.stack(
        [lax.axis_index(ROWS)] + [lax.axis_index(a) for a in ("zl", "zh", "c")]
    ).astype(jnp.int32)

    pieces = call(
        pieces_kernel,
        f32(4, PIECE, 128),
        [SMEM, SMEM, VMEM],
        (at, in_pattern, state),
        [pltpu.VMEM((rows, cols), jnp.float32)],
    )
    got = lax.all_to_all(pieces, "y", 0, 0)
    left, near = call(
        unpack_kernel, (f32(4, LEFT, 128), f32(2, 2 * RUN, cols)), [VMEM], (got,)
    )
    left = lax.all_gather(left, "zl", axis=0)
    right = gather(gather(gather(near, "zh"), "x"), "c")

    partial = call(
        product_kernel,
        f32(4, rows, cols),
        [SMEM, VMEM, VMEM],
        (at, left, right),
        [pltpu.VMEM((8, 160, cols), jnp.bfloat16)] * 2,
        flops=3 * 10**9,
        size=6 * 10**6,
    )
    shares = lax.all_to_all(partial, "y", 0, 0)
    inflated, sums = call(
        inflate_kernel,
        (f32(rows, cols), f32(8, rows)),
        [SMEM, SMEM, VMEM],
        (at, out_pattern, shares),
    )
    sums = lax.all_to_all(sums.reshape(8, 1, rows), "zl", 0, 0).reshape(8, rows)
    return call(
        functools.partial(scale_kernel, float(nodes)),
        f32(rows, cols),
        [VMEM, VMEM],
        (inflated, sums),
    )


def solution(mesh):
    fine = Mesh(
        mesh.devices.reshape(8, 4, 4, 2, 2), ("zl", "x", "y", "zh", "c")
    )
    return jax.shard_map(
        body,
        mesh=fine,
        in_specs=(P(ROWS, "zl"), P(), P()),
        out_specs=P(ROWS, "zl"),
        check_vma=False,
    )
```

```python
import functools

import jax
import jax.numpy as jnp
from jax import lax
from jax.experimental import pallas as pl
from jax.experimental.pallas import tpu as pltpu
from jax.sharding import Mesh, PartitionSpec as P

BLK = 256
ROWS = ("x", "y", "zh", "c")
MAIN, REST = 80, 24
LEFT = MAIN + REST
RUN, PAD = 20, 24
PIECE = LEFT + 5 * PAD
VMEM = pl.BlockSpec(memory_space=pltpu.VMEM)
SMEM = pl.BlockSpec(memory_space=pltpu.SMEM)


def split(x):
    hi = x.astype(jnp.bfloat16)
    return hi, (x - hi.astype(jnp.float32)).astype(jnp.bfloat16)


def dot(a, b):
    return jnp.dot(a, b, preferred_element_type=jnp.float32)


def call(kernel, outs, in_specs, args, scratch=(), flops=10**6, size=10**6):
    return pl.pallas_call(
        kernel,
        out_shape=outs,
        in_specs=in_specs,
        out_specs=jax.tree.map(lambda _: VMEM, outs),
        scratch_shapes=scratch,
        compiler_params=pltpu.CompilerParams(vmem_limit_bytes=40 * 2**20),
        cost_estimate=pl.CostEstimate(
            flops=flops, bytes_accessed=size, transcendentals=0
        ),
    )(*args)


def masked_block(at_ref, owner, pattern_ref, h, x):
    row = owner * 80
    col = (5 * at_ref[1] + h) // 2
    first = row // BLK
    low = pattern_ref[first, col].astype(jnp.float32)
    high = pattern_ref[jnp.minimum(first + 1, 19), col].astype(jnp.float32)
    here = lax.broadcasted_iota(jnp.int32, (80, 128), 0) + row < (first + 1) * BLK
    return x * jnp.where(here, low, high)


def pack_right(at_ref, owner, pattern_ref, state_ref, masked_ref, out_ref, base):
    for h in range(5):
        lanes = slice(128 * h, 128 * h + 128)
        masked_ref[:, lanes] = masked_block(at_ref, owner, pattern_ref, h, state_ref[:, lanes])
    out_ref[...] = jnp.zeros_like(out_ref)
    for y in range(4):
        for h in range(5):
            rows = slice(base + PAD * h, base + PAD * h + RUN)
            out_ref[y, rows] = masked_ref[RUN * y : RUN * y + RUN, 128 * h : 128 * h + 128]


def pieces_kernel(at_ref, pattern_ref, state_ref, out_ref, masked_ref):
    zh, c = at_ref[2], at_ref[3]
    pack_right(at_ref, at_ref[0], pattern_ref, state_ref, masked_ref, out_ref, LEFT)
    n = lax.broadcasted_iota(jnp.int32, (1, 640), 1)
    late = n >= 512
    y = jnp.where(late, (n - 512) // 32, n // 128)
    m = jnp.where(late, 128 + n % 32, n % 128)
    dzh, dc, y0, t = m // 80, m // 40 % 2, m // 20 % 2, m % 20
    zh_of = jnp.where(dzh == 0, zh, 1 - zh)
    c_of = jnp.where(dc == 0, c, 1 - c)
    source = 80 * (4 * y0 + 2 * zh_of + c_of) + 20 * y + t
    order = lax.broadcasted_iota(jnp.int32, (640, 640), 0) == source
    order = order.astype(jnp.float32).astype(jnp.bfloat16)
    x = masked_ref[...]
    hi, rest = x.astype(jnp.bfloat16), x
    rest = x - hi.astype(jnp.float32)
    mid, low = split(rest)
    moved = (dot(hi, order) + dot(mid, order)) + dot(low, order)
    lane = lax.broadcasted_iota(jnp.int32, (8, 128), 1) // 32
    for y in range(4):
        out_ref[y, :MAIN] = moved[:, 128 * y : 128 * y + 128]
        for slot in range(3):
            tile = jnp.zeros((8, 128), jnp.float32)
            for j in range(min(4, 10 - 4 * slot)):
                rows = 8 * (4 * slot + j)
                part = moved[rows : rows + 8, 512:]
                if j != y:
                    part = pltpu.roll(part, 32 * ((j - y) % 4), 1)
                tile = jnp.where(lane == j, part, tile)
            out_ref[y, MAIN + 8 * slot : MAIN + 8 * slot + 8] = tile


def unpack_right(got_ref, right_ref, base):
    for y in range(4):
        for h in range(5):
            right_ref[y // 2, RUN * (y % 2) : RUN * (y % 2) + RUN, 128 * h : 128 * h + 128] = (
                got_ref[y, base + PAD * h : base + PAD * h + RUN]
            )


def unpack_kernel(got_ref, left_ref, right_ref):
    left_ref[...] = got_ref[:, :LEFT]
    unpack_right(got_ref, right_ref, LEFT)


def product_kernel(at_ref, *refs):
    lefts, rights, out_ref, hi_ref, lo_ref = refs[:2], refs[2:6], *refs[6:]
    for part, ref in enumerate(rights):
        for dx in range(4):
            for y1 in range(2):
                hi, lo = split(ref[dx, y1])
                rows = slice(40 * part, 40 * part + 40)
                hi_ref[2 * dx + y1, rows] = hi
                lo_ref[2 * dx + y1, rows] = lo
    lane = lax.broadcasted_iota(jnp.int32, (8, 128), 1) // 32
    zl, x = at_ref[1], at_ref[4]
    total = jnp.zeros((320, 640), jnp.float32)
    for d in range(8):
        ref = lefts[d // 4].at[d % 4]
        source = 4 * lax.rem(zl // 4 + d // 4, 2) + d % 4
        block = 2 * lax.rem(x - source // 2 + 4, 4) + lax.rem(source, 2)
        whole = []
        for y in range(4):
            rest = []
            for tile in range(10):
                rows = MAIN + 8 * (tile // 4)
                rest.append(jnp.where(lane == tile % 4, ref[y, rows : rows + 8], 0.0))
            rest = jnp.concatenate(rest, axis=0)
            whole.append(jnp.concatenate([ref[y, :MAIN], rest], axis=1))
        left_hi, left_lo = split(jnp.concatenate(whole, axis=0))
        right_hi, right_lo = hi_ref[block], lo_ref[block]
        right_hi = jnp.concatenate([right_hi] + [right_hi[128:]] * 3, axis=0)
        right_lo = jnp.concatenate([right_lo] + [right_lo[128:]] * 3, axis=0)
        total += dot(left_hi, right_hi) + (dot(left_hi, right_lo) + dot(left_lo, right_hi))
    out_ref[...] = total.reshape(4, 80, 640)


def inflate_kernel(at_ref, pattern_ref, shares_ref, out_ref, sums_ref):
    for h in range(5):
        lanes = slice(128 * h, 128 * h + 128)
        x = (shares_ref[0, :, lanes] + shares_ref[1, :, lanes]) + (
            shares_ref[2, :, lanes] + shares_ref[3, :, lanes]
        )
        out_ref[:, lanes] = masked_block(at_ref, at_ref[0], pattern_ref, h, x * x)
    sums_ref[...] = lax.dot_general(
        jnp.ones((8, 640), jnp.float32),
        out_ref[...],
        (((1,), (1,)), ((), ())),
        precision=lax.Precision.HIGHEST,
        preferred_element_type=jnp.float32,
    )


def scale_kernel(nodes, inflated_ref, sums_ref, out_ref):
    totals = lax.dot_general(
        sums_ref[...],
        jnp.ones((8, 128), jnp.float32),
        (((0,), (0,)), ((), ())),
        precision=lax.Precision.HIGHEST,
        preferred_element_type=jnp.float32,
    )
    scale = nodes / totals
    for h in range(5):
        lanes = slice(128 * h, 128 * h + 128)
        out_ref[:, lanes] = inflated_ref[:, lanes] * scale


def shift(x, axis_name, by):
    size = lax.axis_size(axis_name)
    return lax.ppermute(x, axis_name, [(i, (i + by) % size) for i in range(size)])


def across_x(block):
    return jnp.stack([block] + [shift(block, "x", by) for by in (1, 2, 3)], 0)


def f32(*shape):
    return jax.ShapeDtypeStruct(shape, jnp.float32)


def body(state, in_pattern, out_pattern):
    rows, cols = state.shape
    nodes = cols * lax.axis_size("zl")
    at = jnp.stack(
        [lax.axis_index(ROWS)] + [lax.axis_index(a) for a in ("zl", "zh", "c", "x")]
    ).astype(jnp.int32)

    pieces = call(
        pieces_kernel,
        f32(4, PIECE, 128),
        [SMEM, SMEM, VMEM],
        (at, in_pattern, state),
        [pltpu.VMEM((rows, cols), jnp.float32)],
    )
    got = lax.all_to_all(pieces, "y", 0, 0)
    left, near = call(
        unpack_kernel, (f32(4, LEFT, 128), f32(2, 2 * RUN, cols)), [VMEM], (got,)
    )

    tie = lax.optimization_barrier
    halves = [[0, 1, 2, 3], [4, 5, 6, 7]]
    away = lax.ppermute(left, "zl", [(i, i ^ 4) for i in range(8)])
    far = shift(near, "zh", 1)
    near = across_x(near)
    here = lax.all_gather(left, "zl", axis=0, axis_index_groups=halves)
    away, far, near, here = tie((away, far, near, here))

    far = across_x(far)
    near_swapped = shift(near, "c", 1)
    away = lax.all_gather(away, "zl", axis=0, axis_index_groups=halves)
    away, far, near_swapped = tie((away, far, near_swapped))
    far_swapped = shift(far, "c", 1)

    partial = call(
        product_kernel,
        f32(4, rows, cols),
        [SMEM] + [VMEM] * 6,
        (at, here, away, near, near_swapped, far, far_swapped),
        [pltpu.VMEM((8, 160, cols), jnp.bfloat16)] * 2,
        flops=3 * 10**9,
        size=6 * 10**6,
    )
    shares = lax.all_to_all(partial, "y", 0, 0)
    inflated, sums = call(
        inflate_kernel,
        (f32(rows, cols), f32(8, rows)),
        [SMEM, SMEM, VMEM],
        (at, out_pattern, shares),
    )
    sums = lax.all_to_all(sums.reshape(8, 1, rows), "zl", 0, 0).reshape(8, rows)
    return call(
        functools.partial(scale_kernel, float(nodes)),
        f32(rows, cols),
        [VMEM, VMEM],
        (inflated, sums),
    )


def solution(mesh):
    fine = Mesh(
        mesh.devices.reshape(8, 4, 4, 2, 2), ("zl", "x", "y", "zh", "c")
    )
    return jax.shard_map(
        body,
        mesh=fine,
        in_specs=(P(ROWS, "zl"), P(), P()),
        out_specs=P(ROWS, "zl"),
        check_vma=False,
    )
```

```python
import functools

import jax
import jax.numpy as jnp
from jax import lax
from jax.experimental import pallas as pl
from jax.experimental.pallas import tpu as pltpu
from jax.sharding import Mesh, PartitionSpec as P

BLK = 256
ROWS = ("x", "y", "zh", "c")
MAIN, REST = 80, 24
LEFT = MAIN + REST
RUN, PAD = 20, 24
VMEM = pl.BlockSpec(memory_space=pltpu.VMEM)
SMEM = pl.BlockSpec(memory_space=pltpu.SMEM)


def split(x):
    hi = x.astype(jnp.bfloat16)
    return hi, (x - hi.astype(jnp.float32)).astype(jnp.bfloat16)


def dot(a, b):
    return jnp.dot(a, b, preferred_element_type=jnp.float32)


def call(kernel, outs, in_specs, args, scratch=(), flops=10**6, size=10**6):
    return pl.pallas_call(
        kernel,
        out_shape=outs,
        in_specs=in_specs,
        out_specs=jax.tree.map(lambda _: VMEM, outs),
        scratch_shapes=scratch,
        compiler_params=pltpu.CompilerParams(vmem_limit_bytes=40 * 2**20),
        cost_estimate=pl.CostEstimate(
            flops=flops, bytes_accessed=size, transcendentals=0
        ),
    )(*args)


def masked_block(at_ref, owner, pattern_ref, h, x):
    row = owner * 80
    col = (5 * at_ref[1] + h) // 2
    first = row // BLK
    low = pattern_ref[first, col].astype(jnp.float32)
    high = pattern_ref[jnp.minimum(first + 1, 19), col].astype(jnp.float32)
    here = lax.broadcasted_iota(jnp.int32, (80, 128), 0) + row < (first + 1) * BLK
    return x * jnp.where(here, low, high)


def mask(at_ref, pattern_ref, state_ref, masked_ref):
    for h in range(5):
        lanes = slice(128 * h, 128 * h + 128)
        masked_ref[:, lanes] = masked_block(at_ref, at_ref[0], pattern_ref, h, state_ref[:, lanes])


def left_kernel(at_ref, pattern_ref, state_ref, out_ref, masked_ref):
    zh, c = at_ref[2], at_ref[3]
    mask(at_ref, pattern_ref, state_ref, masked_ref)
    n = lax.broadcasted_iota(jnp.int32, (1, 640), 1)
    late = n >= 512
    y = jnp.where(late, (n - 512) // 32, n // 128)
    m = jnp.where(late, 128 + n % 32, n % 128)
    dzh, dc, y0, t = m // 80, m // 40 % 2, m // 20 % 2, m % 20
    zh_of = jnp.where(dzh == 0, zh, 1 - zh)
    c_of = jnp.where(dc == 0, c, 1 - c)
    source = 80 * (4 * y0 + 2 * zh_of + c_of) + 20 * y + t
    order = lax.broadcasted_iota(jnp.int32, (640, 640), 0) == source
    order = order.astype(jnp.float32).astype(jnp.bfloat16)
    x = masked_ref[...]
    hi = x.astype(jnp.bfloat16)
    mid, low = split(x - hi.astype(jnp.float32))
    moved = (dot(hi, order) + dot(mid, order)) + dot(low, order)
    lane = lax.broadcasted_iota(jnp.int32, (8, 128), 1) // 32
    for y in range(4):
        out_ref[y, :MAIN] = moved[:, 128 * y : 128 * y + 128]
        for slot in range(3):
            tile = jnp.zeros((8, 128), jnp.float32)
            for j in range(min(4, 10 - 4 * slot)):
                rows = 8 * (4 * slot + j)
                part = moved[rows : rows + 8, 512:]
                if j != y:
                    part = pltpu.roll(part, 32 * ((j - y) % 4), 1)
                tile = jnp.where(lane == j, part, tile)
            out_ref[y, MAIN + 8 * slot : MAIN + 8 * slot + 8] = tile


def right_kernel(at_ref, pattern_ref, state_ref, out_ref, masked_ref):
    mask(at_ref, pattern_ref, state_ref, masked_ref)
    out_ref[...] = jnp.zeros_like(out_ref)
    for y in range(4):
        for h in range(5):
            out_ref[y, PAD * h : PAD * h + RUN] = masked_ref[
                RUN * y : RUN * y + RUN, 128 * h : 128 * h + 128
            ]


def unpack_kernel(got_ref, right_ref):
    for y in range(4):
        for h in range(5):
            right_ref[y // 2, RUN * (y % 2) : RUN * (y % 2) + RUN, 128 * h : 128 * h + 128] = (
                got_ref[y, PAD * h : PAD * h + RUN]
            )


def halves_kernel(at_ref, right_ref, hi_ref, lo_ref):
    zh, c = at_ref[2], at_ref[3]
    for x in range(4):
        for y1 in range(2):
            rows = [
                right_ref[lax.rem(c + dc, 2), x, lax.rem(zh + dzh, 2), y1]
                for dzh in range(2)
                for dc in range(2)
            ]
            rows = jnp.concatenate(rows + [rows[3][8:]] * 3, axis=0)
            hi_ref[2 * x + y1], lo_ref[2 * x + y1] = split(rows)


def product_kernel(left_hbm, hi_ref, lo_ref, out_ref, left_ref, sems):
    copies = [
        pltpu.make_async_copy(left_hbm.at[block], left_ref.at[block], sems.at[block])
        for block in range(8)
    ]
    for copy in copies:
        copy.start()
    lane = lax.broadcasted_iota(jnp.int32, (8, 128), 1) // 32
    total = jnp.zeros((320, 640), jnp.float32)
    for block in range(8):
        copies[block].wait()
        whole = []
        for y in range(4):
            rest = []
            for tile in range(10):
                rows = MAIN + 8 * (tile // 4)
                part = left_ref[block, y, rows : rows + 8]
                rest.append(jnp.where(lane == tile % 4, part, 0.0))
            rest = jnp.concatenate(rest, axis=0)
            whole.append(jnp.concatenate([left_ref[block, y, :MAIN], rest], axis=1))
        left_hi, left_lo = split(jnp.concatenate(whole, axis=0))
        right_hi, right_lo = hi_ref[block], lo_ref[block]
        total += dot(left_hi, right_hi) + (dot(left_hi, right_lo) + dot(left_lo, right_hi))
    out_ref[...] = total.reshape(4, 80, 640)


def inflate_kernel(at_ref, pattern_ref, shares_ref, out_ref, sums_ref):
    for h in range(5):
        lanes = slice(128 * h, 128 * h + 128)
        x = (shares_ref[0, :, lanes] + shares_ref[1, :, lanes]) + (
            shares_ref[2, :, lanes] + shares_ref[3, :, lanes]
        )
        out_ref[:, lanes] = masked_block(at_ref, at_ref[0], pattern_ref, h, x * x)
    sums_ref[...] = lax.dot_general(
        jnp.ones((8, 640), jnp.float32),
        out_ref[...],
        (((1,), (1,)), ((), ())),
        precision=lax.Precision.HIGHEST,
        preferred_element_type=jnp.float32,
    )


def scale_kernel(nodes, inflated_ref, sums_ref, out_ref):
    totals = lax.dot_general(
        sums_ref[...],
        jnp.ones((8, 128), jnp.float32),
        (((0,), (0,)), ((), ())),
        precision=lax.Precision.HIGHEST,
        preferred_element_type=jnp.float32,
    )
    scale = nodes / totals
    for h in range(5):
        lanes = slice(128 * h, 128 * h + 128)
        out_ref[:, lanes] = inflated_ref[:, lanes] * scale


def gather(block, axis_name):
    size = lax.axis_size(axis_name)
    copies = jnp.broadcast_to(block[None], (size,) + block.shape)
    return lax.all_to_all(copies, axis_name, 0, 0)


def f32(*shape):
    return jax.ShapeDtypeStruct(shape, jnp.float32)


def body(state, in_pattern, out_pattern):
    rows, cols = state.shape
    nodes = cols * lax.axis_size("zl")
    at = jnp.stack(
        [lax.axis_index(ROWS)] + [lax.axis_index(a) for a in ("zl", "zh", "c")]
    ).astype(jnp.int32)

    work = [pltpu.VMEM((rows, cols), jnp.float32)]
    specs = [SMEM, SMEM, VMEM]
    left = call(left_kernel, f32(4, LEFT, 128), specs, (at, in_pattern, state), work)
    left = lax.all_to_all(left, "y", 0, 0)
    left, later = lax.optimization_barrier((left, state))
    left = lax.all_gather(left, "zl", axis=0)

    right = call(right_kernel, f32(4, 5 * PAD, 128), specs, (at, in_pattern, later), work)
    right = lax.all_to_all(right, "y", 0, 0)
    right = call(unpack_kernel, f32(2, 2 * RUN, cols), [VMEM], (right,))
    right = gather(gather(gather(right, "zh"), "x"), "c")
    half = jax.ShapeDtypeStruct((8, 256, cols), jnp.bfloat16)
    right_hi, right_lo = call(halves_kernel, (half, half), [SMEM, VMEM], (at, right))

    partial = call(
        product_kernel,
        f32(4, rows, cols),
        [pl.BlockSpec(memory_space=pltpu.HBM), VMEM, VMEM],
        (left, right_hi, right_lo),
        [pltpu.VMEM((8, 4, LEFT, 128), jnp.float32), pltpu.SemaphoreType.DMA((8,))],
        flops=3 * 10**9,
        size=6 * 10**6,
    )
    shares = lax.all_to_all(partial, "y", 0, 0)
    inflated, sums = call(
        inflate_kernel,
        (f32(rows, cols), f32(8, rows)),
        [SMEM, SMEM, VMEM],
        (at, out_pattern, shares),
    )
    sums = lax.all_to_all(sums.reshape(8, 1, rows), "zl", 0, 0).reshape(8, rows)
    return call(
        functools.partial(scale_kernel, float(nodes)),
        f32(rows, cols),
        [VMEM, VMEM],
        (inflated, sums),
    )


def solution(mesh):
    fine = Mesh(
        mesh.devices.reshape(8, 4, 4, 2, 2), ("zl", "x", "y", "zh", "c")
    )
    return jax.shard_map(
        body,
        mesh=fine,
        in_specs=(P(ROWS, "zl"), P(), P()),
        out_specs=P(ROWS, "zl"),
        check_vma=False,
    )
```

```python
import functools

import jax
import jax.numpy as jnp
from jax import lax
from jax.experimental import pallas as pl
from jax.experimental.pallas import tpu as pltpu
from jax.sharding import Mesh, PartitionSpec as P

BLK = 256
ROWS = ("x", "y", "zh", "c")
MAIN, REST = 80, 24
LEFT = MAIN + REST
RUN, PAD = 20, 24
PIECE = LEFT + 5 * PAD
VMEM = pl.BlockSpec(memory_space=pltpu.VMEM)
SMEM = pl.BlockSpec(memory_space=pltpu.SMEM)
HBM = pl.BlockSpec(memory_space=pltpu.HBM)


def split(x):
    hi = x.astype(jnp.bfloat16)
    return hi, (x - hi.astype(jnp.float32)).astype(jnp.bfloat16)


def dot(a, b):
    return jnp.dot(a, b, preferred_element_type=jnp.float32)


def call(kernel, outs, in_specs, args, scratch=(), flops=10**6, size=10**6, vmem=40):
    return pl.pallas_call(
        kernel,
        out_shape=outs,
        in_specs=in_specs,
        out_specs=jax.tree.map(lambda _: VMEM, outs),
        scratch_shapes=scratch,
        compiler_params=pltpu.CompilerParams(vmem_limit_bytes=vmem * 2**20),
        cost_estimate=pl.CostEstimate(
            flops=flops, bytes_accessed=size, transcendentals=0
        ),
    )(*args)


def masked_block(at_ref, owner, pattern_ref, h, x):
    row = owner * 80
    col = (5 * at_ref[1] + h) // 2
    first = row // BLK
    low = pattern_ref[first, col].astype(jnp.float32)
    high = pattern_ref[jnp.minimum(first + 1, 19), col].astype(jnp.float32)
    here = lax.broadcasted_iota(jnp.int32, (80, 128), 0) + row < (first + 1) * BLK
    return x * jnp.where(here, low, high)


def pieces_kernel(
    at_ref, pattern_hbm, state_hbm, out_ref, pattern_ref, state_ref, masked_ref, sems
):
    pattern_copy = pltpu.make_async_copy(pattern_hbm, pattern_ref, sems.at[0])
    state_copy = pltpu.make_async_copy(state_hbm, state_ref, sems.at[1])
    pattern_copy.start()
    state_copy.start()
    zh, c = at_ref[2], at_ref[3]
    n = lax.broadcasted_iota(jnp.int32, (1, 640), 1)
    late = n >= 512
    y = jnp.where(late, (n - 512) // 32, n // 128)
    m = jnp.where(late, 128 + n % 32, n % 128)
    dzh, dc, y0, t = m // 80, m // 40 % 2, m // 20 % 2, m % 20
    zh_of = jnp.where(dzh == 0, zh, 1 - zh)
    c_of = jnp.where(dc == 0, c, 1 - c)
    source = 80 * (4 * y0 + 2 * zh_of + c_of) + 20 * y + t
    order = lax.broadcasted_iota(jnp.int32, (640, 640), 0) == source
    order = order.astype(jnp.float32).astype(jnp.bfloat16)
    pattern_copy.wait()
    state_copy.wait()
    for h in range(5):
        lanes = slice(128 * h, 128 * h + 128)
        masked_ref[:, lanes] = masked_block(
            at_ref, at_ref[0], pattern_ref, h, state_ref[:, lanes]
        )
    x = masked_ref[...]
    hi = x.astype(jnp.bfloat16)
    mid, low = split(x - hi.astype(jnp.float32))
    moved = (dot(hi, order) + dot(mid, order)) + dot(low, order)
    lane = lax.broadcasted_iota(jnp.int32, (8, 128), 1) // 32
    for y in range(4):
        for h in range(5):
            out_ref[y, LEFT + PAD * h : LEFT + PAD * h + RUN] = masked_ref[
                RUN * y : RUN * y + RUN, 128 * h : 128 * h + 128
            ]
            out_ref[y, LEFT + PAD * h + RUN : LEFT + PAD * h + PAD] = jnp.zeros(
                (PAD - RUN, 128), jnp.float32
            )
        out_ref[y, :MAIN] = moved[:, 128 * y : 128 * y + 128]
        for slot in range(3):
            tile = jnp.zeros((8, 128), jnp.float32)
            for j in range(min(4, 10 - 4 * slot)):
                rows = 8 * (4 * slot + j)
                part = moved[rows : rows + 8, 512:]
                if j != y:
                    part = pltpu.roll(part, 32 * ((j - y) % 4), 1)
                tile = jnp.where(lane == j, part, tile)
            out_ref[y, MAIN + 8 * slot : MAIN + 8 * slot + 8] = tile


def unpack_left_kernel(got_ref, left_ref):
    left_ref[...] = got_ref[:, :LEFT]


def unpack_right_kernel(got_ref, right_ref):
    for y in range(4):
        for h in range(5):
            right_ref[y // 2, RUN * (y % 2) : RUN * (y % 2) + RUN, 128 * h : 128 * h + 128] = (
                got_ref[y, LEFT + PAD * h : LEFT + PAD * h + RUN]
            )


def product_kernel(at_ref, left_hbm, right_hbm, out_ref, left_ref, right_ref, sems):
    def left_copy(block):
        return pltpu.make_async_copy(left_hbm.at[block], left_ref.at[block], sems.at[0, block])

    def right_copy(c, x):
        return pltpu.make_async_copy(
            right_hbm.at[c, x], right_ref.at[c, x], sems.at[1, 2 * x + c]
        )

    for x in range(4):
        for part in range(2):
            right_copy(part, x).start()
        for part in range(2):
            left_copy(2 * x + part).start()
    lane = lax.broadcasted_iota(jnp.int32, (8, 128), 1) // 32
    zh, c = at_ref[2], at_ref[3]
    total = jnp.zeros((320, 640), jnp.float32)
    for x in range(4):
        for part in range(2):
            right_copy(part, x).wait()
        for y1 in range(2):
            rows = [
                right_ref[lax.rem(c + dc, 2), x, lax.rem(zh + dzh, 2), y1]
                for dzh in range(2)
                for dc in range(2)
            ]
            right_hi, right_lo = split(jnp.concatenate(rows + [rows[3][8:]] * 3, axis=0))
            block = 2 * x + y1
            left_copy(block).wait()
            whole = []
            for y in range(4):
                rest = []
                for tile in range(10):
                    start = MAIN + 8 * (tile // 4)
                    part = left_ref[block, y, start : start + 8]
                    rest.append(jnp.where(lane == tile % 4, part, 0.0))
                rest = jnp.concatenate(rest, axis=0)
                whole.append(jnp.concatenate([left_ref[block, y, :MAIN], rest], axis=1))
            left_hi, left_lo = split(jnp.concatenate(whole, axis=0))
            total += dot(left_hi, right_hi) + (dot(left_hi, right_lo) + dot(left_lo, right_hi))
    out_ref[...] = total.reshape(4, 80, 640)


def inflate_kernel(at_ref, pattern_ref, shares_ref, out_ref, sums_ref):
    for h in range(5):
        lanes = slice(128 * h, 128 * h + 128)
        x = (shares_ref[0, :, lanes] + shares_ref[1, :, lanes]) + (
            shares_ref[2, :, lanes] + shares_ref[3, :, lanes]
        )
        out_ref[:, lanes] = masked_block(at_ref, at_ref[0], pattern_ref, h, x * x)
    sums_ref[...] = lax.dot_general(
        jnp.ones((8, 640), jnp.float32),
        out_ref[...],
        (((1,), (1,)), ((), ())),
        precision=lax.Precision.HIGHEST,
        preferred_element_type=jnp.float32,
    )


def scale_kernel(nodes, inflated_ref, sums_ref, out_ref):
    totals = lax.dot_general(
        sums_ref[...],
        jnp.ones((8, 128), jnp.float32),
        (((0,), (0,)), ((), ())),
        precision=lax.Precision.HIGHEST,
        preferred_element_type=jnp.float32,
    )
    scale = nodes / totals
    for h in range(5):
        lanes = slice(128 * h, 128 * h + 128)
        out_ref[:, lanes] = inflated_ref[:, lanes] * scale


def gather(block, axis_name):
    size = lax.axis_size(axis_name)
    copies = jnp.broadcast_to(block[None], (size,) + block.shape)
    return lax.all_to_all(copies, axis_name, 0, 0)


def f32(*shape):
    return jax.ShapeDtypeStruct(shape, jnp.float32)


def body(state, in_pattern, out_pattern):
    rows, cols = state.shape
    nodes = cols * lax.axis_size("zl")
    at = jnp.stack(
        [lax.axis_index(ROWS)] + [lax.axis_index(a) for a in ("zl", "zh", "c")]
    ).astype(jnp.int32)

    pieces = call(
        pieces_kernel,
        f32(4, PIECE, 128),
        [SMEM, HBM, HBM],
        (at, in_pattern, state),
        [
            pltpu.SMEM(in_pattern.shape, jnp.int32),
            pltpu.VMEM((rows, cols), jnp.float32),
            pltpu.VMEM((rows, cols), jnp.float32),
            pltpu.SemaphoreType.DMA((2,)),
        ],
        vmem=60,
    )
    got = lax.all_to_all(pieces, "y", 0, 0)
    left = call(unpack_left_kernel, f32(4, LEFT, 128), [VMEM], (got,))
    left, got = lax.optimization_barrier((left, got))
    left = lax.all_gather(left, "zl", axis=0)
    near = call(unpack_right_kernel, f32(2, 2 * RUN, cols), [VMEM], (got,))
    right = gather(gather(gather(near, "zh"), "x"), "c")

    partial = call(
        product_kernel,
        f32(4, rows, cols),
        [SMEM, HBM, HBM],
        (at, left, right),
        [
            pltpu.VMEM(left.shape, jnp.float32),
            pltpu.VMEM(right.shape, jnp.float32),
            pltpu.SemaphoreType.DMA((2, 8)),
        ],
        flops=3 * 10**9,
        size=6 * 10**6,
        vmem=60,
    )
    shares = lax.all_to_all(partial, "y", 0, 0)
    inflated, sums = call(
        inflate_kernel,
        (f32(rows, cols), f32(8, rows)),
        [SMEM, SMEM, VMEM],
        (at, out_pattern, shares),
    )
    sums = lax.all_to_all(sums.reshape(8, 1, rows), "zl", 0, 0).reshape(8, rows)
    return call(
        functools.partial(scale_kernel, float(nodes)),
        f32(rows, cols),
        [VMEM, VMEM],
        (inflated, sums),
    )


def solution(mesh):
    fine = Mesh(
        mesh.devices.reshape(8, 4, 4, 2, 2), ("zl", "x", "y", "zh", "c")
    )
    return jax.shard_map(
        body,
        mesh=fine,
        in_specs=(P(ROWS, "zl"), P(), P()),
        out_specs=P(ROWS, "zl"),
        check_vma=False,
    )
```

```python
import functools

import jax
import jax.numpy as jnp
from jax import lax
from jax.experimental import pallas as pl
from jax.experimental.pallas import tpu as pltpu
from jax.sharding import Mesh, PartitionSpec as P

BLK = 256
ROWS = ("x", "y", "zh", "c")
MAIN, REST = 80, 24
LEFT = MAIN + REST
RUN, PAD = 20, 24
VMEM = pl.BlockSpec(memory_space=pltpu.VMEM)
SMEM = pl.BlockSpec(memory_space=pltpu.SMEM)


def split(x):
    hi = x.astype(jnp.bfloat16)
    return hi, (x - hi.astype(jnp.float32)).astype(jnp.bfloat16)


def dot(a, b):
    return jnp.dot(a, b, preferred_element_type=jnp.float32)


def call(kernel, outs, in_specs, args, scratch=(), flops=10**6, size=10**6):
    return pl.pallas_call(
        kernel,
        out_shape=outs,
        in_specs=in_specs,
        out_specs=jax.tree.map(lambda _: VMEM, outs),
        scratch_shapes=scratch,
        compiler_params=pltpu.CompilerParams(vmem_limit_bytes=40 * 2**20),
        cost_estimate=pl.CostEstimate(
            flops=flops, bytes_accessed=size, transcendentals=0
        ),
    )(*args)


def masked_block(at_ref, owner, pattern_ref, h, x):
    row = owner * 80
    col = (5 * at_ref[1] + h) // 2
    first = row // BLK
    low = pattern_ref[first, col].astype(jnp.float32)
    high = pattern_ref[jnp.minimum(first + 1, 19), col].astype(jnp.float32)
    here = lax.broadcasted_iota(jnp.int32, (80, 128), 0) + row < (first + 1) * BLK
    return x * jnp.where(here, low, high)


def left_kernel(at_ref, pattern_ref, state_ref, out_ref, masked_ref):
    zh, c = at_ref[2], at_ref[3]
    for h in range(5):
        lanes = slice(128 * h, 128 * h + 128)
        masked_ref[:, lanes] = masked_block(
            at_ref, at_ref[0], pattern_ref, h, state_ref[:, lanes]
        )
    n = lax.broadcasted_iota(jnp.int32, (1, 640), 1)
    late = n >= 512
    y = jnp.where(late, (n - 512) // 32, n // 128)
    m = jnp.where(late, 128 + n % 32, n % 128)
    dzh, dc, y0, t = m // 80, m // 40 % 2, m // 20 % 2, m % 20
    zh_of = jnp.where(dzh == 0, zh, 1 - zh)
    c_of = jnp.where(dc == 0, c, 1 - c)
    source = 80 * (4 * y0 + 2 * zh_of + c_of) + 20 * y + t
    order = lax.broadcasted_iota(jnp.int32, (640, 640), 0) == source
    order = order.astype(jnp.float32).astype(jnp.bfloat16)
    x = masked_ref[...]
    hi = x.astype(jnp.bfloat16)
    mid, low = split(x - hi.astype(jnp.float32))
    moved = (dot(hi, order) + dot(mid, order)) + dot(low, order)
    lane = lax.broadcasted_iota(jnp.int32, (8, 128), 1) // 32
    for y in range(4):
        out_ref[y, :MAIN] = moved[:, 128 * y : 128 * y + 128]
        for slot in range(3):
            tile = jnp.zeros((8, 128), jnp.float32)
            for j in range(min(4, 10 - 4 * slot)):
                rows = 8 * (4 * slot + j)
                part = moved[rows : rows + 8, 512:]
                if j != y:
                    part = pltpu.roll(part, 32 * ((j - y) % 4), 1)
                tile = jnp.where(lane == j, part, tile)
            out_ref[y, MAIN + 8 * slot : MAIN + 8 * slot + 8] = tile


def pack_kernel(masked_ref, out_ref):
    out_ref[...] = jnp.zeros_like(out_ref)
    for y in range(4):
        for zh in range(2):
            for h in range(5):
                out_ref[y, zh, PAD * h : PAD * h + RUN] = masked_ref[
                    zh, RUN * y : RUN * y + RUN, 128 * h : 128 * h + 128
                ]


def unpack_kernel(got_ref, right_ref):
    for y in range(4):
        for zh in range(2):
            for h in range(5):
                right_ref[
                    zh, y // 2, RUN * (y % 2) : RUN * (y % 2) + RUN, 128 * h : 128 * h + 128
                ] = got_ref[y, zh, PAD * h : PAD * h + RUN]


def product_kernel(at_ref, left_ref, right_ref, out_ref, hi_ref, lo_ref):
    for dc in range(2):
        c = lax.rem(at_ref[3] + dc, 2)
        for dzh in range(2):
            rows = slice(40 * (2 * dzh + dc), 40 * (2 * dzh + dc) + 40)
            for x in range(4):
                for y1 in range(2):
                    hi, lo = split(right_ref[c, x, lax.rem(at_ref[2] + dzh, 2), y1])
                    hi_ref[2 * x + y1, rows] = hi
                    lo_ref[2 * x + y1, rows] = lo
    lane = lax.broadcasted_iota(jnp.int32, (8, 128), 1) // 32
    total = jnp.zeros((320, 640), jnp.float32)
    for block in range(8):
        whole = []
        for y in range(4):
            rest = []
            for tile in range(10):
                rows = MAIN + 8 * (tile // 4)
                part = left_ref[block, y, rows : rows + 8]
                rest.append(jnp.where(lane == tile % 4, part, 0.0))
            rest = jnp.concatenate(rest, axis=0)
            whole.append(jnp.concatenate([left_ref[block, y, :MAIN], rest], axis=1))
        left_hi, left_lo = split(jnp.concatenate(whole, axis=0))
        right_hi, right_lo = hi_ref[block], lo_ref[block]
        right_hi = jnp.concatenate([right_hi] + [right_hi[128:]] * 3, axis=0)
        right_lo = jnp.concatenate([right_lo] + [right_lo[128:]] * 3, axis=0)
        total += dot(left_hi, right_hi) + (dot(left_hi, right_lo) + dot(left_lo, right_hi))
    out_ref[...] = total.reshape(4, 80, 640)


def inflate_kernel(at_ref, pattern_ref, shares_ref, out_ref, sums_ref):
    for h in range(5):
        lanes = slice(128 * h, 128 * h + 128)
        x = (shares_ref[0, :, lanes] + shares_ref[1, :, lanes]) + (
            shares_ref[2, :, lanes] + shares_ref[3, :, lanes]
        )
        out_ref[:, lanes] = masked_block(at_ref, at_ref[0], pattern_ref, h, x * x)
    sums_ref[...] = lax.dot_general(
        jnp.ones((8, 640), jnp.float32),
        out_ref[...],
        (((1,), (1,)), ((), ())),
        precision=lax.Precision.HIGHEST,
        preferred_element_type=jnp.float32,
    )


def scale_kernel(nodes, inflated_ref, sums_ref, out_ref):
    totals = lax.dot_general(
        sums_ref[...],
        jnp.ones((8, 128), jnp.float32),
        (((0,), (0,)), ((), ())),
        precision=lax.Precision.HIGHEST,
        preferred_element_type=jnp.float32,
    )
    scale = nodes / totals
    for h in range(5):
        lanes = slice(128 * h, 128 * h + 128)
        out_ref[:, lanes] = inflated_ref[:, lanes] * scale


def gather(block, axis_name):
    size = lax.axis_size(axis_name)
    copies = jnp.broadcast_to(block[None], (size,) + block.shape)
    return lax.all_to_all(copies, axis_name, 0, 0)


def f32(*shape):
    return jax.ShapeDtypeStruct(shape, jnp.float32)


def body(state, in_pattern, out_pattern):
    rows, cols = state.shape
    nodes = cols * lax.axis_size("zl")
    at = jnp.stack(
        [lax.axis_index(ROWS)] + [lax.axis_index(a) for a in ("zl", "zh", "c")]
    ).astype(jnp.int32)

    left, masked = call(
        left_kernel,
        (f32(4, LEFT, 128), f32(rows, cols)),
        [SMEM, SMEM, VMEM],
        (at, in_pattern, state),
    )
    left = lax.all_to_all(left, "y", 0, 0)
    left, masked = lax.optimization_barrier((left, masked))
    left = lax.all_gather(left, "zl", axis=0)

    right = call(pack_kernel, f32(4, 2, 5 * PAD, 128), [VMEM], (gather(masked, "zh"),))
    right = lax.all_to_all(right, "y", 0, 0)
    right = call(unpack_kernel, f32(2, 2, 2 * RUN, cols), [VMEM], (right,))
    right = gather(gather(right, "x"), "c")

    partial = call(
        product_kernel,
        f32(4, rows, cols),
        [SMEM, VMEM, VMEM],
        (at, left, right),
        [pltpu.VMEM((8, 160, cols), jnp.bfloat16)] * 2,
        flops=3 * 10**9,
        size=6 * 10**6,
    )
    shares = lax.all_to_all(partial, "y", 0, 0)
    inflated, sums = call(
        inflate_kernel,
        (f32(rows, cols), f32(8, rows)),
        [SMEM, SMEM, VMEM],
        (at, out_pattern, shares),
    )
    sums = lax.all_to_all(sums.reshape(8, 1, rows), "zl", 0, 0).reshape(8, rows)
    return call(
        functools.partial(scale_kernel, float(nodes)),
        f32(rows, cols),
        [VMEM, VMEM],
        (inflated, sums),
    )


def solution(mesh):
    fine = Mesh(
        mesh.devices.reshape(8, 4, 4, 2, 2), ("zl", "x", "y", "zh", "c")
    )
    return jax.shard_map(
        body,
        mesh=fine,
        in_specs=(P(ROWS, "zl"), P(), P()),
        out_specs=P(ROWS, "zl"),
        check_vma=False,
    )
```

```python
import functools

import jax
import jax.numpy as jnp
from jax import lax
from jax.experimental import pallas as pl
from jax.experimental.pallas import tpu as pltpu
from jax.sharding import Mesh, PartitionSpec as P

BLK = 256
ROWS = ("x", "y", "zh", "c")
MAIN, REST = 80, 24
LEFT = MAIN + REST
SLOTS = 248
ALL = 400
UNITS = 32
EXACT = lax.Precision.HIGHEST
VMEM = pl.BlockSpec(memory_space=pltpu.VMEM)
SMEM = pl.BlockSpec(memory_space=pltpu.SMEM)


def iota(shape, axis):
    return lax.broadcasted_iota(jnp.int32, shape, axis)


def one_hot(mask):
    return mask.astype(jnp.float32).astype(jnp.bfloat16)


def split(x):
    hi = x.astype(jnp.bfloat16)
    return hi, (x - hi.astype(jnp.float32)).astype(jnp.bfloat16)


def split3(x):
    hi = x.astype(jnp.bfloat16)
    return (hi, *split(x - hi.astype(jnp.float32)))


def dot(a, b, precision=None):
    return jnp.dot(a, b, preferred_element_type=jnp.float32, precision=precision)


def dot_rows(a, b, precision=None):
    return lax.dot_general(
        a, b, (((1,), (1,)), ((), ())), precision=precision, preferred_element_type=jnp.float32
    )


def call(kernel, outs, in_specs, args, scratch=(), flops=10**6, size=10**6, out_specs=None):
    return pl.pallas_call(
        kernel,
        out_shape=outs,
        in_specs=in_specs,
        out_specs=out_specs or jax.tree.map(lambda _: VMEM, outs),
        scratch_shapes=scratch,
        compiler_params=pltpu.CompilerParams(vmem_limit_bytes=40 * 2**20),
        cost_estimate=pl.CostEstimate(
            flops=flops, bytes_accessed=size, transcendentals=0
        ),
    )(*args)


def masked_block(at_ref, owner, pattern_ref, h, x):
    row = owner * 80
    col = (5 * at_ref[1] + h) // 2
    first = row // BLK
    low = pattern_ref[first, col].astype(jnp.float32)
    high = pattern_ref[jnp.minimum(first + 1, 19), col].astype(jnp.float32)
    here = lax.broadcasted_iota(jnp.int32, (80, 128), 0) + row < (first + 1) * BLK
    return x * jnp.where(here, low, high)


def chunk_of(q, zh, c):
    return 20 * (q // 5) + 10 * zh + 5 * c + q % 5


def places(pattern, zh, c):
    rows = one_hot(chunk_of(iota((80, 1), 0), zh, c) // 16 == iota((80, 20), 1))
    cols = one_hot(iota((20, 40), 1) // 2 == iota((20, 40), 0))
    live = dot(dot(rows, pattern).astype(jnp.bfloat16), cols)
    before = dot(one_hot(iota((80, 80), 1) < iota((80, 80), 0)), live.astype(jnp.bfloat16))
    total = jnp.broadcast_to(jnp.sum(live, axis=0, keepdims=True), (80, 40))
    a, b = iota((40, 40), 0), iota((40, 40), 1)
    earlier = dot(total.astype(jnp.bfloat16), one_hot((a // 5 == b // 5) & (a < b)))
    return jnp.where(live > 0, before + earlier, -1.0)


def places_across(pattern, zh, c):
    rows = one_hot(chunk_of(iota((1, 80), 1), zh, c) // 16 == iota((20, 80), 0))
    cols = one_hot(iota((40, 20), 0) // 2 == iota((40, 20), 1))
    live = dot(dot_rows(cols, pattern).astype(jnp.bfloat16), rows)
    before = dot(live.astype(jnp.bfloat16), one_hot(iota((80, 80), 0) < iota((80, 80), 1)))
    total = jnp.broadcast_to(jnp.sum(live, axis=1, keepdims=True), (40, 80))
    a, b = iota((40, 40), 1), iota((40, 40), 0)
    earlier = dot(one_hot((a // 5 == b // 5) & (a < b)), total.astype(jnp.bfloat16))
    return jnp.where(live > 0, before + earlier, -1.0)


def most_live(pattern):
    counts = []
    for group in range(4):
        rows = chunk_of(iota((80, 1), 0), group // 2, group % 2) // 16 == iota((80, 20), 1)
        counts.append(jnp.sum(rows.astype(jnp.float32), axis=0, keepdims=True))
    counts = jnp.concatenate(counts * 2, axis=0).astype(jnp.bfloat16)
    wide = jnp.zeros((20, 8), jnp.float32)
    for h in range(5):
        wide += ((5 * iota((20, 8), 1) + h) // 2 == iota((20, 8), 0)).astype(jnp.float32)
    most = dot(dot(counts, pattern).astype(jnp.bfloat16), wide.astype(jnp.bfloat16))
    return jnp.max(most).astype(jnp.int32)


def left_kernel(at_ref, pattern_ref, blocks_ref, state_ref, out_ref, masked_ref, most_ref):
    zh, c = at_ref[2], at_ref[3]
    most_ref[0, 0] = most_live(blocks_ref[...].astype(jnp.float32).astype(jnp.bfloat16))
    for h in range(5):
        lanes = slice(128 * h, 128 * h + 128)
        masked_ref[:, lanes] = masked_block(
            at_ref, at_ref[0], pattern_ref, h, state_ref[:, lanes]
        )
    n = lax.broadcasted_iota(jnp.int32, (1, 640), 1)
    late = n >= 512
    y = jnp.where(late, (n - 512) // 32, n // 128)
    m = jnp.where(late, 128 + n % 32, n % 128)
    dzh, dc, t, y0, e = m // 80, m // 40 % 2, m % 40 // 10, m % 10 // 5, m % 5
    zh_of = jnp.where(dzh == 0, zh, 1 - zh)
    c_of = jnp.where(dc == 0, c, 1 - c)
    source = 80 * (4 * y0 + 2 * zh_of + c_of) + 16 * e + 4 * y + t
    order = lax.broadcasted_iota(jnp.int32, (640, 640), 0) == source
    order = order.astype(jnp.float32).astype(jnp.bfloat16)
    x = masked_ref[...]
    hi = x.astype(jnp.bfloat16)
    mid, low = split(x - hi.astype(jnp.float32))
    moved = (dot(hi, order) + dot(mid, order)) + dot(low, order)
    lane = lax.broadcasted_iota(jnp.int32, (8, 128), 1) // 32
    for y in range(4):
        out_ref[y, :MAIN] = moved[:, 128 * y : 128 * y + 128]
        for slot in range(3):
            tile = jnp.zeros((8, 128), jnp.float32)
            for j in range(min(4, 10 - 4 * slot)):
                rows = 8 * (4 * slot + j)
                part = moved[rows : rows + 8, 512:]
                if j != y:
                    part = pltpu.roll(part, 32 * ((j - y) % 4), 1)
                tile = jnp.where(lane == j, part, tile)
            out_ref[y, MAIN + 8 * slot : MAIN + 8 * slot + 8] = tile


def units_kernel(masked_ref, out_ref, plain_ref):
    for h in range(5):
        plain_ref[h] = masked_ref[:, 128 * h : 128 * h + 128]
    for x in range(4):
        for y in range(4):
            for h in range(5):
                out_ref[4 * x + y, 5 * h : 5 * h + 5] = plain_ref[
                    h, pl.ds(4 * y + x, 5, stride=16), :
                ]
            out_ref[4 * x + y, 25:] = jnp.zeros((UNITS - 25, 128), jnp.float32)


def pack_kernel(slots, at_ref, pattern_ref, got_ref, right_ref):
    pattern = pattern_ref[...].astype(jnp.float32).astype(jnp.bfloat16)
    place = places_across(pattern, at_ref[2], at_ref[3])
    count = 16 * UNITS
    units = jnp.concatenate(split3(got_ref[...].reshape(count, 128)), axis=1)
    row = iota((1, count), 1)
    j = row % UNITS
    q = 5 * (row // UNITS) + j % 5
    expand = (q == iota((80, count), 0)).astype(jnp.float32)
    spread = dot(place, expand, EXACT)
    mine = 5 * at_ref[1] + j // 5 == iota((40, count), 0)
    slot = jnp.sum(jnp.where(mine, spread, 0.0), axis=0, keepdims=True)
    slot = jnp.where(j < 25, slot, -1.0)
    pick = one_hot(slot == iota((slots, count), 0).astype(jnp.float32))
    got = dot(pick, units)
    right_ref[...] = (got[:, :128] + got[:, 128:256]) + got[:, 256:]


def spread_kernel(slots, at_ref, pattern_ref, own_ref, swap_ref, out_ref):
    pattern = pattern_ref[...].astype(jnp.float32).astype(jnp.bfloat16)
    zl, zh, c = at_ref[1], at_ref[2], at_ref[3]
    slot = iota((80, slots), 1).astype(jnp.float32)
    half = iota((80, 40), 1)
    for dc, ref in ((0, own_ref), (1, swap_ref)):
        for dzh in range(2):
            there = jnp.abs(zh - dzh)
            place = places(pattern, there, jnp.abs(c - dc))
            pick = []
            for h in range(5):
                at = jnp.sum(jnp.where(half == 5 * zl + h, place, 0.0), axis=1, keepdims=True)
                pick.append(one_hot(at == slot))
            pick = jnp.concatenate(pick, axis=0)
            for t in range(4):
                got = dot(pick, jnp.concatenate(split3(ref[t, there]), axis=1))
                got = (got[:, :128] + got[:, 128:256]) + got[:, 256:]
                got = jnp.concatenate([got[80 * h : 80 * h + 80] for h in range(5)], axis=1)
                base = 40 * (2 * dzh + dc) + 10 * t
                for block in range(8):
                    out_ref[block, base : base + 10] = got[10 * block : 10 * block + 10]


def product_kernel(left_ref, right_ref, out_ref):
    lane = lax.broadcasted_iota(jnp.int32, (8, 128), 1) // 32
    total = jnp.zeros((320, 640), jnp.float32)
    for block in range(8):
        whole = []
        for y in range(4):
            rest = []
            for tile in range(10):
                rows = MAIN + 8 * (tile // 4)
                part = left_ref[block, y, rows : rows + 8]
                rest.append(jnp.where(lane == tile % 4, part, 0.0))
            rest = jnp.concatenate(rest, axis=0)
            whole.append(jnp.concatenate([left_ref[block, y, :MAIN], rest], axis=1))
        left_hi, left_lo = split(jnp.concatenate(whole, axis=0))
        right = right_ref[block]
        right_hi, right_lo = split(jnp.concatenate([right] + [right[128:]] * 3, axis=0))
        total += dot(left_hi, right_hi) + (dot(left_hi, right_lo) + dot(left_lo, right_hi))
    out_ref[...] = total.reshape(4, 80, 640)


def inflate_kernel(at_ref, pattern_ref, shares_ref, out_ref, sums_ref):
    for h in range(5):
        lanes = slice(128 * h, 128 * h + 128)
        x = (shares_ref[0, :, lanes] + shares_ref[1, :, lanes]) + (
            shares_ref[2, :, lanes] + shares_ref[3, :, lanes]
        )
        out_ref[:, lanes] = masked_block(at_ref, at_ref[0], pattern_ref, h, x * x)
    sums_ref[...] = lax.dot_general(
        jnp.ones((8, 640), jnp.float32),
        out_ref[...],
        (((1,), (1,)), ((), ())),
        precision=lax.Precision.HIGHEST,
        preferred_element_type=jnp.float32,
    )


def scale_kernel(nodes, inflated_ref, sums_ref, out_ref):
    totals = lax.dot_general(
        sums_ref[...],
        jnp.ones((8, 128), jnp.float32),
        (((0,), (0,)), ((), ())),
        precision=lax.Precision.HIGHEST,
        preferred_element_type=jnp.float32,
    )
    scale = nodes / totals
    for h in range(5):
        lanes = slice(128 * h, 128 * h + 128)
        out_ref[:, lanes] = inflated_ref[:, lanes] * scale


def swap(x, axis_name):
    return lax.ppermute(x, axis_name, [(0, 1), (1, 0)])


def gather(x, axis_name, limit):
    rows = x.shape[-2]
    parts = -(-rows // limit)
    size = rows // parts
    done = [
        lax.all_gather(x[..., i * size : (i + 1) * size, :], axis_name, axis=0)
        for i in range(parts)
    ]
    return done[0] if parts == 1 else jnp.concatenate(done, axis=-2)


def f32(*shape):
    return jax.ShapeDtypeStruct(shape, jnp.float32)


def partial_product(slots, at, in_pattern, left, masked):
    rows, cols = masked.shape
    left, masked = lax.optimization_barrier((left, masked))
    left = lax.all_gather(left, "zl", axis=0)

    units = call(
        units_kernel,
        f32(16, UNITS, 128),
        [VMEM],
        (masked,),
        [pltpu.VMEM((5, rows, 128), jnp.float32)],
    )
    got = lax.all_to_all(units, ("x", "y"), 0, 0)
    right = call(
        functools.partial(pack_kernel, slots),
        f32(slots, 128),
        [SMEM, VMEM, VMEM],
        (at, in_pattern, got),
    )
    own = gather(gather(right, "zh", SLOTS), "x", SLOTS)
    right = call(
        functools.partial(spread_kernel, slots),
        f32(8, 160, cols),
        [SMEM, VMEM, VMEM, VMEM],
        (at, in_pattern, own, swap(own, "c")),
    )
    return call(
        product_kernel,
        f32(4, rows, cols),
        [VMEM, VMEM],
        (left, right),
        flops=3 * 10**9,
        size=6 * 10**6,
    )


def body(state, in_pattern, out_pattern):
    rows, cols = state.shape
    nodes = cols * lax.axis_size("zl")
    at = jnp.stack([lax.axis_index(ROWS)] + [lax.axis_index(a) for a in ("zl", "zh", "c")])
    at = at.astype(jnp.int32)
    left, masked, most = call(
        left_kernel,
        (f32(4, LEFT, 128), f32(rows, cols), jax.ShapeDtypeStruct((1, 1), jnp.int32)),
        [SMEM, SMEM, VMEM, VMEM],
        (at, in_pattern, in_pattern, state),
        out_specs=(VMEM, VMEM, SMEM),
    )
    left = lax.all_to_all(left, "y", 0, 0)
    partial = lax.cond(
        most[0, 0] <= SLOTS,
        functools.partial(partial_product, SLOTS),
        functools.partial(partial_product, ALL),
        at,
        in_pattern,
        left,
        masked,
    )
    shares = lax.all_to_all(partial, "y", 0, 0)
    inflated, sums = call(
        inflate_kernel,
        (f32(rows, cols), f32(8, rows)),
        [SMEM, SMEM, VMEM],
        (at, out_pattern, shares),
    )
    sums = lax.all_to_all(sums.reshape(8, 1, rows), "zl", 0, 0).reshape(8, rows)
    return call(
        functools.partial(scale_kernel, float(nodes)),
        f32(rows, cols),
        [VMEM, VMEM],
        (inflated, sums),
    )


def solution(mesh):
    fine = Mesh(
        mesh.devices.reshape(8, 4, 4, 2, 2), ("zl", "x", "y", "zh", "c")
    )
    return jax.shard_map(
        body,
        mesh=fine,
        in_specs=(P(ROWS, "zl"), P(), P()),
        out_specs=P(ROWS, "zl"),
        check_vma=False,
    )
```

```python
import functools

import jax
import jax.numpy as jnp
from jax import lax
from jax.experimental import pallas as pl
from jax.experimental.pallas import tpu as pltpu
from jax.sharding import Mesh, PartitionSpec as P

BLK = 256
ROWS = ("x", "y", "zh", "c")
MAIN, REST = 80, 24
LEFT = MAIN + REST
SLOTS = 248
ALL = 400
UNITS = 32
EXACT = lax.Precision.HIGHEST
VMEM = pl.BlockSpec(memory_space=pltpu.VMEM)
SMEM = pl.BlockSpec(memory_space=pltpu.SMEM)


def iota(shape, axis):
    return lax.broadcasted_iota(jnp.int32, shape, axis)


def one_hot(mask):
    return mask.astype(jnp.float32).astype(jnp.bfloat16)


def split(x):
    hi = x.astype(jnp.bfloat16)
    return hi, (x - hi.astype(jnp.float32)).astype(jnp.bfloat16)


def split3(x):
    hi = x.astype(jnp.bfloat16)
    return (hi, *split(x - hi.astype(jnp.float32)))


def dot(a, b, precision=None):
    return jnp.dot(a, b, preferred_element_type=jnp.float32, precision=precision)


def dot_rows(a, b, precision=None):
    return lax.dot_general(
        a, b, (((1,), (1,)), ((), ())), precision=precision, preferred_element_type=jnp.float32
    )


def call(kernel, outs, in_specs, args, scratch=(), flops=10**6, size=10**6, out_specs=None):
    return pl.pallas_call(
        kernel,
        out_shape=outs,
        in_specs=in_specs,
        out_specs=out_specs or jax.tree.map(lambda _: VMEM, outs),
        scratch_shapes=scratch,
        compiler_params=pltpu.CompilerParams(vmem_limit_bytes=40 * 2**20),
        cost_estimate=pl.CostEstimate(
            flops=flops, bytes_accessed=size, transcendentals=0
        ),
    )(*args)


def masked_block(at_ref, owner, pattern_ref, h, x):
    row = owner * 80
    col = (5 * at_ref[1] + h) // 2
    first = row // BLK
    low = pattern_ref[first, col].astype(jnp.float32)
    high = pattern_ref[jnp.minimum(first + 1, 19), col].astype(jnp.float32)
    here = lax.broadcasted_iota(jnp.int32, (80, 128), 0) + row < (first + 1) * BLK
    return x * jnp.where(here, low, high)


def chunk_of(q, zh, c):
    return 20 * (q // 5) + 10 * zh + 5 * c + q % 5


def places(pattern, zh, c):
    rows = one_hot(chunk_of(iota((80, 1), 0), zh, c) // 16 == iota((80, 20), 1))
    cols = one_hot(iota((20, 40), 1) // 2 == iota((20, 40), 0))
    live = dot(dot(rows, pattern).astype(jnp.bfloat16), cols)
    before = dot(one_hot(iota((80, 80), 1) < iota((80, 80), 0)), live.astype(jnp.bfloat16))
    total = jnp.broadcast_to(jnp.sum(live, axis=0, keepdims=True), (80, 40))
    a, b = iota((40, 40), 0), iota((40, 40), 1)
    earlier = dot(total.astype(jnp.bfloat16), one_hot((a // 5 == b // 5) & (a < b)))
    return jnp.where(live > 0, before + earlier, -1.0)


def places_across(pattern, zh, c):
    rows = one_hot(chunk_of(iota((1, 80), 1), zh, c) // 16 == iota((20, 80), 0))
    cols = one_hot(iota((40, 20), 0) // 2 == iota((40, 20), 1))
    live = dot(dot_rows(cols, pattern).astype(jnp.bfloat16), rows)
    before = dot(live.astype(jnp.bfloat16), one_hot(iota((80, 80), 0) < iota((80, 80), 1)))
    total = jnp.broadcast_to(jnp.sum(live, axis=1, keepdims=True), (40, 80))
    a, b = iota((40, 40), 1), iota((40, 40), 0)
    earlier = dot(one_hot((a // 5 == b // 5) & (a < b)), total.astype(jnp.bfloat16))
    return jnp.where(live > 0, before + earlier, -1.0)


def most_live(pattern):
    counts = []
    for group in range(4):
        rows = chunk_of(iota((80, 1), 0), group // 2, group % 2) // 16 == iota((80, 20), 1)
        counts.append(jnp.sum(rows.astype(jnp.float32), axis=0, keepdims=True))
    counts = jnp.concatenate(counts * 2, axis=0).astype(jnp.bfloat16)
    wide = jnp.zeros((20, 8), jnp.float32)
    for h in range(5):
        wide += ((5 * iota((20, 8), 1) + h) // 2 == iota((20, 8), 0)).astype(jnp.float32)
    most = dot(dot(counts, pattern).astype(jnp.bfloat16), wide.astype(jnp.bfloat16))
    return jnp.max(most).astype(jnp.int32)


def left_kernel(at_ref, pattern_ref, state_ref, out_ref, masked_ref):
    zh, c = at_ref[2], at_ref[3]
    for h in range(5):
        lanes = slice(128 * h, 128 * h + 128)
        masked_ref[:, lanes] = masked_block(
            at_ref, at_ref[0], pattern_ref, h, state_ref[:, lanes]
        )
    n = lax.broadcasted_iota(jnp.int32, (1, 640), 1)
    late = n >= 512
    y = jnp.where(late, (n - 512) // 32, n // 128)
    m = jnp.where(late, 128 + n % 32, n % 128)
    dzh, dc, t, y0, e = m // 80, m // 40 % 2, m % 40 // 10, m % 10 // 5, m % 5
    zh_of = jnp.where(dzh == 0, zh, 1 - zh)
    c_of = jnp.where(dc == 0, c, 1 - c)
    source = 80 * (4 * y0 + 2 * zh_of + c_of) + 16 * e + 4 * y + t
    order = lax.broadcasted_iota(jnp.int32, (640, 640), 0) == source
    order = order.astype(jnp.float32).astype(jnp.bfloat16)
    x = masked_ref[...]
    hi = x.astype(jnp.bfloat16)
    mid, low = split(x - hi.astype(jnp.float32))
    moved = (dot(hi, order) + dot(mid, order)) + dot(low, order)
    lane = lax.broadcasted_iota(jnp.int32, (8, 128), 1) // 32
    for y in range(4):
        out_ref[y, :MAIN] = moved[:, 128 * y : 128 * y + 128]
        for slot in range(3):
            tile = jnp.zeros((8, 128), jnp.float32)
            for j in range(min(4, 10 - 4 * slot)):
                rows = 8 * (4 * slot + j)
                part = moved[rows : rows + 8, 512:]
                if j != y:
                    part = pltpu.roll(part, 32 * ((j - y) % 4), 1)
                tile = jnp.where(lane == j, part, tile)
            out_ref[y, MAIN + 8 * slot : MAIN + 8 * slot + 8] = tile


def units_kernel(pattern_ref, masked_ref, out_ref, most_ref, plain_ref):
    most_ref[0, 0] = most_live(pattern_ref[...].astype(jnp.float32).astype(jnp.bfloat16))
    for h in range(5):
        plain_ref[h] = masked_ref[:, 128 * h : 128 * h + 128]
    for x in range(4):
        for y in range(4):
            for h in range(5):
                out_ref[4 * x + y, 5 * h : 5 * h + 5] = plain_ref[
                    h, pl.ds(4 * y + x, 5, stride=16), :
                ]
            out_ref[4 * x + y, 25:] = jnp.zeros((UNITS - 25, 128), jnp.float32)


def pack_kernel(slots, at_ref, pattern_ref, got_ref, right_ref):
    pattern = pattern_ref[...].astype(jnp.float32).astype(jnp.bfloat16)
    place = places_across(pattern, at_ref[2], at_ref[3])
    count = 16 * UNITS
    units = jnp.concatenate(split3(got_ref[...].reshape(count, 128)), axis=1)
    row = iota((1, count), 1)
    j = row % UNITS
    q = 5 * (row // UNITS) + j % 5
    expand = (q == iota((80, count), 0)).astype(jnp.float32)
    spread = dot(place, expand, EXACT)
    mine = 5 * at_ref[1] + j // 5 == iota((40, count), 0)
    slot = jnp.sum(jnp.where(mine, spread, 0.0), axis=0, keepdims=True)
    slot = jnp.where(j < 25, slot, -1.0)
    pick = one_hot(slot == iota((slots, count), 0).astype(jnp.float32))
    got = dot(pick, units)
    right_ref[...] = (got[:, :128] + got[:, 128:256]) + got[:, 256:]


def spread_kernel(slots, at_ref, pattern_ref, own_ref, swap_ref, hi_ref, lo_ref, out_ref):
    pattern = pattern_ref[...].astype(jnp.float32).astype(jnp.bfloat16)
    zl, zh, c = at_ref[1], at_ref[2], at_ref[3]
    slot = iota((80, slots), 1).astype(jnp.float32)
    half = iota((80, 40), 1)
    for dc, ref in ((0, own_ref), (1, swap_ref)):
        for dzh in range(2):
            there = jnp.abs(zh - dzh)
            place = places(pattern, there, jnp.abs(c - dc))
            pick = []
            for h in range(5):
                at = jnp.sum(jnp.where(half == 5 * zl + h, place, 0.0), axis=1, keepdims=True)
                pick.append(one_hot(at == slot))
            pick = jnp.concatenate(pick, axis=0)
            for t in range(4):
                got = dot(pick, jnp.concatenate(split3(ref[t, there]), axis=1))
                got = (got[:, :128] + got[:, 128:256]) + got[:, 256:]
                got = jnp.concatenate([got[80 * h : 80 * h + 80] for h in range(5)], axis=1)
                base = 40 * (2 * dzh + dc) + 10 * t
                for block in range(8):
                    out_ref[block, base : base + 10] = got[10 * block : 10 * block + 10]
    for block in range(8):
        rows = out_ref[block]
        rows = jnp.concatenate([rows] + [rows[128:]] * 3, axis=0)
        hi_ref[block], lo_ref[block] = split(rows)


def product_kernel(left_ref, hi_ref, lo_ref, out_ref):
    lane = lax.broadcasted_iota(jnp.int32, (8, 128), 1) // 32
    total = jnp.zeros((320, 640), jnp.float32)
    for block in range(8):
        whole = []
        for y in range(4):
            rest = []
            for tile in range(10):
                rows = MAIN + 8 * (tile // 4)
                part = left_ref[block, y, rows : rows + 8]
                rest.append(jnp.where(lane == tile % 4, part, 0.0))
            rest = jnp.concatenate(rest, axis=0)
            whole.append(jnp.concatenate([left_ref[block, y, :MAIN], rest], axis=1))
        left_hi, left_lo = split(jnp.concatenate(whole, axis=0))
        right_hi, right_lo = hi_ref[block], lo_ref[block]
        total += dot(left_hi, right_hi) + (dot(left_hi, right_lo) + dot(left_lo, right_hi))
    out_ref[...] = total.reshape(4, 80, 640)


def inflate_kernel(at_ref, pattern_ref, shares_ref, out_ref, sums_ref):
    for h in range(5):
        lanes = slice(128 * h, 128 * h + 128)
        x = (shares_ref[0, :, lanes] + shares_ref[1, :, lanes]) + (
            shares_ref[2, :, lanes] + shares_ref[3, :, lanes]
        )
        out_ref[:, lanes] = masked_block(at_ref, at_ref[0], pattern_ref, h, x * x)
    sums_ref[...] = lax.dot_general(
        jnp.ones((8, 640), jnp.float32),
        out_ref[...],
        (((1,), (1,)), ((), ())),
        precision=lax.Precision.HIGHEST,
        preferred_element_type=jnp.float32,
    )


def scale_kernel(nodes, inflated_ref, sums_ref, out_ref):
    totals = lax.dot_general(
        sums_ref[...],
        jnp.ones((8, 128), jnp.float32),
        (((0,), (0,)), ((), ())),
        precision=lax.Precision.HIGHEST,
        preferred_element_type=jnp.float32,
    )
    scale = nodes / totals
    for h in range(5):
        lanes = slice(128 * h, 128 * h + 128)
        out_ref[:, lanes] = inflated_ref[:, lanes] * scale


def swap(x, axis_name):
    return lax.ppermute(x, axis_name, [(0, 1), (1, 0)])


def gather(x, axis_name, limit):
    rows = x.shape[-2]
    parts = -(-rows // limit)
    size = rows // parts
    done = [
        lax.all_gather(x[..., i * size : (i + 1) * size, :], axis_name, axis=0)
        for i in range(parts)
    ]
    return done[0] if parts == 1 else jnp.concatenate(done, axis=-2)


def f32(*shape):
    return jax.ShapeDtypeStruct(shape, jnp.float32)


def right_halves(slots, at, in_pattern, got):
    cols = 640
    right = call(
        functools.partial(pack_kernel, slots),
        f32(slots, 128),
        [SMEM, VMEM, VMEM],
        (at, in_pattern, got),
    )
    own = gather(gather(right, "zh", SLOTS), "x", SLOTS)
    half = jax.ShapeDtypeStruct((8, 256, cols), jnp.bfloat16)
    return call(
        functools.partial(spread_kernel, slots),
        (half, half),
        [SMEM, VMEM, VMEM, VMEM],
        (at, in_pattern, own, swap(own, "c")),
        [pltpu.VMEM((8, 160, cols), jnp.float32)],
    )


def body(state, in_pattern, out_pattern):
    rows, cols = state.shape
    nodes = cols * lax.axis_size("zl")
    at = jnp.stack([lax.axis_index(ROWS)] + [lax.axis_index(a) for a in ("zl", "zh", "c")])
    at = at.astype(jnp.int32)
    left, masked = call(
        left_kernel,
        (f32(4, LEFT, 128), f32(rows, cols)),
        [SMEM, SMEM, VMEM],
        (at, in_pattern, state),
    )
    left = lax.all_to_all(left, "y", 0, 0)
    left, masked = lax.optimization_barrier((left, masked))
    left = lax.all_gather(left, "zl", axis=0)

    units, most = call(
        units_kernel,
        (f32(16, UNITS, 128), jax.ShapeDtypeStruct((1, 1), jnp.int32)),
        [VMEM, VMEM],
        (in_pattern, masked),
        [pltpu.VMEM((5, rows, 128), jnp.float32)],
        out_specs=(VMEM, SMEM),
    )
    got = lax.all_to_all(units, ("x", "y"), 0, 0)
    right_hi, right_lo = lax.cond(
        most[0, 0] <= SLOTS,
        functools.partial(right_halves, SLOTS),
        functools.partial(right_halves, ALL),
        at,
        in_pattern,
        got,
    )
    partial = call(
        product_kernel,
        f32(4, rows, cols),
        [VMEM, VMEM, VMEM],
        (left, right_hi, right_lo),
        flops=3 * 10**9,
        size=6 * 10**6,
    )
    shares = lax.all_to_all(partial, "y", 0, 0)
    inflated, sums = call(
        inflate_kernel,
        (f32(rows, cols), f32(8, rows)),
        [SMEM, SMEM, VMEM],
        (at, out_pattern, shares),
    )
    sums = lax.all_to_all(sums.reshape(8, 1, rows), "zl", 0, 0).reshape(8, rows)
    return call(
        functools.partial(scale_kernel, float(nodes)),
        f32(rows, cols),
        [VMEM, VMEM],
        (inflated, sums),
    )


def solution(mesh):
    fine = Mesh(
        mesh.devices.reshape(8, 4, 4, 2, 2), ("zl", "x", "y", "zh", "c")
    )
    return jax.shard_map(
        body,
        mesh=fine,
        in_specs=(P(ROWS, "zl"), P(), P()),
        out_specs=P(ROWS, "zl"),
        check_vma=False,
    )
```

```python
import functools

import jax
import jax.numpy as jnp
from jax import lax
from jax.experimental import pallas as pl
from jax.experimental.pallas import tpu as pltpu
from jax.sharding import Mesh, PartitionSpec as P

BLK = 256
ROWS = ("x", "y", "zh", "c")
MAIN, REST = 80, 24
LEFT = MAIN + REST
SLOTS = 248
ALL = 400
UNITS = 32
EXACT = lax.Precision.HIGHEST
VMEM = pl.BlockSpec(memory_space=pltpu.VMEM)
SMEM = pl.BlockSpec(memory_space=pltpu.SMEM)


def iota(shape, axis):
    return lax.broadcasted_iota(jnp.int32, shape, axis)


def one_hot(mask):
    return mask.astype(jnp.float32).astype(jnp.bfloat16)


def split(x):
    hi = x.astype(jnp.bfloat16)
    return hi, (x - hi.astype(jnp.float32)).astype(jnp.bfloat16)


def split3(x):
    hi = x.astype(jnp.bfloat16)
    return (hi, *split(x - hi.astype(jnp.float32)))


def dot(a, b, precision=None):
    return jnp.dot(a, b, preferred_element_type=jnp.float32, precision=precision)


def dot_rows(a, b, precision=None):
    return lax.dot_general(
        a, b, (((1,), (1,)), ((), ())), precision=precision, preferred_element_type=jnp.float32
    )


def call(kernel, outs, in_specs, args, scratch=(), flops=10**6, size=10**6, out_specs=None):
    return pl.pallas_call(
        kernel,
        out_shape=outs,
        in_specs=in_specs,
        out_specs=out_specs or jax.tree.map(lambda _: VMEM, outs),
        scratch_shapes=scratch,
        compiler_params=pltpu.CompilerParams(vmem_limit_bytes=26 * 2**20),
        cost_estimate=pl.CostEstimate(
            flops=flops, bytes_accessed=size, transcendentals=0
        ),
    )(*args)


def masked_block(at_ref, owner, pattern_ref, h, x):
    row = owner * 80
    col = (5 * at_ref[1] + h) // 2
    first = row // BLK
    low = pattern_ref[first, col].astype(jnp.float32)
    high = pattern_ref[jnp.minimum(first + 1, 19), col].astype(jnp.float32)
    here = lax.broadcasted_iota(jnp.int32, (80, 128), 0) + row < (first + 1) * BLK
    return x * jnp.where(here, low, high)


def chunk_of(q, zh, c):
    return 20 * (q // 5) + 10 * zh + 5 * c + q % 5


def places(pattern, zh, c):
    rows = one_hot(chunk_of(iota((80, 1), 0), zh, c) // 16 == iota((80, 20), 1))
    cols = one_hot(iota((20, 40), 1) // 2 == iota((20, 40), 0))
    live = dot(dot(rows, pattern).astype(jnp.bfloat16), cols)
    before = dot(one_hot(iota((80, 80), 1) < iota((80, 80), 0)), live.astype(jnp.bfloat16))
    total = jnp.broadcast_to(jnp.sum(live, axis=0, keepdims=True), (80, 40))
    a, b = iota((40, 40), 0), iota((40, 40), 1)
    earlier = dot(total.astype(jnp.bfloat16), one_hot((a // 5 == b // 5) & (a < b)))
    return jnp.where(live > 0, before + earlier, -1.0)


def places_across(pattern, zh, c):
    rows = one_hot(chunk_of(iota((1, 80), 1), zh, c) // 16 == iota((20, 80), 0))
    cols = one_hot(iota((40, 20), 0) // 2 == iota((40, 20), 1))
    live = dot(dot_rows(cols, pattern).astype(jnp.bfloat16), rows)
    before = dot(live.astype(jnp.bfloat16), one_hot(iota((80, 80), 0) < iota((80, 80), 1)))
    total = jnp.broadcast_to(jnp.sum(live, axis=1, keepdims=True), (40, 80))
    a, b = iota((40, 40), 1), iota((40, 40), 0)
    earlier = dot(one_hot((a // 5 == b // 5) & (a < b)), total.astype(jnp.bfloat16))
    return jnp.where(live > 0, before + earlier, -1.0)


def most_live(pattern):
    counts = []
    for group in range(4):
        rows = chunk_of(iota((80, 1), 0), group // 2, group % 2) // 16 == iota((80, 20), 1)
        counts.append(jnp.sum(rows.astype(jnp.float32), axis=0, keepdims=True))
    counts = jnp.concatenate(counts * 2, axis=0).astype(jnp.bfloat16)
    wide = jnp.zeros((20, 8), jnp.float32)
    for h in range(5):
        wide += ((5 * iota((20, 8), 1) + h) // 2 == iota((20, 8), 0)).astype(jnp.float32)
    most = dot(dot(counts, pattern).astype(jnp.bfloat16), wide.astype(jnp.bfloat16))
    return jnp.max(most).astype(jnp.int32)


def left_kernel(at_ref, pattern_ref, state_ref, out_ref, masked_ref):
    zh, c = at_ref[2], at_ref[3]
    for h in range(5):
        lanes = slice(128 * h, 128 * h + 128)
        masked_ref[:, lanes] = masked_block(
            at_ref, at_ref[0], pattern_ref, h, state_ref[:, lanes]
        )
    n = lax.broadcasted_iota(jnp.int32, (1, 640), 1)
    late = n >= 512
    y = jnp.where(late, (n - 512) // 32, n // 128)
    m = jnp.where(late, 128 + n % 32, n % 128)
    dzh, dc, t, y0, e = m // 80, m // 40 % 2, m % 40 // 10, m % 10 // 5, m % 5
    zh_of = jnp.where(dzh == 0, zh, 1 - zh)
    c_of = jnp.where(dc == 0, c, 1 - c)
    source = 80 * (4 * y0 + 2 * zh_of + c_of) + 16 * e + 4 * y + t
    order = lax.broadcasted_iota(jnp.int32, (640, 640), 0) == source
    order = order.astype(jnp.float32).astype(jnp.bfloat16)
    x = masked_ref[...]
    hi = x.astype(jnp.bfloat16)
    mid, low = split(x - hi.astype(jnp.float32))
    moved = (dot(hi, order) + dot(mid, order)) + dot(low, order)
    lane = lax.broadcasted_iota(jnp.int32, (8, 128), 1) // 32
    for y in range(4):
        out_ref[y, :MAIN] = moved[:, 128 * y : 128 * y + 128]
        for slot in range(3):
            tile = jnp.zeros((8, 128), jnp.float32)
            for j in range(min(4, 10 - 4 * slot)):
                rows = 8 * (4 * slot + j)
                part = moved[rows : rows + 8, 512:]
                if j != y:
                    part = pltpu.roll(part, 32 * ((j - y) % 4), 1)
                tile = jnp.where(lane == j, part, tile)
            out_ref[y, MAIN + 8 * slot : MAIN + 8 * slot + 8] = tile


def units_kernel(pattern_ref, masked_ref, out_ref, most_ref, plain_ref):
    most_ref[0, 0] = most_live(pattern_ref[...].astype(jnp.float32).astype(jnp.bfloat16))
    for h in range(5):
        plain_ref[h] = masked_ref[:, 128 * h : 128 * h + 128]
    for x in range(4):
        for y in range(4):
            for h in range(5):
                out_ref[4 * x + y, 5 * h : 5 * h + 5] = plain_ref[
                    h, pl.ds(4 * y + x, 5, stride=16), :
                ]
            out_ref[4 * x + y, 25:] = jnp.zeros((UNITS - 25, 128), jnp.float32)


def pack_kernel(slots, at_ref, pattern_ref, got_ref, right_ref):
    pattern = pattern_ref[...].astype(jnp.float32).astype(jnp.bfloat16)
    place = places_across(pattern, at_ref[2], at_ref[3])
    count = 16 * UNITS
    units = jnp.concatenate(split3(got_ref[...].reshape(count, 128)), axis=1)
    row = iota((1, count), 1)
    j = row % UNITS
    q = 5 * (row // UNITS) + j % 5
    expand = (q == iota((80, count), 0)).astype(jnp.float32)
    spread = dot(place, expand, EXACT)
    mine = 5 * at_ref[1] + j // 5 == iota((40, count), 0)
    slot = jnp.sum(jnp.where(mine, spread, 0.0), axis=0, keepdims=True)
    slot = jnp.where(j < 25, slot, -1.0)
    pick = one_hot(slot == iota((slots, count), 0).astype(jnp.float32))
    got = dot(pick, units)
    right_ref[...] = (got[:, :128] + got[:, 128:256]) + got[:, 256:]


def spread_kernel(slots, at_ref, pattern_ref, own_ref, swap_ref, out_ref):
    pattern = pattern_ref[...].astype(jnp.float32).astype(jnp.bfloat16)
    zl, zh, c = at_ref[1], at_ref[2], at_ref[3]
    slot = iota((80, slots), 1).astype(jnp.float32)
    half = iota((80, 40), 1)
    for dc, ref in ((0, own_ref), (1, swap_ref)):
        for dzh in range(2):
            there = jnp.abs(zh - dzh)
            place = places(pattern, there, jnp.abs(c - dc))
            pick = []
            for h in range(5):
                at = jnp.sum(jnp.where(half == 5 * zl + h, place, 0.0), axis=1, keepdims=True)
                pick.append(one_hot(at == slot))
            pick = jnp.concatenate(pick, axis=0)
            for t in range(4):
                got = dot(pick, jnp.concatenate(split3(ref[t, there]), axis=1))
                got = (got[:, :128] + got[:, 128:256]) + got[:, 256:]
                got = jnp.concatenate([got[80 * h : 80 * h + 80] for h in range(5)], axis=1)
                base = 40 * (2 * dzh + dc) + 10 * t
                for block in range(8):
                    out_ref[block, base : base + 10] = got[10 * block : 10 * block + 10]


def product_kernel(left_ref, right_ref, out_ref, both_ref, hi_ref, lo_ref):
    lane = iota((8, 128), 1) // 32
    for block in range(8):
        main = slice(256 * block, 256 * block + 128)
        last = slice(256 * block + 128, 256 * block + 256)
        rows = slice(256 * block, 256 * block + 256)
        right = right_ref[block]
        right = jnp.concatenate([right] + [right[128:]] * 3, axis=0)
        hi_ref[rows], lo_ref[rows] = split(right)
        for y in range(4):
            rest = []
            for tile in range(10):
                start = MAIN + 8 * (tile // 4)
                part = left_ref[block, y, start : start + 8]
                rest.append(jnp.where(lane == tile % 4, part, 0.0))
            upper = slice(80 * y, 80 * y + 80)
            lower = slice(320 + 80 * y, 400 + 80 * y)
            both_ref[upper, main], both_ref[lower, main] = split(left_ref[block, y, :MAIN])
            both_ref[upper, last], both_ref[lower, last] = split(jnp.concatenate(rest, axis=0))
    total = dot(both_ref[...], hi_ref[...])
    total = total[:320] + (dot(both_ref[:320], lo_ref[...]) + total[320:])
    out_ref[...] = total.reshape(4, 80, 640)


def inflate_kernel(at_ref, pattern_ref, shares_ref, out_ref, sums_ref):
    for h in range(5):
        lanes = slice(128 * h, 128 * h + 128)
        x = (shares_ref[0, :, lanes] + shares_ref[1, :, lanes]) + (
            shares_ref[2, :, lanes] + shares_ref[3, :, lanes]
        )
        out_ref[:, lanes] = masked_block(at_ref, at_ref[0], pattern_ref, h, x * x)
    sums_ref[...] = lax.dot_general(
        jnp.ones((8, 640), jnp.float32),
        out_ref[...],
        (((1,), (1,)), ((), ())),
        precision=lax.Precision.HIGHEST,
        preferred_element_type=jnp.float32,
    )


def scale_kernel(nodes, inflated_ref, sums_ref, out_ref):
    totals = lax.dot_general(
        sums_ref[...],
        jnp.ones((8, 128), jnp.float32),
        (((0,), (0,)), ((), ())),
        precision=lax.Precision.HIGHEST,
        preferred_element_type=jnp.float32,
    )
    scale = nodes / totals
    for h in range(5):
        lanes = slice(128 * h, 128 * h + 128)
        out_ref[:, lanes] = inflated_ref[:, lanes] * scale


def swap(x, axis_name):
    return lax.ppermute(x, axis_name, [(0, 1), (1, 0)])


def gather(x, axis_name, limit):
    rows = x.shape[-2]
    parts = -(-rows // limit)
    size = rows // parts
    done = [
        lax.all_gather(x[..., i * size : (i + 1) * size, :], axis_name, axis=0)
        for i in range(parts)
    ]
    return done[0] if parts == 1 else jnp.concatenate(done, axis=-2)


def f32(*shape):
    return jax.ShapeDtypeStruct(shape, jnp.float32)


def right_blocks(slots, at, in_pattern, got):
    cols = 640
    right = call(
        functools.partial(pack_kernel, slots),
        f32(slots, 128),
        [SMEM, VMEM, VMEM],
        (at, in_pattern, got),
    )
    own = gather(gather(right, "zh", SLOTS), "x", SLOTS)
    return call(
        functools.partial(spread_kernel, slots),
        f32(8, 160, cols),
        [SMEM, VMEM, VMEM, VMEM],
        (at, in_pattern, own, swap(own, "c")),
    )


def body(state, in_pattern, out_pattern):
    rows, cols = state.shape
    nodes = cols * lax.axis_size("zl")
    at = jnp.stack([lax.axis_index(ROWS)] + [lax.axis_index(a) for a in ("zl", "zh", "c")])
    at = at.astype(jnp.int32)
    left, masked = call(
        left_kernel,
        (f32(4, LEFT, 128), f32(rows, cols)),
        [SMEM, SMEM, VMEM],
        (at, in_pattern, state),
    )
    left = lax.all_to_all(left, "y", 0, 0)
    left, masked = lax.optimization_barrier((left, masked))
    left = lax.all_gather(left, "zl", axis=0)

    units, most = call(
        units_kernel,
        (f32(16, UNITS, 128), jax.ShapeDtypeStruct((1, 1), jnp.int32)),
        [VMEM, VMEM],
        (in_pattern, masked),
        [pltpu.VMEM((5, rows, 128), jnp.float32)],
        out_specs=(VMEM, SMEM),
    )
    got = lax.all_to_all(units, ("x", "y"), 0, 0)
    right = lax.cond(
        most[0, 0] <= SLOTS,
        functools.partial(right_blocks, SLOTS),
        functools.partial(right_blocks, ALL),
        at,
        in_pattern,
        got,
    )
    partial = call(
        product_kernel,
        f32(4, rows, cols),
        [VMEM, VMEM],
        (left, right),
        [pltpu.VMEM((640, 8 * 256), jnp.bfloat16)] + [pltpu.VMEM((8 * 256, cols), jnp.bfloat16)] * 2,
        flops=3 * 10**9,
        size=6 * 10**6,
    )
    shares = lax.all_to_all(partial, "y", 0, 0)
    inflated, sums = call(
        inflate_kernel,
        (f32(rows, cols), f32(8, rows)),
        [SMEM, SMEM, VMEM],
        (at, out_pattern, shares),
    )
    sums = lax.all_to_all(sums.reshape(8, 1, rows), "zl", 0, 0).reshape(8, rows)
    return call(
        functools.partial(scale_kernel, float(nodes)),
        f32(rows, cols),
        [VMEM, VMEM],
        (inflated, sums),
    )


def solution(mesh):
    fine = Mesh(
        mesh.devices.reshape(8, 4, 4, 2, 2), ("zl", "x", "y", "zh", "c")
    )
    return jax.shard_map(
        body,
        mesh=fine,
        in_specs=(P(ROWS, "zl"), P(), P()),
        out_specs=P(ROWS, "zl"),
        check_vma=False,
    )
```

```python
import functools

import jax
import jax.numpy as jnp
from jax import lax
from jax.experimental import pallas as pl
from jax.experimental.pallas import tpu as pltpu
from jax.sharding import Mesh, PartitionSpec as P

BLK = 256
ROWS = ("x", "y", "zh", "c")
MAIN, REST = 80, 24
LEFT = MAIN + REST
SLOTS = 248
ALL = 400
UNITS = 32
EXACT = lax.Precision.HIGHEST
VMEM = pl.BlockSpec(memory_space=pltpu.VMEM)
SMEM = pl.BlockSpec(memory_space=pltpu.SMEM)


def iota(shape, axis):
    return lax.broadcasted_iota(jnp.int32, shape, axis)


def one_hot(mask):
    return mask.astype(jnp.float32).astype(jnp.bfloat16)


def split(x):
    hi = x.astype(jnp.bfloat16)
    return hi, (x - hi.astype(jnp.float32)).astype(jnp.bfloat16)


def split3(x):
    hi = x.astype(jnp.bfloat16)
    return (hi, *split(x - hi.astype(jnp.float32)))


def dot(a, b, precision=None):
    return jnp.dot(a, b, preferred_element_type=jnp.float32, precision=precision)


def dot_rows(a, b, precision=None):
    return lax.dot_general(
        a, b, (((1,), (1,)), ((), ())), precision=precision, preferred_element_type=jnp.float32
    )


def call(kernel, outs, in_specs, args, scratch=(), flops=10**6, size=10**6, out_specs=None):
    return pl.pallas_call(
        kernel,
        out_shape=outs,
        in_specs=in_specs,
        out_specs=out_specs or jax.tree.map(lambda _: VMEM, outs),
        scratch_shapes=scratch,
        compiler_params=pltpu.CompilerParams(vmem_limit_bytes=26 * 2**20),
        cost_estimate=pl.CostEstimate(
            flops=flops, bytes_accessed=size, transcendentals=0
        ),
    )(*args)


def masked_block(at_ref, owner, pattern_ref, h, x):
    row = owner * 80
    col = (5 * at_ref[1] + h) // 2
    first = row // BLK
    low = pattern_ref[first, col].astype(jnp.float32)
    high = pattern_ref[jnp.minimum(first + 1, 19), col].astype(jnp.float32)
    here = lax.broadcasted_iota(jnp.int32, (80, 128), 0) + row < (first + 1) * BLK
    return x * jnp.where(here, low, high)


def chunk_of(q, zh, c):
    return 20 * (q // 5) + 10 * zh + 5 * c + q % 5


def places(pattern, zh, c):
    rows = one_hot(chunk_of(iota((80, 1), 0), zh, c) // 16 == iota((80, 20), 1))
    cols = one_hot(iota((20, 40), 1) // 2 == iota((20, 40), 0))
    live = dot(dot(rows, pattern).astype(jnp.bfloat16), cols)
    before = dot(one_hot(iota((80, 80), 1) < iota((80, 80), 0)), live.astype(jnp.bfloat16))
    total = jnp.broadcast_to(jnp.sum(live, axis=0, keepdims=True), (80, 40))
    a, b = iota((40, 40), 0), iota((40, 40), 1)
    earlier = dot(total.astype(jnp.bfloat16), one_hot((a // 5 == b // 5) & (a < b)))
    return jnp.where(live > 0, before + earlier, -1.0)


def places_across(pattern, zh, c):
    rows = one_hot(chunk_of(iota((1, 80), 1), zh, c) // 16 == iota((20, 80), 0))
    cols = one_hot(iota((40, 20), 0) // 2 == iota((40, 20), 1))
    live = dot(dot_rows(cols, pattern).astype(jnp.bfloat16), rows)
    before = dot(live.astype(jnp.bfloat16), one_hot(iota((80, 80), 0) < iota((80, 80), 1)))
    total = jnp.broadcast_to(jnp.sum(live, axis=1, keepdims=True), (40, 80))
    a, b = iota((40, 40), 1), iota((40, 40), 0)
    earlier = dot(one_hot((a // 5 == b // 5) & (a < b)), total.astype(jnp.bfloat16))
    return jnp.where(live > 0, before + earlier, -1.0)


def most_live(pattern):
    counts = []
    for group in range(4):
        rows = chunk_of(iota((80, 1), 0), group // 2, group % 2) // 16 == iota((80, 20), 1)
        counts.append(jnp.sum(rows.astype(jnp.float32), axis=0, keepdims=True))
    counts = jnp.concatenate(counts * 2, axis=0).astype(jnp.bfloat16)
    wide = jnp.zeros((20, 8), jnp.float32)
    for h in range(5):
        wide += ((5 * iota((20, 8), 1) + h) // 2 == iota((20, 8), 0)).astype(jnp.float32)
    most = dot(dot(counts, pattern).astype(jnp.bfloat16), wide.astype(jnp.bfloat16))
    return jnp.max(most).astype(jnp.int32)


def left_kernel(at_ref, pattern_ref, state_ref, out_ref, masked_ref):
    zh, c = at_ref[2], at_ref[3]
    for h in range(5):
        lanes = slice(128 * h, 128 * h + 128)
        masked_ref[:, lanes] = masked_block(
            at_ref, at_ref[0], pattern_ref, h, state_ref[:, lanes]
        )
    n = lax.broadcasted_iota(jnp.int32, (1, 640), 1)
    late = n >= 512
    y = jnp.where(late, (n - 512) // 32, n // 128)
    m = jnp.where(late, 128 + n % 32, n % 128)
    dzh, dc, t, y0, e = m // 80, m // 40 % 2, m % 40 // 10, m % 10 // 5, m % 5
    zh_of = jnp.where(dzh == 0, zh, 1 - zh)
    c_of = jnp.where(dc == 0, c, 1 - c)
    source = 80 * (4 * y0 + 2 * zh_of + c_of) + 16 * e + 4 * y + t
    order = lax.broadcasted_iota(jnp.int32, (640, 640), 0) == source
    order = order.astype(jnp.float32).astype(jnp.bfloat16)
    x = masked_ref[...]
    hi = x.astype(jnp.bfloat16)
    mid, low = split(x - hi.astype(jnp.float32))
    moved = (dot(hi, order) + dot(mid, order)) + dot(low, order)
    lane = lax.broadcasted_iota(jnp.int32, (8, 128), 1) // 32
    for y in range(4):
        out_ref[y, :MAIN] = moved[:, 128 * y : 128 * y + 128]
        for slot in range(3):
            tile = jnp.zeros((8, 128), jnp.float32)
            for j in range(min(4, 10 - 4 * slot)):
                rows = 8 * (4 * slot + j)
                part = moved[rows : rows + 8, 512:]
                if j != y:
                    part = pltpu.roll(part, 32 * ((j - y) % 4), 1)
                tile = jnp.where(lane == j, part, tile)
            out_ref[y, MAIN + 8 * slot : MAIN + 8 * slot + 8] = tile


def units_kernel(pattern_ref, masked_ref, out_ref, most_ref, plain_ref):
    most_ref[0, 0] = most_live(pattern_ref[...].astype(jnp.float32).astype(jnp.bfloat16))
    for h in range(5):
        plain_ref[h] = masked_ref[:, 128 * h : 128 * h + 128]
    for x in range(4):
        for y in range(4):
            for h in range(5):
                out_ref[4 * x + y, 5 * h : 5 * h + 5] = plain_ref[
                    h, pl.ds(4 * y + x, 5, stride=16), :
                ]
            out_ref[4 * x + y, 25:] = jnp.zeros((UNITS - 25, 128), jnp.float32)


def pack_kernel(slots, at_ref, pattern_ref, got_ref, right_ref):
    pattern = pattern_ref[...].astype(jnp.float32).astype(jnp.bfloat16)
    place = places_across(pattern, at_ref[2], at_ref[3])
    count = 16 * UNITS
    units = jnp.concatenate(split3(got_ref[...].reshape(count, 128)), axis=1)
    row = iota((1, count), 1)
    j = row % UNITS
    q = 5 * (row // UNITS) + j % 5
    expand = (q == iota((80, count), 0)).astype(jnp.float32)
    spread = dot(place, expand, EXACT)
    mine = 5 * at_ref[1] + j // 5 == iota((40, count), 0)
    slot = jnp.sum(jnp.where(mine, spread, 0.0), axis=0, keepdims=True)
    slot = jnp.where(j < 25, slot, -1.0)
    pick = one_hot(slot == iota((slots, count), 0).astype(jnp.float32))
    got = dot(pick, units)
    right_ref[...] = (got[:, :128] + got[:, 128:256]) + got[:, 256:]


def spread_kernel(slots, at_ref, pattern_ref, own_ref, swap_ref, out_ref):
    pattern = pattern_ref[...].astype(jnp.float32).astype(jnp.bfloat16)
    zl, zh, c = at_ref[1], at_ref[2], at_ref[3]
    slot = iota((80, slots), 1).astype(jnp.float32)
    half = iota((80, 40), 1)
    for dc, ref in ((0, own_ref), (1, swap_ref)):
        for dzh in range(2):
            there = jnp.abs(zh - dzh)
            place = places(pattern, there, jnp.abs(c - dc))
            pick = []
            for h in range(5):
                at = jnp.sum(jnp.where(half == 5 * zl + h, place, 0.0), axis=1, keepdims=True)
                pick.append(one_hot(at == slot))
            pick = jnp.concatenate(pick, axis=0)
            for t in range(4):
                got = dot(pick, jnp.concatenate(split3(ref[t, there]), axis=1))
                got = (got[:, :128] + got[:, 128:256]) + got[:, 256:]
                got = jnp.concatenate([got[80 * h : 80 * h + 80] for h in range(5)], axis=1)
                base = 40 * (2 * dzh + dc) + 10 * t
                for block in range(8):
                    out_ref[block, base : base + 10] = got[10 * block : 10 * block + 10]


def product_kernel(left_ref, right_ref, out_ref, both_ref, hi_ref, lo_ref):
    lane = iota((8, 128), 1) // 32
    for block in range(8):
        main = slice(256 * block, 256 * block + 128)
        last = slice(256 * block + 128, 256 * block + 256)
        rows = slice(256 * block, 256 * block + 256)
        right = right_ref[block]
        right = jnp.concatenate([right] + [right[128:]] * 3, axis=0)
        hi_ref[rows], lo_ref[rows] = split(right)
        for y in range(4):
            rest = []
            for tile in range(10):
                start = MAIN + 8 * (tile // 4)
                part = left_ref[block, y, start : start + 8]
                rest.append(jnp.where(lane == tile % 4, part, 0.0))
            upper = slice(80 * y, 80 * y + 80)
            lower = slice(320 + 80 * y, 400 + 80 * y)
            both_ref[upper, main], both_ref[lower, main] = split(left_ref[block, y, :MAIN])
            both_ref[upper, last], both_ref[lower, last] = split(jnp.concatenate(rest, axis=0))
    total = dot(both_ref[...], hi_ref[...])
    total = total[:320] + (dot(both_ref[:320], lo_ref[...]) + total[320:])
    out_ref[...] = total.reshape(4, 80, 640)


def inflate_kernel(at_ref, pattern_ref, shares_ref, out_ref, sums_ref):
    for h in range(5):
        lanes = slice(128 * h, 128 * h + 128)
        x = (shares_ref[0, :, lanes] + shares_ref[1, :, lanes]) + (
            shares_ref[2, :, lanes] + shares_ref[3, :, lanes]
        )
        out_ref[:, lanes] = masked_block(at_ref, at_ref[0], pattern_ref, h, x * x)
    sums_ref[...] = lax.dot_general(
        jnp.ones((8, 640), jnp.float32),
        out_ref[...],
        (((1,), (1,)), ((), ())),
        precision=lax.Precision.HIGHEST,
        preferred_element_type=jnp.float32,
    )


def scale_kernel(nodes, inflated_ref, sums_ref, out_ref):
    totals = lax.dot_general(
        sums_ref[...],
        jnp.ones((8, 128), jnp.float32),
        (((0,), (0,)), ((), ())),
        precision=lax.Precision.HIGHEST,
        preferred_element_type=jnp.float32,
    )
    scale = nodes / totals
    for h in range(5):
        lanes = slice(128 * h, 128 * h + 128)
        out_ref[:, lanes] = inflated_ref[:, lanes] * scale


def swap(x, axis_name):
    return lax.ppermute(x, axis_name, [(0, 1), (1, 0)])


def gather(x, axis_name, limit):
    rows = x.shape[-2]
    parts = -(-rows // limit)
    size = rows // parts
    done = [
        lax.all_gather(x[..., i * size : (i + 1) * size, :], axis_name, axis=0)
        for i in range(parts)
    ]
    return done[0] if parts == 1 else jnp.concatenate(done, axis=-2)


def f32(*shape):
    return jax.ShapeDtypeStruct(shape, jnp.float32)


def right_blocks(slots, at, in_pattern, got):
    cols = 640
    right = call(
        functools.partial(pack_kernel, slots),
        f32(slots, 128),
        [SMEM, VMEM, VMEM],
        (at, in_pattern, got),
    )
    own = gather(gather(right, "zh", ALL), "x", SLOTS)
    return call(
        functools.partial(spread_kernel, slots),
        f32(8, 160, cols),
        [SMEM, VMEM, VMEM, VMEM],
        (at, in_pattern, own, swap(own, "c")),
    )


def body(state, in_pattern, out_pattern):
    rows, cols = state.shape
    nodes = cols * lax.axis_size("zl")
    at = jnp.stack([lax.axis_index(ROWS)] + [lax.axis_index(a) for a in ("zl", "zh", "c")])
    at = at.astype(jnp.int32)
    left, masked = call(
        left_kernel,
        (f32(4, LEFT, 128), f32(rows, cols)),
        [SMEM, SMEM, VMEM],
        (at, in_pattern, state),
    )
    left = lax.all_to_all(left, "y", 0, 0)
    left, masked = lax.optimization_barrier((left, masked))
    left = lax.all_gather(left, "zl", axis=0)

    units, most = call(
        units_kernel,
        (f32(16, UNITS, 128), jax.ShapeDtypeStruct((1, 1), jnp.int32)),
        [VMEM, VMEM],
        (in_pattern, masked),
        [pltpu.VMEM((5, rows, 128), jnp.float32)],
        out_specs=(VMEM, SMEM),
    )
    got = lax.all_to_all(units, ("x", "y"), 0, 0)
    right = lax.cond(
        most[0, 0] <= SLOTS,
        functools.partial(right_blocks, SLOTS),
        functools.partial(right_blocks, ALL),
        at,
        in_pattern,
        got,
    )
    partial = call(
        product_kernel,
        f32(4, rows, cols),
        [VMEM, VMEM],
        (left, right),
        [pltpu.VMEM((640, 8 * 256), jnp.bfloat16)] + [pltpu.VMEM((8 * 256, cols), jnp.bfloat16)] * 2,
        flops=3 * 10**9,
        size=6 * 10**6,
    )
    shares = lax.all_to_all(partial, "y", 0, 0)
    inflated, sums = call(
        inflate_kernel,
        (f32(rows, cols), f32(8, rows)),
        [SMEM, SMEM, VMEM],
        (at, out_pattern, shares),
    )
    sums = lax.all_to_all(sums.reshape(8, 1, rows), "zl", 0, 0).reshape(8, rows)
    return call(
        functools.partial(scale_kernel, float(nodes)),
        f32(rows, cols),
        [VMEM, VMEM],
        (inflated, sums),
    )


def solution(mesh):
    fine = Mesh(
        mesh.devices.reshape(8, 4, 4, 2, 2), ("zl", "x", "y", "zh", "c")
    )
    return jax.shard_map(
        body,
        mesh=fine,
        in_specs=(P(ROWS, "zl"), P(), P()),
        out_specs=P(ROWS, "zl"),
        check_vma=False,
    )
```

```python
import functools

import jax
import jax.numpy as jnp
from jax import lax
from jax.experimental import pallas as pl
from jax.experimental.pallas import tpu as pltpu
from jax.sharding import Mesh, PartitionSpec as P

BLK = 256
ROWS = ("x", "y", "zh", "c")
MAIN, REST = 80, 24
LEFT = MAIN + REST
SLOTS = 248
ALL = 400
UNITS = 32
EXACT = lax.Precision.HIGHEST
VMEM = pl.BlockSpec(memory_space=pltpu.VMEM)
SMEM = pl.BlockSpec(memory_space=pltpu.SMEM)


def iota(shape, axis):
    return lax.broadcasted_iota(jnp.int32, shape, axis)


def one_hot(mask):
    return mask.astype(jnp.float32).astype(jnp.bfloat16)


def split(x):
    hi = x.astype(jnp.bfloat16)
    return hi, (x - hi.astype(jnp.float32)).astype(jnp.bfloat16)


def split3(x):
    hi = x.astype(jnp.bfloat16)
    return (hi, *split(x - hi.astype(jnp.float32)))


def dot(a, b, precision=None):
    return jnp.dot(a, b, preferred_element_type=jnp.float32, precision=precision)


def dot_rows(a, b, precision=None):
    return lax.dot_general(
        a, b, (((1,), (1,)), ((), ())), precision=precision, preferred_element_type=jnp.float32
    )


def call(kernel, outs, in_specs, args, scratch=(), flops=10**6, size=10**6, out_specs=None):
    return pl.pallas_call(
        kernel,
        out_shape=outs,
        in_specs=in_specs,
        out_specs=out_specs or jax.tree.map(lambda _: VMEM, outs),
        scratch_shapes=scratch,
        compiler_params=pltpu.CompilerParams(vmem_limit_bytes=26 * 2**20),
        cost_estimate=pl.CostEstimate(
            flops=flops, bytes_accessed=size, transcendentals=0
        ),
    )(*args)


def masked_block(at_ref, owner, pattern_ref, h, x):
    row = owner * 80
    col = (5 * at_ref[1] + h) // 2
    first = row // BLK
    low = pattern_ref[first, col].astype(jnp.float32)
    high = pattern_ref[jnp.minimum(first + 1, 19), col].astype(jnp.float32)
    here = lax.broadcasted_iota(jnp.int32, (80, 128), 0) + row < (first + 1) * BLK
    return x * jnp.where(here, low, high)


def chunk_of(q, zh, c):
    return 20 * (q // 5) + 10 * zh + 5 * c + q % 5


def places(pattern, zh, c):
    rows = one_hot(chunk_of(iota((80, 1), 0), zh, c) // 16 == iota((80, 20), 1))
    cols = one_hot(iota((20, 40), 1) // 2 == iota((20, 40), 0))
    live = dot(dot(rows, pattern).astype(jnp.bfloat16), cols)
    before = dot(one_hot(iota((80, 80), 1) < iota((80, 80), 0)), live.astype(jnp.bfloat16))
    total = jnp.broadcast_to(jnp.sum(live, axis=0, keepdims=True), (80, 40))
    a, b = iota((40, 40), 0), iota((40, 40), 1)
    earlier = dot(total.astype(jnp.bfloat16), one_hot((a // 5 == b // 5) & (a < b)))
    return jnp.where(live > 0, before + earlier, -1.0)


def places_across(pattern, zh, c):
    rows = one_hot(chunk_of(iota((1, 80), 1), zh, c) // 16 == iota((20, 80), 0))
    cols = one_hot(iota((40, 20), 0) // 2 == iota((40, 20), 1))
    live = dot(dot_rows(cols, pattern).astype(jnp.bfloat16), rows)
    before = dot(live.astype(jnp.bfloat16), one_hot(iota((80, 80), 0) < iota((80, 80), 1)))
    total = jnp.broadcast_to(jnp.sum(live, axis=1, keepdims=True), (40, 80))
    a, b = iota((40, 40), 1), iota((40, 40), 0)
    earlier = dot(one_hot((a // 5 == b // 5) & (a < b)), total.astype(jnp.bfloat16))
    return jnp.where(live > 0, before + earlier, -1.0)


def most_live(pattern):
    counts = []
    for group in range(4):
        rows = chunk_of(iota((80, 1), 0), group // 2, group % 2) // 16 == iota((80, 20), 1)
        counts.append(jnp.sum(rows.astype(jnp.float32), axis=0, keepdims=True))
    counts = jnp.concatenate(counts * 2, axis=0).astype(jnp.bfloat16)
    wide = jnp.zeros((20, 8), jnp.float32)
    for h in range(5):
        wide += ((5 * iota((20, 8), 1) + h) // 2 == iota((20, 8), 0)).astype(jnp.float32)
    most = dot(dot(counts, pattern).astype(jnp.bfloat16), wide.astype(jnp.bfloat16))
    return jnp.max(most).astype(jnp.int32)


def left_kernel(at_ref, pattern_ref, state_ref, out_ref, masked_ref):
    zh, c = at_ref[2], at_ref[3]
    for h in range(5):
        lanes = slice(128 * h, 128 * h + 128)
        masked_ref[:, lanes] = masked_block(
            at_ref, at_ref[0], pattern_ref, h, state_ref[:, lanes]
        )
    n = lax.broadcasted_iota(jnp.int32, (1, 640), 1)
    late = n >= 512
    y = jnp.where(late, (n - 512) // 32, n // 128)
    m = jnp.where(late, 128 + n % 32, n % 128)
    dzh, dc, t, y0, e = m // 80, m // 40 % 2, m % 40 // 10, m % 10 // 5, m % 5
    zh_of = jnp.where(dzh == 0, zh, 1 - zh)
    c_of = jnp.where(dc == 0, c, 1 - c)
    source = 80 * (4 * y0 + 2 * zh_of + c_of) + 16 * e + 4 * y + t
    order = lax.broadcasted_iota(jnp.int32, (640, 640), 0) == source
    order = order.astype(jnp.float32).astype(jnp.bfloat16)
    x = masked_ref[...]
    hi, lo = split(x)
    moved = dot(hi, order) + dot(lo, order)
    lane = lax.broadcasted_iota(jnp.int32, (8, 128), 1) // 32
    for y in range(4):
        out_ref[y, :MAIN] = moved[:, 128 * y : 128 * y + 128]
        for slot in range(3):
            tile = jnp.zeros((8, 128), jnp.float32)
            for j in range(min(4, 10 - 4 * slot)):
                rows = 8 * (4 * slot + j)
                part = moved[rows : rows + 8, 512:]
                if j != y:
                    part = pltpu.roll(part, 32 * ((j - y) % 4), 1)
                tile = jnp.where(lane == j, part, tile)
            out_ref[y, MAIN + 8 * slot : MAIN + 8 * slot + 8] = tile


def units_kernel(pattern_ref, masked_ref, out_ref, most_ref, plain_ref):
    most_ref[0, 0] = most_live(pattern_ref[...].astype(jnp.float32).astype(jnp.bfloat16))
    for h in range(5):
        plain_ref[h] = masked_ref[:, 128 * h : 128 * h + 128]
    for x in range(4):
        for y in range(4):
            for h in range(5):
                out_ref[4 * x + y, 5 * h : 5 * h + 5] = plain_ref[
                    h, pl.ds(4 * y + x, 5, stride=16), :
                ]
            out_ref[4 * x + y, 25:] = jnp.zeros((UNITS - 25, 128), jnp.float32)


def pack_kernel(slots, at_ref, pattern_ref, got_ref, right_ref):
    pattern = pattern_ref[...].astype(jnp.float32).astype(jnp.bfloat16)
    place = places_across(pattern, at_ref[2], at_ref[3])
    count = 16 * UNITS
    units = jnp.concatenate(split3(got_ref[...].reshape(count, 128)), axis=1)
    row = iota((1, count), 1)
    j = row % UNITS
    q = 5 * (row // UNITS) + j % 5
    expand = (q == iota((80, count), 0)).astype(jnp.float32)
    spread = dot(place, expand, EXACT)
    mine = 5 * at_ref[1] + j // 5 == iota((40, count), 0)
    slot = jnp.sum(jnp.where(mine, spread, 0.0), axis=0, keepdims=True)
    slot = jnp.where(j < 25, slot, -1.0)
    pick = one_hot(slot == iota((slots, count), 0).astype(jnp.float32))
    got = dot(pick, units)
    right_ref[...] = (got[:, :128] + got[:, 128:256]) + got[:, 256:]


def spread_kernel(slots, at_ref, pattern_ref, own_ref, swap_ref, out_ref):
    pattern = pattern_ref[...].astype(jnp.float32).astype(jnp.bfloat16)
    zl, zh, c = at_ref[1], at_ref[2], at_ref[3]
    slot = iota((80, slots), 1).astype(jnp.float32)
    half = iota((80, 40), 1)
    for dc, ref in ((0, own_ref), (1, swap_ref)):
        for dzh in range(2):
            there = jnp.abs(zh - dzh)
            place = places(pattern, there, jnp.abs(c - dc))
            pick = []
            for h in range(5):
                at = jnp.sum(jnp.where(half == 5 * zl + h, place, 0.0), axis=1, keepdims=True)
                pick.append(one_hot(at == slot))
            pick = jnp.concatenate(pick, axis=0)
            for t in range(4):
                got = dot(pick, jnp.concatenate(split3(ref[t, there]), axis=1))
                got = (got[:, :128] + got[:, 128:256]) + got[:, 256:]
                got = jnp.concatenate([got[80 * h : 80 * h + 80] for h in range(5)], axis=1)
                base = 40 * (2 * dzh + dc) + 10 * t
                for block in range(8):
                    out_ref[block, base : base + 10] = got[10 * block : 10 * block + 10]


def product_kernel(left_ref, right_ref, out_ref, both_ref, hi_ref, lo_ref):
    lane = iota((8, 128), 1) // 32
    for block in range(8):
        main = slice(256 * block, 256 * block + 128)
        last = slice(256 * block + 128, 256 * block + 256)
        rows = slice(256 * block, 256 * block + 256)
        right = right_ref[block]
        right = jnp.concatenate([right] + [right[128:]] * 3, axis=0)
        hi_ref[rows], lo_ref[rows] = split(right)
        for y in range(4):
            rest = []
            for tile in range(10):
                start = MAIN + 8 * (tile // 4)
                part = left_ref[block, y, start : start + 8]
                rest.append(jnp.where(lane == tile % 4, part, 0.0))
            upper = slice(80 * y, 80 * y + 80)
            lower = slice(320 + 80 * y, 400 + 80 * y)
            both_ref[upper, main], both_ref[lower, main] = split(left_ref[block, y, :MAIN])
            both_ref[upper, last], both_ref[lower, last] = split(jnp.concatenate(rest, axis=0))
    total = dot(both_ref[...], hi_ref[...])
    total = total[:320] + (dot(both_ref[:320], lo_ref[...]) + total[320:])
    out_ref[...] = total.reshape(4, 80, 640)


def inflate_kernel(at_ref, pattern_ref, shares_ref, out_ref, sums_ref):
    for h in range(5):
        lanes = slice(128 * h, 128 * h + 128)
        x = (shares_ref[0, :, lanes] + shares_ref[1, :, lanes]) + (
            shares_ref[2, :, lanes] + shares_ref[3, :, lanes]
        )
        out_ref[:, lanes] = masked_block(at_ref, at_ref[0], pattern_ref, h, x * x)
    sums_ref[...] = lax.dot_general(
        jnp.ones((8, 640), jnp.float32),
        out_ref[...],
        (((1,), (1,)), ((), ())),
        precision=lax.Precision.HIGHEST,
        preferred_element_type=jnp.float32,
    )


def scale_kernel(nodes, inflated_ref, sums_ref, out_ref):
    totals = lax.dot_general(
        sums_ref[...],
        jnp.ones((8, 128), jnp.float32),
        (((0,), (0,)), ((), ())),
        precision=lax.Precision.HIGHEST,
        preferred_element_type=jnp.float32,
    )
    scale = nodes / totals
    for h in range(5):
        lanes = slice(128 * h, 128 * h + 128)
        out_ref[:, lanes] = inflated_ref[:, lanes] * scale


def swap(x, axis_name):
    return lax.ppermute(x, axis_name, [(0, 1), (1, 0)])


def gather(x, axis_name, limit):
    rows = x.shape[-2]
    parts = -(-rows // limit)
    size = rows // parts
    done = [
        lax.all_gather(x[..., i * size : (i + 1) * size, :], axis_name, axis=0)
        for i in range(parts)
    ]
    return done[0] if parts == 1 else jnp.concatenate(done, axis=-2)


def f32(*shape):
    return jax.ShapeDtypeStruct(shape, jnp.float32)


def right_blocks(slots, at, in_pattern, got):
    cols = 640
    right = call(
        functools.partial(pack_kernel, slots),
        f32(slots, 128),
        [SMEM, VMEM, VMEM],
        (at, in_pattern, got),
    )
    own = gather(gather(right, "zh", ALL), "x", SLOTS)
    return call(
        functools.partial(spread_kernel, slots),
        f32(8, 160, cols),
        [SMEM, VMEM, VMEM, VMEM],
        (at, in_pattern, own, swap(own, "c")),
    )


def body(state, in_pattern, out_pattern):
    rows, cols = state.shape
    nodes = cols * lax.axis_size("zl")
    at = jnp.stack([lax.axis_index(ROWS)] + [lax.axis_index(a) for a in ("zl", "zh", "c")])
    at = at.astype(jnp.int32)
    left, masked = call(
        left_kernel,
        (f32(4, LEFT, 128), f32(rows, cols)),
        [SMEM, SMEM, VMEM],
        (at, in_pattern, state),
    )
    left = lax.all_to_all(left, "y", 0, 0)
    left, masked = lax.optimization_barrier((left, masked))
    left = lax.all_gather(left, "zl", axis=0)

    units, most = call(
        units_kernel,
        (f32(16, UNITS, 128), jax.ShapeDtypeStruct((1, 1), jnp.int32)),
        [VMEM, VMEM],
        (in_pattern, masked),
        [pltpu.VMEM((5, rows, 128), jnp.float32)],
        out_specs=(VMEM, SMEM),
    )
    got = lax.all_to_all(units, ("x", "y"), 0, 0)
    right = lax.cond(
        most[0, 0] <= SLOTS,
        functools.partial(right_blocks, SLOTS),
        functools.partial(right_blocks, ALL),
        at,
        in_pattern,
        got,
    )
    partial = call(
        product_kernel,
        f32(4, rows, cols),
        [VMEM, VMEM],
        (left, right),
        [pltpu.VMEM((640, 8 * 256), jnp.bfloat16)] + [pltpu.VMEM((8 * 256, cols), jnp.bfloat16)] * 2,
        flops=3 * 10**9,
        size=6 * 10**6,
    )
    shares = lax.all_to_all(partial, "y", 0, 0)
    inflated, sums = call(
        inflate_kernel,
        (f32(rows, cols), f32(8, rows)),
        [SMEM, SMEM, VMEM],
        (at, out_pattern, shares),
    )
    sums = lax.all_to_all(sums.reshape(8, 1, rows), "zl", 0, 0).reshape(8, rows)
    return call(
        functools.partial(scale_kernel, float(nodes)),
        f32(rows, cols),
        [VMEM, VMEM],
        (inflated, sums),
    )


def solution(mesh):
    fine = Mesh(
        mesh.devices.reshape(8, 4, 4, 2, 2), ("zl", "x", "y", "zh", "c")
    )
    return jax.shard_map(
        body,
        mesh=fine,
        in_specs=(P(ROWS, "zl"), P(), P()),
        out_specs=P(ROWS, "zl"),
        check_vma=False,
    )
```
